32 devices in a mesh: dp: 4 (over y, x), expert: 4 (over z), tensor: 2 (over core).
Axes of the slice: x: 2, y: 2, z: 4, core: 2. Of those that a mesh axis runs over, the one named last changes fastest.
Arguments:
- tokens: bfloat16 [8192, 1536], P(('dp', 'expert')), may hold values from -6 to 6
- out_grad: bfloat16 [8192, 1536], P(('dp', 'expert')), may hold values from -6 to 6
- attn_gain: float32 [1536], replicated, may hold values from 0.5 to 1.5
- query_weight: bfloat16 [1536, 1536], P(None, 'tensor'), may hold values from -0.625 to 0.625
- key_value_weight: bfloat16 [2, 1536, 512], P(None, None, 'tensor'), may hold values from -0.625 to 0.625
- output_weight: bfloat16 [1536, 1536], P('tensor'), may hold values from -0.625 to 0.625
- expert_gain: float32 [1536], replicated, may hold values from 0.5 to 1.5
- router_weight: bfloat16 [1536, 20], replicated, may hold values from -0.078125 to 0.078125
- gateup_weight: bfloat16 [20, 2, 1536, 512], P('expert', None, None, 'tensor'), may hold values from -0.15625 to 0.15625
- down_weight: bfloat16 [20, 512, 1536], P('expert', 'tensor'), may hold values from -4 to 4
- routes: int32 [8192, 8], P(('dp', 'expert')), may hold values from 0 to 19, all different within a row; in each aligned block of 512 rows (0 to 511, 512 to 1023, ...) at most 256 rows name the same one
Outputs:
- mixed: bfloat16 [8192, 1536], P(('dp', 'expert'))
- tokens_grad: float32 [8192, 1536], P(('dp', 'expert'))
- attn_gain_grad: float32 [1536], P(('dp', 'expert'))
- query_grad: float32 [1536, 1536], P(('dp', 'expert'), 'tensor')
- keyvalue_grad: float32 [2, 1536, 512], P(None, ('dp', 'expert'), 'tensor')
- output_weight_grad: float32 [1536, 1536], P('tensor', ('dp', 'expert'))
- expert_gain_grad: float32 [1536], P(('dp', 'expert'))
- router_grad: float32 [1536, 20], P(('dp', 'expert'))
- gateup_grad: float32 [20, 2, 1536, 512], P('expert', None, 'dp', 'tensor')
- down_grad: float32 [20, 512, 1536], P('expert', 'tensor', 'dp')
The draws below stay inside these ranges and needn't reach their ends.
Inputs may be any that keep to these rules, and one draw needn't show every extreme that they name: `routes`: each row names 8 different experts. Within each aligned block of 512 rows no expert is named by more than 256 rows, a bound that some block reaches.
All inputs are finite; a program needn't handle non-finite values.
Results may differ from the reference program's by a relative error of at most 0.018.
The reference program's roundings to bfloat16 on the way count: a program that leaves them out, or rounds other values in their place, can miss the bound.
Values may be sent and summed in bfloat16 or wider, within the bound.
A program may use at most 320 MiB of HBM per device.

```python
import math
import jax
import jax.numpy as jnp
import numpy as np
from jax import lax

MODEL_WIDTH = 1536
HQ = 24
KEY_VALUE_HEADS = 8
HEAD_SIZE = 64
FF = 512
TOPK = 8
SEQUENCE_LENGTH = 512
TOK_DEV = 512
EXPERTS = 20
CAP = 256
TOKENS = 8192


def level_of(stream_key, shape, cuts, low, high):
    loudness = 1.0
    for axis_at, shards_of in cuts:
        draws = jax.random.uniform(jax.random.fold_in(jax.random.fold_in(stream_key, 6), axis_at), (shards_of,), jnp.float32, low / len(cuts), high / len(cuts))
        loudness = loudness * jnp.repeat(jnp.exp(draws), shape[axis_at] // shards_of).reshape((-1,) + (1,) * (len(shape) - 1 - axis_at))
    return loudness


def routed_block(rng, own, number, rows, count, top, most, lean):
    sequence = jax.random.permutation(rng, count)
    crowded, common = portions_of(count, rows * top, most, lean, True), portions_of(count, rows * top, most, lean, False)
    places = jnp.arange(count)

    def named(tallies, rotation):
        used = int((tallies > 0).sum())
        fixed = max(1, used // 4)
        shifted = fixed + (places - fixed + rotation * (used - fixed)) % max(1, count - fixed)
        return jnp.zeros((count,), jnp.int32).at[sequence[jnp.where(places < fixed, places, shifted)]].set(jnp.asarray(tallies, jnp.int32))

    tallies = jnp.where(number % 4 == 0, named(crowded, number // 4), named(common, number - number // 4 - 1))
    mixed = jax.random.permutation(jax.random.fold_in(own, 3), count)
    source_of, receiver = mixed[0:count // 2 * 2:2], mixed[1:count // 2 * 2:2]
    slack = jnp.minimum(tallies[source_of] - 1, most - tallies[receiver]) // 2
    slack = jnp.where((source_of == sequence[0]) | (receiver == sequence[0]) | (tallies[receiver] == 0), 0, jnp.maximum(slack, 0))
    shifted = jax.random.randint(jax.random.fold_in(own, 4), (count // 2,), 0, 1 << 20) % (slack + 1)
    tallies = tallies.at[source_of].add(-shifted).at[receiver].add(shifted)
    labels = jnp.searchsorted(jnp.cumsum(tallies), jnp.arange(rows * top), side="right").astype(jnp.int32)
    table = labels.reshape(top, rows).T
    table = table[jax.random.permutation(jax.random.fold_in(own, 1), rows)]
    rotation = jax.random.randint(jax.random.fold_in(own, 2), (rows, 1), 0, top)
    return jnp.take_along_axis(table, (jnp.arange(top)[None, :] + rotation) % top, axis=1)


def portions_of(number_of, total, limit, slope, full):
    weights = [(1 << 20) // math.isqrt(standing ** slope) + 1 for standing in range(1, number_of + 1)]
    largest = limit if full else min(limit, max(-(-total // number_of), total * weights[0] // sum(weights)))
    least = 1 if total - largest >= number_of - 1 else 0
    given, spare = [largest] + [least] * (number_of - 1), total - largest - least * (number_of - 1)
    while spare > 0:
        candidates = [i for i in range(1, number_of) if given[i] < largest] or [i for i in range(1, number_of) if given[i] < limit]
        mass, left = sum([weights[i] for i in candidates]), spare
        for i in candidates:
            addition = min(limit - given[i], max(1, left * weights[i] // mass), spare)
            given[i] = given[i] + addition
            spare = spare - addition
    return np.array(given)


def normal_values(stream_key, dims, spread, limit, cuts=(), held_as=jnp.bfloat16):
    loudness = level_of(stream_key, dims, cuts, -0.22, 0.18) if cuts else 1.0
    values = jax.random.normal(stream_key, dims, jnp.float32) * spread * loudness
    return jnp.minimum(jnp.maximum(values, -limit), limit).astype(held_as)


def setup_inputs(seed: int = 0) -> dict:
    key_list = jax.random.split(jax.random.key(seed), 12)
    tokens = normal_values(key_list[0], (TOKENS, MODEL_WIDTH), 1.0, 6.0, ((0, 16),))
    out_grad = normal_values(key_list[1], (TOKENS, MODEL_WIDTH), 1.0, 6.0, ((0, 16),))
    attn_gain = jnp.clip(1.0 + 0.1 * jax.random.normal(key_list[2], (MODEL_WIDTH,), jnp.float32), 0.5, 1.5)
    query_weight = normal_values(key_list[3], (MODEL_WIDTH, HQ * HEAD_SIZE), (MODEL_WIDTH // 16) ** -0.5, 0.625, ((1, 2),))
    key_value_weight = normal_values(key_list[4], (2, MODEL_WIDTH, KEY_VALUE_HEADS * HEAD_SIZE), (MODEL_WIDTH // 16) ** -0.5, 0.625, ((2, 2),))
    output_weight = normal_values(key_list[5], (HQ * HEAD_SIZE, MODEL_WIDTH), (HQ * HEAD_SIZE // 16) ** -0.5, 0.625, ((0, 2),))
    expert_gain = jnp.clip(1.0 + 0.1 * jax.random.normal(key_list[6], (MODEL_WIDTH,), jnp.float32), 0.5, 1.5)
    router_weight = normal_values(key_list[7], (MODEL_WIDTH, EXPERTS), (4 * MODEL_WIDTH) ** -0.5, 0.078125)
    gateup_weight = normal_values(key_list[8], (EXPERTS, 2, MODEL_WIDTH, FF), MODEL_WIDTH ** -0.5, 0.15625, ((0, 4), (3, 2)))
    down_weight = normal_values(key_list[9], (EXPERTS, FF, MODEL_WIDTH), (max(1, FF // 256)) ** -0.5, 4.0, ((0, 4), (1, 2)))
    routes_keys = jax.random.split(jax.random.fold_in(key_list[10], 1), TOKENS // TOK_DEV)
    routes_turns = jax.random.permutation(jax.random.fold_in(key_list[10], 3), TOKENS // TOK_DEV)
    routes = jax.vmap(lambda own, number: routed_block(jax.random.fold_in(key_list[10], 2), own, number, TOK_DEV, EXPERTS, TOPK, CAP, 1))(routes_keys, routes_turns).reshape((TOKENS, TOPK))
    return {"tokens": tokens, "out_grad": out_grad, "attn_gain": attn_gain, "query_weight": query_weight, "key_value_weight": key_value_weight, "output_weight": output_weight, "expert_gain": expert_gain, "router_weight": router_weight, "gateup_weight": gateup_weight, "down_weight": down_weight, "routes": routes}


EPSILON = 1e-06
RESIDUAL = 0.22
ATTN_SCALE = 0.015625
ROPE_BASE = 10000.0
NEGATIVE = -1e+30
HIGHEST = lax.Precision.HIGHEST

@jax.custom_vjp
def low(v):
    return lax.optimization_barrier(v.astype(jnp.bfloat16)).astype(jnp.float32)

@jax.custom_vjp
def low_back(v):
    return v

def low_keep(v):
    return (low(v), None)

def low_pass(kept, grad):
    return (grad,)

def back_keep(v):
    return (v, None)

def back_low(kept, grad):
    return (low(grad),)
low.defvjp(low_keep, low_pass)
low_back.defvjp(back_keep, back_low)

def matmul(left, right):
    return jnp.dot(left, right, precision=HIGHEST, preferred_element_type=jnp.float32)

def normalize(value_rows, gain):
    return value_rows * lax.rsqrt(lax.optimization_barrier(jnp.mean(value_rows * value_rows, axis=-1, keepdims=True)) + EPSILON) * gain

def rotary_embedding(value_rows):
    half_dim = HEAD_SIZE // 2
    frequency = ROPE_BASE ** (-jnp.arange(half_dim, dtype=jnp.float32) * 2.0 / HEAD_SIZE)
    angles = jnp.arange(SEQUENCE_LENGTH, dtype=jnp.float32)[:, None] * frequency[None, :]
    cosine = jnp.cos(angles)[:, None, :]
    sine_table = jnp.sin(angles)[:, None, :]
    first = value_rows[..., :half_dim]
    second = value_rows[..., half_dim:]
    return jnp.concatenate([first * cosine - second * sine_table, second * cosine + first * sine_table], axis=-1)

def attend_one(block_item):
    queries, heads_of_key, value_rows = block_item
    group_ratio = queries.shape[1] // heads_of_key.shape[1]
    keys_all = jnp.repeat(heads_of_key, group_ratio, axis=1)
    values_all = jnp.repeat(value_rows, group_ratio, axis=1)
    scores = low_back(jnp.einsum('qhd,khd->hqk', queries, keys_all, precision=HIGHEST) * ATTN_SCALE)
    positions = jnp.arange(queries.shape[0])
    scores = jnp.where((positions[:, None] >= positions[None, :])[None], scores, NEGATIVE)
    weights = jax.nn.softmax(scores, axis=-1)
    return jnp.einsum('hqk,khd->qhd', low(weights), values_all, precision=HIGHEST)

def reference(tokens, out_grad, attn_gain, query_weight, key_value_weight, output_weight, expert_gain, router_weight, gateup_weight, down_weight, routes):
    tok_total = tokens.shape[0]
    group_count = tok_total // TOK_DEV
    sequence_count = tok_total // SEQUENCE_LENGTH
    pair_count = TOK_DEV * TOPK
    pair_expert = routes.reshape(group_count, pair_count)
    hit_table = (pair_expert[:, :, None] == jnp.arange(EXPERTS, dtype=jnp.int32)[None, None, :]).astype(jnp.int32)
    slot_place = lax.optimization_barrier(jnp.sum((jnp.cumsum(hit_table, axis=1) - hit_table) * hit_table, axis=2))
    pair_index = jnp.broadcast_to(jnp.arange(pair_count, dtype=jnp.int32)[None, :], pair_expert.shape)
    group_index = jnp.broadcast_to(jnp.arange(group_count, dtype=jnp.int32)[:, None], pair_expert.shape)
    slot_pair = jnp.full((group_count, EXPERTS, CAP), pair_count, jnp.int32).at[group_index, pair_expert, slot_place].set(pair_index)
    slot_token = slot_pair // TOPK

    def forward(tokens, attn_gain, query_weight, key_value_weight, output_weight, expert_gain, router_weight, gateup_weight, down_weight):
        normed = low(normalize(tokens, attn_gain))
        queries = low_back(matmul(normed, query_weight))
        heads_of_key = low_back(matmul(normed, key_value_weight[0]))
        value_rows = low(low_back(matmul(normed, key_value_weight[1])))
        queries = low(rotary_embedding(queries.reshape(sequence_count, SEQUENCE_LENGTH, HQ, HEAD_SIZE)))
        heads_of_key = low(rotary_embedding(heads_of_key.reshape(sequence_count, SEQUENCE_LENGTH, KEY_VALUE_HEADS, HEAD_SIZE)))
        value_rows = value_rows.reshape(sequence_count, SEQUENCE_LENGTH, KEY_VALUE_HEADS, HEAD_SIZE)
        heads_out = lax.map(jax.checkpoint(attend_one), (queries, heads_of_key, value_rows))
        heads_out = low(low_back(heads_out.reshape(tok_total, HQ * HEAD_SIZE)))
        attention = low_back(matmul(heads_out, output_weight))
        middle = tokens + RESIDUAL * attention
        expert_in = low(normalize(middle, expert_gain))
        logits = low_back(matmul(expert_in, router_weight))
        gates = jax.nn.softmax(jnp.take_along_axis(logits, routes, axis=1), axis=-1)

        def group_experts(group_item):
            rows_in, gates_in, token_slots, pair_slots = group_item
            padded_in = jnp.concatenate([rows_in, jnp.zeros((1, MODEL_WIDTH), jnp.float32)], axis=0)
            padded_gates = jnp.concatenate([gates_in.reshape(-1), jnp.zeros((1,), jnp.float32)])

            def one_expert(accumulate, expert_item):
                gateup, down, token_rows, pair_rows = expert_item
                expert_rows = low_back(padded_in[token_rows])
                hidden = low_back(jnp.einsum('rd,cdf->rcf', expert_rows, gateup, precision=HIGHEST))
                activation = low(jax.nn.silu(hidden[:, 0]) * hidden[:, 1])
                result = low(low_back(matmul(activation, down)))
                return (accumulate.at[token_rows].add(padded_gates[pair_rows][:, None] * result), None)
            start_sum = jnp.zeros((TOK_DEV + 1, MODEL_WIDTH), jnp.float32)
            total_sum = lax.scan(one_expert, start_sum, (gateup_weight, down_weight, token_slots, pair_slots))[0]
            return total_sum[:TOK_DEV]
        combined = lax.map(jax.checkpoint(group_experts), (expert_in.reshape(group_count, TOK_DEV, MODEL_WIDTH), gates.reshape(group_count, TOK_DEV, TOPK), slot_token, slot_pair))
        return middle + RESIDUAL * combined.reshape(tok_total, MODEL_WIDTH)
    mixed, pullback = jax.vjp(forward, tokens.astype(jnp.float32), attn_gain.astype(jnp.float32), query_weight.astype(jnp.float32), key_value_weight.astype(jnp.float32), output_weight.astype(jnp.float32), expert_gain.astype(jnp.float32), router_weight.astype(jnp.float32), gateup_weight.astype(jnp.float32), down_weight.astype(jnp.float32))
    grads = pullback(out_grad.astype(jnp.float32))
    return (mixed.astype(jnp.bfloat16), grads[0], grads[1], grads[2], grads[3], grads[4], grads[5], grads[6], grads[7], grads[8])
```

```python
import functools

import jax
import jax.numpy as jnp
from jax import lax
from jax.experimental import pallas as pl
from jax.experimental.pallas import tpu as pltpu
from jax.sharding import PartitionSpec as P

HEAD_SIZE = 64
TOPK = 8
SEQUENCE_LENGTH = 512


EPSILON = 1e-06
RESIDUAL = 0.22
ATTN_SCALE = 0.015625
ROPE_BASE = 10000.0
NEGATIVE = -1e30


def rotary_tables(length):
    half_dim = HEAD_SIZE // 2
    frequency = ROPE_BASE ** (-jnp.arange(half_dim, dtype=jnp.float32) * 2.0 / HEAD_SIZE)
    angles = jnp.arange(length, dtype=jnp.float32)[:, None] * frequency[None, :]
    return (jnp.cos(angles)[:, None, :], jnp.sin(angles)[:, None, :])


def rotate(value_rows, cosine, sine_table):
    half_dim = value_rows.shape[-1] // 2
    first = value_rows[..., :half_dim]
    second = value_rows[..., half_dim:]
    return jnp.concatenate(
        [first * cosine - second * sine_table, second * cosine + first * sine_table], axis=-1
    )


def rotate_back(grads, cosine, sine_table):
    half_dim = grads.shape[-1] // 2
    first = grads[..., :half_dim]
    second = grads[..., half_dim:]
    return jnp.concatenate(
        [first * cosine + second * sine_table, second * cosine - first * sine_table], axis=-1
    )


def norm_forward(value_rows):
    inv_rms = lax.rsqrt(jnp.mean(value_rows * value_rows, axis=-1, keepdims=True) + EPSILON)
    return (value_rows * inv_rms, inv_rms)


def norm_backward(grad_normed, gain, normal_unit, inv_rms):
    grad_unit = grad_normed * gain
    grad_input = inv_rms * (
        grad_unit - normal_unit * jnp.mean(grad_unit * normal_unit, axis=-1, keepdims=True)
    )
    return (grad_input, jnp.sum(grad_normed * normal_unit, axis=0))


def block_scores(query_block, key_block, row_start):
    scores = (
        jnp.einsum("sqjgd,skjd->sjgqk", query_block, key_block, preferred_element_type=jnp.float32)
        * ATTN_SCALE
    )
    row_ids = row_start + jnp.arange(query_block.shape[1])[:, None]
    col_ids = jnp.arange(key_block.shape[1])[None, :]
    return jnp.where(row_ids >= col_ids, scores, NEGATIVE)


def contract(left, right, left_dim, right_dim):
    return lax.dot_general(
        left, right, (((left_dim,), (right_dim,)), ((), ())), preferred_element_type=jnp.float32
    )


def experts_body(
    rows_ref,
    cot_ref,
    hits_ref,
    router_ref,
    gateup_ref,
    down_ref,
    comb_ref,
    grad_ref,
    act_ref,
    hidden_ref,
    gates_ref,
    comb_sum,
    grad_sum,
    dot_sum,
):
    step = pl.program_id(0)
    steps = pl.num_programs(0)
    hidden_units = down_ref.shape[1]
    feat_width = rows_ref.shape[1]
    number = lax.axis_index("expert") * steps + step
    lane = lax.broadcasted_iota(jnp.int32, hits_ref.shape, 1)

    @pl.when(step == 0)
    def _():
        hits = hits_ref[...] > 0
        logits = jnp.dot(rows_ref[...], router_ref[...], preferred_element_type=jnp.float32)
        logits = jnp.where(hits, logits, NEGATIVE)
        raised = jnp.where(hits, jnp.exp(logits - jnp.max(logits, axis=1, keepdims=True)), 0.0)
        gates_ref[...] = raised / jnp.sum(raised, axis=1, keepdims=True)

    rows = rows_ref[...]
    gate_part = jnp.dot(rows, gateup_ref[0, 0], preferred_element_type=jnp.float32)
    up_part = jnp.dot(rows, gateup_ref[0, 1], preferred_element_type=jnp.float32)
    raw = contract(cot_ref[...], down_ref[0], 1, 1)
    here = lane == number
    weight = jnp.sum(jnp.where(here, gates_ref[...], 0.0), axis=1, keepdims=True)
    sigmoid_gate = jax.nn.sigmoid(gate_part)
    silu_gate = gate_part * sigmoid_gate
    activation = silu_gate * up_part
    dots = jnp.where(here, jnp.sum(activation * raw, axis=1, keepdims=True), 0.0)
    weighted = (activation * weight).astype(jnp.bfloat16)
    act_ref[...] = weighted
    grad_act = raw * (RESIDUAL * weight)
    grad_gatepart = (
        grad_act * up_part * (sigmoid_gate * (1.0 + gate_part * (1.0 - sigmoid_gate)))
    ).astype(jnp.bfloat16)
    grad_uppart = (grad_act * silu_gate).astype(jnp.bfloat16)
    hidden_ref[:, :hidden_units] = grad_gatepart
    hidden_ref[:, hidden_units:] = grad_uppart
    comb = jnp.dot(weighted, down_ref[0], preferred_element_type=jnp.float32)
    grad = contract(grad_gatepart, gateup_ref[0, 0], 1, 1) + contract(
        grad_uppart, gateup_ref[0, 1], 1, 1
    )

    @pl.when(step == 0)
    def _():
        comb_sum[...] = comb
        grad_sum[...] = grad
        dot_sum[...] = dots

    @pl.when(step > 0)
    def _():
        comb_sum[...] += comb
        grad_sum[...] += grad
        dot_sum[...] += dots

    @pl.when(step == steps - 1)
    def _():
        comb_ref[...] = comb_sum[...].astype(jnp.bfloat16)
        grad_ref[:, :feat_width] = grad_sum[...].astype(jnp.bfloat16)
        grad_ref[:, feat_width:] = split_two(dot_sum[...])


def split_two(values):
    lane = lax.broadcasted_iota(jnp.int32, values.shape, 1)
    high = values.astype(jnp.bfloat16)
    low = values - high.astype(jnp.float32)
    half_lanes = values.shape[1] // 2
    moved = jnp.concatenate([low[:, half_lanes:], low[:, :half_lanes]], axis=1)
    return jnp.where(lane < half_lanes, high.astype(jnp.float32), moved).astype(jnp.bfloat16)


def experts(rows, cot, hits, router, gateup, down):
    count, feat_width = rows.shape
    local = gateup.shape[0]
    units = down.shape[1]
    lanes = hits.shape[1]
    whole = lambda step: (0, 0)
    return pl.pallas_call(
        experts_body,
        grid=(local,),
        in_specs=[
            pl.BlockSpec((count, feat_width), whole),
            pl.BlockSpec((count, feat_width), whole),
            pl.BlockSpec((count, lanes), whole),
            pl.BlockSpec((feat_width, lanes), whole),
            pl.BlockSpec((1, 2, feat_width, units), lambda step: (step, 0, 0, 0)),
            pl.BlockSpec((1, units, feat_width), lambda step: (step, 0, 0)),
        ],
        out_specs=[
            pl.BlockSpec((count, feat_width), whole),
            pl.BlockSpec((count, feat_width + lanes), whole),
            pl.BlockSpec((count, units), lambda step: (0, step)),
            pl.BlockSpec((count, 2 * units), lambda step: (0, step)),
            pl.BlockSpec((count, lanes), whole),
        ],
        out_shape=[
            jax.ShapeDtypeStruct((count, feat_width), jnp.bfloat16),
            jax.ShapeDtypeStruct((count, feat_width + lanes), jnp.bfloat16),
            jax.ShapeDtypeStruct((count, local * units), jnp.bfloat16),
            jax.ShapeDtypeStruct((count, local * 2 * units), jnp.bfloat16),
            jax.ShapeDtypeStruct((count, lanes), jnp.float32),
        ],
        scratch_shapes=[
            pltpu.VMEM((count, feat_width), jnp.float32),
            pltpu.VMEM((count, feat_width), jnp.float32),
            pltpu.VMEM((count, lanes), jnp.float32),
        ],
        compiler_params=pltpu.CompilerParams(vmem_limit_bytes=56 * 2**20),
        cost_estimate=pl.CostEstimate(
            flops=2 * count * feat_width * units * 6 * local,
            bytes_accessed=2 * (gateup.size + down.size) + 10 * count * feat_width,
            transcendentals=count * units * local,
        ),
    )(rows, cot, hits, router, gateup, down)


def weights_body(blocks, chunks, *refs):
    rows_refs, cot_refs = refs[:blocks], refs[blocks : 2 * blocks]
    act_refs, hidden_refs = refs[2 * blocks : 3 * blocks], refs[3 * blocks : 4 * blocks]
    gateup_ref, down_ref = refs[4 * blocks :]
    units = down_ref.shape[2]
    width = down_ref.shape[3]
    for part in range(2):
        total = sum(
            contract(rows_refs[b][...], hidden_refs[b][:, part * units : (part + 1) * units], 0, 0)
            for b in range(blocks)
        ).astype(jnp.bfloat16)
        for chunk in range(chunks):
            gateup_ref[chunk, 0, part] = total[chunk * width : (chunk + 1) * width]
    total = RESIDUAL * sum(
        contract(act_refs[b][...], cot_refs[b][...], 0, 0) for b in range(blocks)
    )
    total = total.astype(jnp.bfloat16)
    for chunk in range(chunks):
        down_ref[chunk, 0] = total[:, chunk * width : (chunk + 1) * width]


def expert_weights(rows, cots, acts, hiddens, chunks, local):
    blocks = len(rows)
    count, feat_width = rows[0].shape
    units = acts[0].shape[1] // local
    width = feat_width // chunks
    whole = lambda step: (0, 0)
    part = lambda step: (0, step)
    return pl.pallas_call(
        functools.partial(weights_body, blocks, chunks),
        grid=(local,),
        in_specs=[pl.BlockSpec((count, feat_width), whole)] * (2 * blocks)
        + [pl.BlockSpec((count, units), part)] * blocks
        + [pl.BlockSpec((count, 2 * units), part)] * blocks,
        out_specs=[
            pl.BlockSpec((chunks, 1, 2, width, units), lambda step: (0, step, 0, 0, 0)),
            pl.BlockSpec((chunks, 1, units, width), lambda step: (0, step, 0, 0)),
        ],
        out_shape=[
            jax.ShapeDtypeStruct((chunks, local, 2, width, units), jnp.bfloat16),
            jax.ShapeDtypeStruct((chunks, local, units, width), jnp.bfloat16),
        ],
        compiler_params=pltpu.CompilerParams(vmem_limit_bytes=56 * 2**20),
        cost_estimate=pl.CostEstimate(
            flops=2 * blocks * count * feat_width * units * 3 * local,
            bytes_accessed=4 * blocks * count * feat_width * 2 + 6 * local * units * feat_width,
            transcendentals=0,
        ),
    )(*rows, *cots, *acts, *hiddens)


def swap_cores(values):
    return lax.ppermute(values, "tensor", [(0, 1), (1, 0)])


def send_along(values, shift):
    count = lax.axis_size("expert")
    return lax.ppermute(values, "expert", [(i, (i + shift) % count) for i in range(count)])


def halving(values, steps, last):
    names = list(last)
    for axis, bit in steps:
        at = names.index((axis, bit))
        mine = (lax.axis_index(axis) >> bit) & 1
        keep = lax.dynamic_index_in_dim(values, mine, at, keepdims=False)
        send = lax.dynamic_index_in_dim(values, 1 - mine, at, keepdims=False)
        count = lax.axis_size(axis)
        got = lax.ppermute(send, axis, [(i, i ^ (1 << bit)) for i in range(count)])
        names.pop(at)
        values = keep.astype(jnp.float32) + got.astype(jnp.float32)
        if names:
            values = values.astype(send.dtype)
    return values


def bits_of(axis):
    return [(axis, bit) for bit in reversed(range(lax.axis_size(axis).bit_length() - 1))]


def per_device(
    tokens,
    out_grad,
    attn_gain,
    query_weight,
    key_value_weight,
    output_weight,
    expert_gain,
    router_weight,
    gateup_weight,
    down_weight,
    routes,
):
    tok_count, feat_width = tokens.shape
    expert_count = router_weight.shape[1]
    owners = lax.axis_size("expert")
    chunks = lax.axis_size("dp")
    core = lax.axis_index("tensor")
    local_experts = gateup_weight.shape[0]
    kv_heads = key_value_weight.shape[2] // HEAD_SIZE
    query_heads = query_weight.shape[1] // HEAD_SIZE
    groups = query_heads // kv_heads
    sequence_count = tok_count // SEQUENCE_LENGTH
    half = tok_count // 2
    lanes = 128
    dp_bits, owner_bits = bits_of("dp"), bits_of("expert")

    def halves(values):
        return (
            lax.dynamic_slice_in_dim(values, core * half, half, 0),
            lax.dynamic_slice_in_dim(values, (1 - core) * half, half, 0),
        )

    def in_order(mine, other):
        return jnp.where(
            core == 0,
            jnp.concatenate([mine, other], axis=0),
            jnp.concatenate([other, mine], axis=0),
        )

    def both_cores(mine):
        return jnp.concatenate([mine, swap_cores(mine)], axis=0)

    cot_mine, cot_other = halves(out_grad)
    cots = [jnp.concatenate([cot_mine, cot_other], axis=0)]
    hit_table = jnp.any(
        routes[:, :, None] == jnp.arange(lanes, dtype=jnp.int32)[None, None, :], axis=1
    ).astype(jnp.bfloat16)
    hits_mine, hits_other = halves(hit_table)
    hits = [jnp.concatenate([hits_mine, hits_other], axis=0)]
    for slot in range(1, owners):
        cots.append(both_cores(send_along(cot_mine, -slot)))
        hits.append(both_cores(send_along(hits_mine, -slot)))
    router_wide = jnp.pad(router_weight, ((0, 0), (0, lanes - expert_count)))

    cosine, sine_table = rotary_tables(SEQUENCE_LENGTH)
    inputs = tokens.astype(jnp.float32)
    unit_first, rms_first = norm_forward(inputs)
    normed = (unit_first * attn_gain).astype(jnp.bfloat16)
    queries = jnp.dot(normed, query_weight, preferred_element_type=jnp.float32)
    key_value = jnp.einsum(
        "td,cde->cte", normed, key_value_weight, preferred_element_type=jnp.float32
    )
    query_rot = (
        rotate(
            queries.reshape(sequence_count, SEQUENCE_LENGTH, query_heads, HEAD_SIZE),
            cosine,
            sine_table,
        )
        .astype(jnp.bfloat16)
        .reshape(sequence_count, SEQUENCE_LENGTH, kv_heads, groups, HEAD_SIZE)
    )
    keys_rot = rotate(
        key_value[0].reshape(sequence_count, SEQUENCE_LENGTH, kv_heads, HEAD_SIZE),
        cosine,
        sine_table,
    ).astype(jnp.bfloat16)
    value_rows = (
        key_value[1]
        .astype(jnp.bfloat16)
        .reshape(sequence_count, SEQUENCE_LENGTH, kv_heads, HEAD_SIZE)
    )
    scores = block_scores(query_rot, keys_rot, 0)
    row_max = jnp.max(scores, axis=-1, keepdims=True)
    exp_scores = jnp.exp(scores - row_max)
    row_sum = jnp.sum(exp_scores, axis=-1, keepdims=True)
    prob_block = (exp_scores / row_sum).astype(jnp.bfloat16)
    outputs = jnp.einsum(
        "sjgqk,skjd->sqjgd", prob_block, value_rows, preferred_element_type=jnp.float32
    )
    heads_out = outputs.astype(jnp.bfloat16).reshape(tok_count, query_heads * HEAD_SIZE)
    partial_value = jnp.dot(heads_out, output_weight, preferred_element_type=jnp.float32)

    part_mine, part_other = halves(partial_value)
    inputs_mine = halves(inputs)[0]
    middle = inputs_mine + RESIDUAL * (part_mine + swap_cores(part_other))
    unit_second, rms_second = norm_forward(middle)
    expert_in = (unit_second * expert_gain).astype(jnp.bfloat16)
    rows = [both_cores(expert_in)]
    for slot in range(1, owners):
        rows.append(both_cores(send_along(expert_in, -slot)))

    comb_total = jnp.zeros((half, feat_width), jnp.float32)
    grad_total = jnp.zeros((half, feat_width), jnp.float32)
    dots_total = jnp.zeros((half, lanes), jnp.float32)
    acts, hiddens = [None] * owners, [None] * owners
    gates = None
    for slot in range(owners):
        comb, grad, acts[slot], hiddens[slot], slot_gates = experts(
            rows[slot], cots[slot], hits[slot], router_wide, gateup_weight, down_weight
        )
        if slot == 0:
            gates = slot_gates[:half]
        comb = comb[:half].astype(jnp.float32) + swap_cores(comb[half:]).astype(jnp.float32)
        grad_other = swap_cores(grad[half:])
        grad_sum = grad[:half, :feat_width].astype(jnp.float32) + grad_other[
            :, :feat_width
        ].astype(jnp.float32)
        dots = grad[:half, feat_width:].astype(jnp.float32) + grad_other[:, feat_width:].astype(
            jnp.float32
        )
        if slot > 0:
            comb = send_along(comb.astype(jnp.bfloat16), slot).astype(jnp.float32)
            dots_whole = dots[:, : lanes // 2] + dots[:, lanes // 2 :]
            dots_whole = jnp.pad(dots_whole, ((0, 0), (0, lanes // 2)))
            back = send_along(
                jnp.concatenate([grad_sum.astype(jnp.bfloat16), split_two(dots_whole)], axis=1),
                slot,
            )
            grad_sum = back[:, :feat_width].astype(jnp.float32)
            dots = back[:, feat_width:].astype(jnp.float32)
        comb_total = comb_total + comb
        grad_total = grad_total + grad_sum
        dots_total = dots_total + dots

    mixed = (middle + RESIDUAL * comb_total).astype(jnp.bfloat16)
    output = in_order(mixed, swap_cores(mixed))

    gateup_grad, down_grad = expert_weights(rows, cots, acts, hiddens, chunks, local_experts)
    dp_shape = (2,) * len(dp_bits)
    parts = []
    for part in range(2):
        order = dp_bits if part == 0 else dp_bits[::-1]
        parts.append(
            (
                halving(
                    gateup_grad[:, :, part].reshape(dp_shape + (local_experts, feat_width // chunks, -1)),
                    order,
                    dp_bits,
                ),
                halving(
                    jnp.split(down_grad, 2, axis=2)[part].reshape(
                        dp_shape + (local_experts, -1, feat_width // chunks)
                    ),
                    order,
                    dp_bits,
                ),
            )
        )
    gateup_total = jnp.stack([parts[0][0], parts[1][0]], axis=1)
    down_total = jnp.concatenate([parts[0][1], parts[1][1]], axis=1)

    dots_whole = dots_total[:, : lanes // 2] + dots_total[:, lanes // 2 :]
    gates = gates[:, : lanes // 2]
    grad_gate = RESIDUAL * dots_whole
    grad_logits = gates * (grad_gate - jnp.sum(gates * grad_gate, axis=-1, keepdims=True))
    grad_logits = grad_logits[:, :expert_count].astype(jnp.bfloat16)
    grad_expert_in = grad_total + jnp.einsum(
        "te,de->td", grad_logits, router_weight, preferred_element_type=jnp.float32
    )
    router_grad = jnp.einsum(
        "te,td->ed", grad_logits, expert_in, preferred_element_type=jnp.float32
    )
    grad_middle_norm, expert_gain_grad = norm_backward(
        grad_expert_in, expert_gain, unit_second, rms_second
    )
    grad_middle = cot_mine.astype(jnp.float32) + grad_middle_norm
    grad_attn_mine = (RESIDUAL * grad_middle).astype(jnp.bfloat16)
    grad_attn = in_order(grad_attn_mine, swap_cores(grad_attn_mine))
    output_weight_grad = jnp.einsum(
        "td,te->de", grad_attn, heads_out, preferred_element_type=jnp.float32
    ).astype(jnp.bfloat16)
    grad_heads = (
        jnp.einsum("td,ed->te", grad_attn, output_weight, preferred_element_type=jnp.float32)
        .astype(jnp.bfloat16)
        .reshape(sequence_count, SEQUENCE_LENGTH, kv_heads, groups, HEAD_SIZE)
    )
    prob_block = exp_scores / row_sum
    grad_probs = jnp.einsum(
        "sqjgd,skjd->sjgqk", grad_heads, value_rows, preferred_element_type=jnp.float32
    )
    grad_values = jnp.einsum(
        "sjgqk,sqjgd->skjd",
        prob_block.astype(jnp.bfloat16),
        grad_heads,
        preferred_element_type=jnp.float32,
    )
    grad_scores = (
        prob_block * (grad_probs - jnp.sum(prob_block * grad_probs, axis=-1, keepdims=True))
    ).astype(jnp.bfloat16)
    grad_queries = (
        jnp.einsum("sjgqk,skjd->sqjgd", grad_scores, keys_rot, preferred_element_type=jnp.float32)
        * ATTN_SCALE
    )
    grad_keys = (
        jnp.einsum("sjgqk,sqjgd->skjd", grad_scores, query_rot, preferred_element_type=jnp.float32)
        * ATTN_SCALE
    )
    grad_query = (
        rotate_back(
            grad_queries.reshape(sequence_count, SEQUENCE_LENGTH, query_heads, HEAD_SIZE),
            cosine,
            sine_table,
        )
        .astype(jnp.bfloat16)
        .reshape(tok_count, query_heads * HEAD_SIZE)
    )
    grad_key = (
        rotate_back(grad_keys, cosine, sine_table)
        .astype(jnp.bfloat16)
        .reshape(tok_count, kv_heads * HEAD_SIZE)
    )
    grad_value = grad_values.astype(jnp.bfloat16).reshape(tok_count, kv_heads * HEAD_SIZE)
    grad_all = jnp.concatenate([grad_query, grad_key, grad_value], axis=1)
    weight_all = jnp.concatenate([query_weight, key_value_weight[0], key_value_weight[1]], axis=1)
    first_grad = jnp.einsum(
        "td,te->de", normed, grad_all, preferred_element_type=jnp.float32
    ).astype(jnp.bfloat16)
    grad_normed = jnp.einsum(
        "te,de->td", grad_all, weight_all, preferred_element_type=jnp.float32
    )
    normed_mine, normed_other = halves(grad_normed)
    grad_normed = normed_mine + swap_cores(normed_other.astype(jnp.bfloat16)).astype(jnp.float32)
    unit_mine, rms_mine = halves(unit_first)[0], halves(rms_first)[0]
    grad_first, attn_gain_grad = norm_backward(grad_normed, attn_gain, unit_mine, rms_mine)
    grad_tokens = grad_middle + grad_first
    tokens_grad = in_order(grad_tokens, swap_cores(grad_tokens))

    all_bits = dp_bits + owner_bits
    all_shape = (2,) * len(all_bits)
    pieces = chunks * owners

    def reduce_whole(values):
        columns = values.shape[1]
        out = []
        for part in range(2):
            order = (dp_bits if part == 0 else dp_bits[::-1]) + owner_bits[::-1]
            out.append(
                halving(
                    jnp.split(values, 2, axis=1)[part].reshape(
                        all_shape + (feat_width // pieces, columns // 2)
                    ),
                    order,
                    all_bits,
                )
            )
        return jnp.concatenate(out, axis=1)

    def reduce_small(values):
        values = values + swap_cores(values)
        values = values.reshape(values.shape[0], pieces, -1).transpose(1, 0, 2)
        return halving(values.reshape(all_shape + values.shape[1:]), all_bits[::-1], all_bits)

    output_total = reduce_whole(output_weight_grad).T
    first_total = reduce_whole(first_grad)
    small = reduce_small(jnp.concatenate([router_grad, expert_gain_grad[None]], axis=0))
    attn_gain_total = reduce_small(attn_gain_grad[None])[0]
    query_width = query_weight.shape[1]
    key_width = key_value_weight.shape[2]
    keyvalue_total = jnp.stack(
        [
            first_total[:, query_width : query_width + key_width],
            first_total[:, query_width + key_width :],
        ],
        axis=0,
    )
    return (
        output,
        tokens_grad,
        attn_gain_total,
        first_total[:, :query_width],
        keyvalue_total,
        output_total,
        small[expert_count],
        small[:expert_count].T,
        gateup_total,
        down_total,
    )


def solution(mesh):
    placed = (
        P(("dp", "expert"), None),
        P(("dp", "expert"), None),
        P(),
        P(None, "tensor"),
        P(None, None, "tensor"),
        P("tensor", None),
        P(),
        P(),
        P("expert", None, None, "tensor"),
        P("expert", "tensor", None),
        P(("dp", "expert"), None),
    )
    return jax.shard_map(
        per_device,
        mesh=mesh,
        in_specs=placed,
        out_specs=(
            P(("dp", "expert"), None),
            P(("dp", "expert"), None),
            P(("dp", "expert")),
            P(("dp", "expert"), "tensor"),
            P(None, ("dp", "expert"), "tensor"),
            P("tensor", ("dp", "expert")),
            P(("dp", "expert")),
            P(("dp", "expert"), None),
            P("expert", None, "dp", "tensor"),
            P("expert", "tensor", "dp"),
        ),
        check_vma=False,
    )
```

```python
import functools

import jax
import jax.numpy as jnp
from jax import lax
from jax.experimental import pallas as pl
from jax.experimental.pallas import tpu as pltpu
from jax.sharding import PartitionSpec as P

HEAD_SIZE = 64
TOPK = 8
SEQUENCE_LENGTH = 512


EPSILON = 1e-06
RESIDUAL = 0.22
ATTN_SCALE = 0.015625
ROPE_BASE = 10000.0
NEGATIVE = -1e30


def rotary_tables(length):
    half_dim = HEAD_SIZE // 2
    frequency = ROPE_BASE ** (-jnp.arange(half_dim, dtype=jnp.float32) * 2.0 / HEAD_SIZE)
    angles = jnp.arange(length, dtype=jnp.float32)[:, None] * frequency[None, :]
    return (jnp.cos(angles)[:, None, :], jnp.sin(angles)[:, None, :])


def rotate(value_rows, cosine, sine_table):
    half_dim = value_rows.shape[-1] // 2
    first = value_rows[..., :half_dim]
    second = value_rows[..., half_dim:]
    return jnp.concatenate(
        [first * cosine - second * sine_table, second * cosine + first * sine_table], axis=-1
    )


def rotate_back(grads, cosine, sine_table):
    half_dim = grads.shape[-1] // 2
    first = grads[..., :half_dim]
    second = grads[..., half_dim:]
    return jnp.concatenate(
        [first * cosine + second * sine_table, second * cosine - first * sine_table], axis=-1
    )


def norm_forward(value_rows):
    inv_rms = lax.rsqrt(jnp.mean(value_rows * value_rows, axis=-1, keepdims=True) + EPSILON)
    return (value_rows * inv_rms, inv_rms)


def norm_backward(grad_normed, gain, normal_unit, inv_rms):
    grad_unit = grad_normed * gain
    grad_input = inv_rms * (
        grad_unit - normal_unit * jnp.mean(grad_unit * normal_unit, axis=-1, keepdims=True)
    )
    return (grad_input, jnp.sum(grad_normed * normal_unit, axis=0))


def block_scores(query_block, key_block, row_start):
    scores = (
        jnp.einsum("sqjgd,skjd->sjgqk", query_block, key_block, preferred_element_type=jnp.float32)
        * ATTN_SCALE
    )
    row_ids = row_start + jnp.arange(query_block.shape[1])[:, None]
    col_ids = jnp.arange(key_block.shape[1])[None, :]
    return jnp.where(row_ids >= col_ids, scores, NEGATIVE)


def contract(left, right, left_dim, right_dim):
    return lax.dot_general(
        left, right, (((left_dim,), (right_dim,)), ((), ())), preferred_element_type=jnp.float32
    )


def split_two(values):
    lane = lax.broadcasted_iota(jnp.int32, values.shape, 1)
    high = values.astype(jnp.bfloat16).astype(jnp.float32)
    low = values - high
    half_lanes = values.shape[1] // 2
    moved = jnp.concatenate([low[:, half_lanes:], low[:, :half_lanes]], axis=1)
    return jnp.where(lane < half_lanes, high, moved).astype(jnp.bfloat16)


def block_order(me, count, turn):
    left, right = me, count - 1 - me
    near = jnp.minimum(left, right)
    sign = jnp.where(left <= right, -1, 1)
    paired = turn <= 2 * near
    distance = jnp.where(paired, (turn + 1) // 2, turn - near)
    toward = jnp.where(paired & (turn % 2 == 1), sign, -sign)
    return me + toward * distance


def expert_kernel(
    owners,
    local,
    chunks,
    rows_hbm,
    cot_hbm,
    router_ref,
    gateup_hbm,
    down_hbm,
    parts_hbm,
    comb_hbm,
    gates_out,
    gateup_grad_hbm,
    down_grad_hbm,
    act_hbm,
    hidden_hbm,
    rows_all,
    cot_all,
    gateup_ref,
    down_ref,
    gates_ref,
    send_grad,
    send_comb,
    recv_grad,
    recv_comb,
    load_sem,
    weight_sem,
    chain_send,
    chain_recv,
    swap_send,
    swap_recv,
    sums_send,
    grad_recv,
    comb_recv,
    back_send,
    back_recv,
    comb_sem,
    stage_sem,
):
    me = lax.axis_index("expert")
    core = lax.axis_index("tensor")
    sibling = {"tensor": 1 - core}
    total, feat_width = rows_all.shape[1], rows_all.shape[2]
    half = total // 2
    units = down_ref.shape[1]
    lanes = gates_ref.shape[1]
    mine = pl.ds(pl.multiple_of(core * half, half), half)
    others = pl.ds(pl.multiple_of((1 - core) * half, half), half)

    barrier = pltpu.get_barrier_semaphore()
    pl.semaphore_signal(barrier, inc=1, device_id=sibling, device_id_type=pl.DeviceIdType.MESH)
    for shift in range(1, owners):
        pl.semaphore_signal(
            barrier,
            inc=1,
            device_id={"expert": lax.rem(me + shift, owners)},
            device_id_type=pl.DeviceIdType.MESH,
        )

    def remote(src, dst, send, recv, device):
        return pltpu.make_async_remote_copy(
            src_ref=src,
            dst_ref=dst,
            send_sem=send,
            recv_sem=recv,
            device_id=device,
            device_id_type=pl.DeviceIdType.MESH,
        )

    own_rows = pltpu.make_async_copy(rows_hbm, rows_all.at[me, mine], load_sem.at[0])
    own_cot = pltpu.make_async_copy(cot_hbm, cot_all.at[me], load_sem.at[1])
    own_rows.start()
    own_cot.start()
    for expert in range(local):
        pltpu.make_async_copy(
            gateup_hbm.at[expert], gateup_ref.at[expert], weight_sem.at[0, expert]
        ).start()
        pltpu.make_async_copy(
            down_hbm.at[expert], down_ref.at[expert], weight_sem.at[1, expert]
        ).start()
    pl.semaphore_wait(barrier, owners)
    own_rows.wait()
    own_cot.wait()

    buffers = (rows_all, cot_all)

    def chain(step, what, side):
        block = me - side * (step - 1)
        to = me + side
        there = (block >= 0) & (block < owners) & (to >= 0) & (to < owners)
        safe = jnp.clip(block, 0, owners - 1)
        at = 0 if side == 1 else 1
        copy = remote(
            buffers[what].at[safe, mine],
            buffers[what].at[safe, mine],
            chain_send.at[what, step - 1, at],
            chain_recv.at[what, safe],
            {"expert": jnp.clip(to, 0, owners - 1)},
        )
        return there, copy

    def swap(what, block):
        return remote(
            buffers[what].at[block, mine],
            buffers[what].at[block, mine],
            swap_send.at[what, block],
            swap_recv.at[what, block],
            sibling,
        )

    def swap_arrival(what, block):
        return remote(
            buffers[what].at[block, others],
            buffers[what].at[block, others],
            swap_send.at[what, block],
            swap_recv.at[what, block],
            sibling,
        )

    def send_step(step):
        for what in range(2):
            for side in (1, -1):
                there, copy = chain(step, what, side)

                @pl.when(there)
                def _():
                    copy.start()

    def arrivals(step):
        for what in range(2):
            for side in (1, -1):
                block = me - side * step
                there = (block >= 0) & (block < owners)
                safe = jnp.clip(block, 0, owners - 1)

                @pl.when(there)
                def _():
                    chain_copy = remote(
                        buffers[what].at[safe, mine],
                        buffers[what].at[safe, mine],
                        chain_send.at[what, step - 1, 0],
                        chain_recv.at[what, safe],
                        sibling,
                    )
                    chain_copy.wait_recv()
                    swap(what, safe).start()

    swap(0, me).start()
    send_step(1)

    def expert_phase(comb_sum, grad_sum, dot_sum, hold_comb, hold_grad, hold_dot, act_stage, hidden_stage):
        lane = lax.broadcasted_iota(jnp.int32, (total, lanes), 1)

        def stage_copies(slot, expert, block):
            return (
                pltpu.make_async_copy(
                    act_stage.at[slot], act_hbm.at[expert, block], stage_sem.at[0, slot]
                ),
                pltpu.make_async_copy(
                    hidden_stage.at[slot], hidden_hbm.at[expert, block], stage_sem.at[1, slot]
                ),
            )

        def sums_copies(turn):
            return (
                remote(send_grad, recv_grad.at[turn], sums_send.at[0], grad_recv.at[turn], sibling),
                remote(send_comb, recv_comb.at[turn], sums_send.at[1], comb_recv.at[turn], sibling),
            )

        def back_copy(turn, block):
            return remote(
                recv_grad.at[turn],
                parts_hbm.at[me],
                back_send.at[turn],
                back_recv.at[me],
                {"expert": block},
            )

        def own_back():
            return pltpu.make_async_copy(recv_grad.at[0], parts_hbm.at[me], back_send.at[0])

        def comb_copy(turn, block):
            return pltpu.make_async_copy(
                recv_comb.at[turn],
                comb_hbm.at[lax.rem(block - me + owners, owners)],
                comb_sem.at[turn],
            )

        def settle(turn):
            block = block_order(me, owners, turn)
            copy_grad, copy_comb = sums_copies(turn)
            copy_grad.wait_recv()
            got = recv_grad[turn].astype(jnp.float32)
            recv_grad[turn, :, :feat_width] = (hold_grad[...] + got[:, :feat_width]).astype(
                jnp.bfloat16
            )
            dots = hold_dot[...] + got[:, feat_width:]
            lower = lanes // 2
            dots = dots + jnp.concatenate([dots[:, lower:], dots[:, :lower]], axis=1)
            low_lane = lax.broadcasted_iota(jnp.int32, (half, lanes), 1) < lower
            recv_grad[turn, :, feat_width:] = split_two(jnp.where(low_lane, dots, 0.0))

            @pl.when(turn > 0)
            def _():
                back_copy(turn, block).start()

            @pl.when(turn == 0)
            def _():
                own_back().start()

            copy_comb.wait_recv()
            recv_comb[turn] = (hold_comb[...] + recv_comb[turn].astype(jnp.float32)).astype(
                jnp.bfloat16
            )
            comb_copy(turn, block).start()

        def body(number, carry):
            turn = number // local
            expert = number % local
            block = block_order(me, owners, turn)
            slot = number % 2

            @pl.when(expert == 0)
            def _():
                swap_arrival_needed = turn > 0

                @pl.when(swap_arrival_needed)
                def _():
                    swap_arrival(1, block).wait_recv()

                swap_arrival(0, block).wait_recv()
                hits = cot_all[block, :, feat_width:].astype(jnp.float32) > 0.5
                logits = jnp.dot(
                    rows_all[block], router_ref[...], preferred_element_type=jnp.float32
                )
                logits = jnp.where(hits, logits, NEGATIVE)
                raised = jnp.where(
                    hits, jnp.exp(logits - jnp.max(logits, axis=1, keepdims=True)), 0.0
                )
                gates_ref[...] = raised / jnp.sum(raised, axis=1, keepdims=True)

                @pl.when(turn == 0)
                def _():
                    gates_out[...] = gates_ref[mine]

            @pl.when(number < local)
            def _():
                pltpu.make_async_copy(
                    gateup_hbm.at[expert], gateup_ref.at[expert], weight_sem.at[0, expert]
                ).wait()
                pltpu.make_async_copy(
                    down_hbm.at[expert], down_ref.at[expert], weight_sem.at[1, expert]
                ).wait()

            @pl.when(number >= 2)
            def _():
                for copy in stage_copies(slot, expert, block):
                    copy.wait()

            rows = rows_all[block]
            gate_weight, up_weight, down = (
                gateup_ref[expert, 0],
                gateup_ref[expert, 1],
                down_ref[expert],
            )
            gate_part = jnp.dot(rows, gate_weight, preferred_element_type=jnp.float32)
            up_part = jnp.dot(rows, up_weight, preferred_element_type=jnp.float32)
            raw = contract(cot_all[block, :, :feat_width], down, 1, 1)
            here = lane == me * local + expert
            weight = jnp.sum(jnp.where(here, gates_ref[...], 0.0), axis=1, keepdims=True)
            sigmoid_gate = jax.nn.sigmoid(gate_part)
            silu_gate = gate_part * sigmoid_gate
            activation = silu_gate * up_part
            dots = jnp.where(here, jnp.sum(activation * raw, axis=1, keepdims=True), 0.0)
            weighted = (activation * weight).astype(jnp.bfloat16)
            act_stage[slot] = weighted
            grad_act = raw * (RESIDUAL * weight)
            grad_gatepart = (
                grad_act * up_part * (sigmoid_gate * (1.0 + gate_part * (1.0 - sigmoid_gate)))
            ).astype(jnp.bfloat16)
            grad_uppart = (grad_act * silu_gate).astype(jnp.bfloat16)
            hidden_stage[slot, :, :units] = grad_gatepart
            hidden_stage[slot, :, units:] = grad_uppart
            for copy in stage_copies(slot, expert, block):
                copy.start()
            comb = jnp.dot(weighted, down, preferred_element_type=jnp.float32)
            grad = contract(grad_gatepart, gate_weight, 1, 1) + contract(
                grad_uppart, up_weight, 1, 1
            )

            @pl.when(expert == 0)
            def _():
                comb_sum[...] = comb
                grad_sum[...] = grad
                dot_sum[...] = dots

            @pl.when(expert > 0)
            def _():
                comb_sum[...] += comb
                grad_sum[...] += grad
                dot_sum[...] += dots

            @pl.when((expert == 1) & (turn > 0))
            def _():
                settle(turn - 1)

            for step in range(1, owners):

                @pl.when(number == step * local - 2)
                def _():
                    arrivals(step)
                    if step + 1 < owners:
                        send_step(step + 1)

            @pl.when(expert == local - 1)
            def _():
                @pl.when(turn > 0)
                def _():
                    for copy in sums_copies(turn):
                        copy.wait_send()

                send_grad[:, :feat_width] = grad_sum[others].astype(jnp.bfloat16)
                send_grad[:, feat_width:] = split_two(dot_sum[others])
                send_comb[...] = comb_sum[others].astype(jnp.bfloat16)
                for copy in sums_copies(turn):
                    copy.start()
                hold_grad[...] = grad_sum[mine]
                hold_comb[...] = comb_sum[mine]
                hold_dot[...] = dot_sum[mine]

            return carry

        lax.fori_loop(0, owners * local, body, 0)
        settle(owners - 1)
        for copy in sums_copies(owners - 1):
            copy.wait_send()
        for slot in range(2):
            for copy in stage_copies(slot, 0, 0):
                copy.wait()
        for turn in range(owners):
            block = block_order(me, owners, turn)
            comb_copy(turn, block).wait()

    pl.run_scoped(
        expert_phase,
        pltpu.VMEM((total, feat_width), jnp.float32),
        pltpu.VMEM((total, feat_width), jnp.float32),
        pltpu.VMEM((total, lanes), jnp.float32),
        pltpu.VMEM((half, feat_width), jnp.float32),
        pltpu.VMEM((half, feat_width), jnp.float32),
        pltpu.VMEM((half, lanes), jnp.float32),
        pltpu.VMEM((2, total, units), jnp.bfloat16),
        pltpu.VMEM((2, total, 2 * units), jnp.bfloat16),
    )

    width = feat_width // chunks

    def weights_body(act_ref, hidden_ref, gateup_out, down_out):
        up_sum = sum(contract(rows_all[b], hidden_ref[0, b], 0, 0) for b in range(owners))
        up_sum = up_sum.astype(jnp.bfloat16)
        for chunk in range(chunks):
            for part in range(2):
                gateup_out[chunk, 0, part] = up_sum[
                    chunk * width : (chunk + 1) * width, part * units : (part + 1) * units
                ]
        down_sum = sum(
            contract(act_ref[0, b], cot_all[b, :, :feat_width], 0, 0) for b in range(owners)
        )
        down_sum = (RESIDUAL * down_sum).astype(jnp.bfloat16)
        for chunk in range(chunks):
            down_out[chunk, 0] = down_sum[:, chunk * width : (chunk + 1) * width]

    pltpu.emit_pipeline(
        weights_body,
        grid=(local,),
        in_specs=[
            pl.BlockSpec((1, owners, total, units), lambda e: (e, 0, 0, 0)),
            pl.BlockSpec((1, owners, total, 2 * units), lambda e: (e, 0, 0, 0)),
        ],
        out_specs=[
            pl.BlockSpec((chunks, 1, 2, width, units), lambda e: (0, e, 0, 0, 0)),
            pl.BlockSpec((chunks, 1, units, width), lambda e: (0, e, 0, 0)),
        ],
    )(act_hbm, hidden_hbm, gateup_grad_hbm, down_grad_hbm)

    swap(0, me).wait_send()
    for step in range(1, owners):
        for what in range(2):
            for side in (1, -1):
                there, copy = chain(step, what, side)

                @pl.when(there)
                def _():
                    copy.wait_send()

                block = me - side * step
                arrived = (block >= 0) & (block < owners)
                safe = jnp.clip(block, 0, owners - 1)

                @pl.when(arrived)
                def _():
                    swap(what, safe).wait_send()

    pltpu.make_async_copy(recv_grad.at[0], parts_hbm.at[me], back_send.at[0]).wait()
    for turn in range(1, owners):
        block = block_order(me, owners, turn)
        remote(
            recv_grad.at[turn],
            parts_hbm.at[me],
            back_send.at[turn],
            back_recv.at[me],
            {"expert": block},
        ).wait_send()
        source = lax.rem(me + turn, owners)
        remote(
            recv_grad.at[turn],
            parts_hbm.at[source],
            back_send.at[turn],
            back_recv.at[source],
            {"expert": source},
        ).wait_recv()


def experts(rows, cot, router, gateup, down, owners, chunks):
    half, feat_width = rows.shape
    total = 2 * half
    local, units = down.shape[0], down.shape[1]
    lanes = router.shape[1]
    wide = feat_width + lanes
    any_space = pl.BlockSpec(memory_space=pl.ANY)
    in_vmem = pl.BlockSpec(memory_space=pltpu.VMEM)
    bf16 = jnp.bfloat16
    return pl.pallas_call(
        functools.partial(expert_kernel, owners, local, chunks),
        in_specs=[any_space, any_space, in_vmem, any_space, any_space],
        out_specs=[any_space, any_space, in_vmem, any_space, any_space, any_space, any_space],
        out_shape=[
            jax.ShapeDtypeStruct((owners, half, wide), bf16),
            jax.ShapeDtypeStruct((owners, half, feat_width), bf16),
            jax.ShapeDtypeStruct((half, lanes), jnp.float32),
            jax.ShapeDtypeStruct((chunks, local, 2, feat_width // chunks, units), bf16),
            jax.ShapeDtypeStruct((chunks, local, units, feat_width // chunks), bf16),
            jax.ShapeDtypeStruct((local, owners, total, units), bf16),
            jax.ShapeDtypeStruct((local, owners, total, 2 * units), bf16),
        ],
        scratch_shapes=[
            pltpu.VMEM((owners, total, feat_width), bf16),
            pltpu.VMEM((owners, total, wide), bf16),
            pltpu.VMEM((local, 2, feat_width, units), bf16),
            pltpu.VMEM((local, units, feat_width), bf16),
            pltpu.VMEM((total, lanes), jnp.float32),
            pltpu.VMEM((half, wide), bf16),
            pltpu.VMEM((half, feat_width), bf16),
            pltpu.VMEM((owners, half, wide), bf16),
            pltpu.VMEM((owners, half, feat_width), bf16),
            pltpu.SemaphoreType.DMA((2,)),
            pltpu.SemaphoreType.DMA((2, local)),
            pltpu.SemaphoreType.DMA((2, owners - 1, 2)),
            pltpu.SemaphoreType.DMA((2, owners)),
            pltpu.SemaphoreType.DMA((2, owners)),
            pltpu.SemaphoreType.DMA((2, owners)),
            pltpu.SemaphoreType.DMA((2,)),
            pltpu.SemaphoreType.DMA((owners,)),
            pltpu.SemaphoreType.DMA((owners,)),
            pltpu.SemaphoreType.DMA((owners,)),
            pltpu.SemaphoreType.DMA((owners,)),
            pltpu.SemaphoreType.DMA((owners,)),
            pltpu.SemaphoreType.DMA((2, 2)),
        ],
        compiler_params=pltpu.CompilerParams(
            vmem_limit_bytes=60 * 2**20, collective_id=0, has_side_effects=True
        ),
        cost_estimate=pl.CostEstimate(
            flops=2 * owners * total * feat_width * units * 9 * local,
            bytes_accessed=80 * 2**20,
            transcendentals=owners * total * units * local,
        ),
    )(rows, cot, router, gateup, down)


def swap_cores(values):
    return lax.ppermute(values, "tensor", [(0, 1), (1, 0)])


def send_along(values, shift):
    count = lax.axis_size("expert")
    return lax.ppermute(values, "expert", [(i, (i + shift) % count) for i in range(count)])


def halving(values, steps, last):
    names = list(last)
    for axis, bit in steps:
        at = names.index((axis, bit))
        mine = (lax.axis_index(axis) >> bit) & 1
        keep = lax.dynamic_index_in_dim(values, mine, at, keepdims=False)
        send = lax.dynamic_index_in_dim(values, 1 - mine, at, keepdims=False)
        count = lax.axis_size(axis)
        got = lax.ppermute(send, axis, [(i, i ^ (1 << bit)) for i in range(count)])
        names.pop(at)
        values = keep.astype(jnp.float32) + got.astype(jnp.float32)
        if names:
            values = values.astype(send.dtype)
    return values


def bits_of(axis):
    return [(axis, bit) for bit in reversed(range(lax.axis_size(axis).bit_length() - 1))]


def per_device(
    tokens,
    out_grad,
    attn_gain,
    query_weight,
    key_value_weight,
    output_weight,
    expert_gain,
    router_weight,
    gateup_weight,
    down_weight,
    routes,
):
    tok_count, feat_width = tokens.shape
    expert_count = router_weight.shape[1]
    owners = lax.axis_size("expert")
    chunks = lax.axis_size("dp")
    core = lax.axis_index("tensor")
    local_experts = gateup_weight.shape[0]
    kv_heads = key_value_weight.shape[2] // HEAD_SIZE
    query_heads = query_weight.shape[1] // HEAD_SIZE
    groups = query_heads // kv_heads
    sequence_count = tok_count // SEQUENCE_LENGTH
    half = tok_count // 2
    lanes = 128
    dp_bits, owner_bits = bits_of("dp"), bits_of("expert")

    def halves(values):
        return (
            lax.dynamic_slice_in_dim(values, core * half, half, 0),
            lax.dynamic_slice_in_dim(values, (1 - core) * half, half, 0),
        )

    def in_order(mine, other):
        return jnp.where(
            core == 0,
            jnp.concatenate([mine, other], axis=0),
            jnp.concatenate([other, mine], axis=0),
        )

    cot_mine, _ = halves(out_grad)
    hit_table = jnp.any(
        routes[:, :, None] == jnp.arange(lanes, dtype=jnp.int32)[None, None, :], axis=1
    ).astype(jnp.bfloat16)
    cot_wide = jnp.concatenate([out_grad, hit_table], axis=1)
    router_wide = jnp.pad(router_weight, ((0, 0), (0, lanes - expert_count)))

    cosine, sine_table = rotary_tables(SEQUENCE_LENGTH)
    inputs = tokens.astype(jnp.float32)
    unit_first, rms_first = norm_forward(inputs)
    normed = (unit_first * attn_gain).astype(jnp.bfloat16)
    queries = jnp.dot(normed, query_weight, preferred_element_type=jnp.float32)
    key_value = jnp.einsum(
        "td,cde->cte", normed, key_value_weight, preferred_element_type=jnp.float32
    )
    query_rot = (
        rotate(
            queries.reshape(sequence_count, SEQUENCE_LENGTH, query_heads, HEAD_SIZE),
            cosine,
            sine_table,
        )
        .astype(jnp.bfloat16)
        .reshape(sequence_count, SEQUENCE_LENGTH, kv_heads, groups, HEAD_SIZE)
    )
    keys_rot = rotate(
        key_value[0].reshape(sequence_count, SEQUENCE_LENGTH, kv_heads, HEAD_SIZE),
        cosine,
        sine_table,
    ).astype(jnp.bfloat16)
    value_rows = (
        key_value[1]
        .astype(jnp.bfloat16)
        .reshape(sequence_count, SEQUENCE_LENGTH, kv_heads, HEAD_SIZE)
    )
    scores = block_scores(query_rot, keys_rot, 0)
    row_max = jnp.max(scores, axis=-1, keepdims=True)
    exp_scores = jnp.exp(scores - row_max)
    row_sum = jnp.sum(exp_scores, axis=-1, keepdims=True)
    prob_block = (exp_scores / row_sum).astype(jnp.bfloat16)
    outputs = jnp.einsum(
        "sjgqk,skjd->sqjgd", prob_block, value_rows, preferred_element_type=jnp.float32
    )
    heads_out = outputs.astype(jnp.bfloat16).reshape(tok_count, query_heads * HEAD_SIZE)
    partial_value = jnp.dot(heads_out, output_weight, preferred_element_type=jnp.float32)

    part_mine, part_other = halves(partial_value)
    inputs_mine = halves(inputs)[0]
    middle = inputs_mine + RESIDUAL * (part_mine + swap_cores(part_other))
    unit_second, rms_second = norm_forward(middle)
    expert_in = (unit_second * expert_gain).astype(jnp.bfloat16)

    parts, combs, gates, gateup_grad, down_grad, _, _ = experts(
        expert_in, cot_wide, router_wide, gateup_weight, down_weight, owners, chunks
    )
    comb_total = combs[0].astype(jnp.float32)
    for slot in range(1, owners):
        comb_total = comb_total + send_along(combs[slot], slot).astype(jnp.float32)
    grad_total = jnp.sum(parts[:, :, :feat_width].astype(jnp.float32), axis=0)
    dots_total = jnp.sum(parts[:, :, feat_width:].astype(jnp.float32), axis=0)

    mixed = (middle + RESIDUAL * comb_total).astype(jnp.bfloat16)
    output = in_order(mixed, swap_cores(mixed))

    dp_shape = (2,) * len(dp_bits)
    parts = []
    for part in range(2):
        order = dp_bits if part == 0 else dp_bits[::-1]
        parts.append(
            (
                halving(
                    gateup_grad[:, :, part].reshape(dp_shape + (local_experts, feat_width // chunks, -1)),
                    order,
                    dp_bits,
                ),
                halving(
                    jnp.split(down_grad, 2, axis=2)[part].reshape(
                        dp_shape + (local_experts, -1, feat_width // chunks)
                    ),
                    order,
                    dp_bits,
                ),
            )
        )
    gateup_total = jnp.stack([parts[0][0], parts[1][0]], axis=1)
    down_total = jnp.concatenate([parts[0][1], parts[1][1]], axis=1)

    dots_whole = dots_total[:, : lanes // 2] + dots_total[:, lanes // 2 :]
    gates = gates[:, : lanes // 2]
    grad_gate = RESIDUAL * dots_whole
    grad_logits = gates * (grad_gate - jnp.sum(gates * grad_gate, axis=-1, keepdims=True))
    grad_logits = grad_logits[:, :expert_count].astype(jnp.bfloat16)
    grad_expert_in = grad_total + jnp.einsum(
        "te,de->td", grad_logits, router_weight, preferred_element_type=jnp.float32
    )
    router_grad = jnp.einsum(
        "te,td->ed", grad_logits, expert_in, preferred_element_type=jnp.float32
    )
    grad_middle_norm, expert_gain_grad = norm_backward(
        grad_expert_in, expert_gain, unit_second, rms_second
    )
    grad_middle = cot_mine.astype(jnp.float32) + grad_middle_norm
    grad_attn_mine = (RESIDUAL * grad_middle).astype(jnp.bfloat16)
    grad_attn = in_order(grad_attn_mine, swap_cores(grad_attn_mine))
    output_weight_grad = jnp.einsum(
        "td,te->de", grad_attn, heads_out, preferred_element_type=jnp.float32
    ).astype(jnp.bfloat16)
    grad_heads = (
        jnp.einsum("td,ed->te", grad_attn, output_weight, preferred_element_type=jnp.float32)
        .astype(jnp.bfloat16)
        .reshape(sequence_count, SEQUENCE_LENGTH, kv_heads, groups, HEAD_SIZE)
    )
    prob_block = exp_scores / row_sum
    grad_probs = jnp.einsum(
        "sqjgd,skjd->sjgqk", grad_heads, value_rows, preferred_element_type=jnp.float32
    )
    grad_values = jnp.einsum(
        "sjgqk,sqjgd->skjd",
        prob_block.astype(jnp.bfloat16),
        grad_heads,
        preferred_element_type=jnp.float32,
    )
    grad_scores = (
        prob_block * (grad_probs - jnp.sum(prob_block * grad_probs, axis=-1, keepdims=True))
    ).astype(jnp.bfloat16)
    grad_queries = (
        jnp.einsum("sjgqk,skjd->sqjgd", grad_scores, keys_rot, preferred_element_type=jnp.float32)
        * ATTN_SCALE
    )
    grad_keys = (
        jnp.einsum("sjgqk,sqjgd->skjd", grad_scores, query_rot, preferred_element_type=jnp.float32)
        * ATTN_SCALE
    )
    grad_query = (
        rotate_back(
            grad_queries.reshape(sequence_count, SEQUENCE_LENGTH, query_heads, HEAD_SIZE),
            cosine,
            sine_table,
        )
        .astype(jnp.bfloat16)
        .reshape(tok_count, query_heads * HEAD_SIZE)
    )
    grad_key = (
        rotate_back(grad_keys, cosine, sine_table)
        .astype(jnp.bfloat16)
        .reshape(tok_count, kv_heads * HEAD_SIZE)
    )
    grad_value = grad_values.astype(jnp.bfloat16).reshape(tok_count, kv_heads * HEAD_SIZE)
    grad_all = jnp.concatenate([grad_query, grad_key, grad_value], axis=1)
    weight_all = jnp.concatenate([query_weight, key_value_weight[0], key_value_weight[1]], axis=1)
    first_grad = jnp.einsum(
        "td,te->de", normed, grad_all, preferred_element_type=jnp.float32
    ).astype(jnp.bfloat16)
    grad_normed = jnp.einsum(
        "te,de->td", grad_all, weight_all, preferred_element_type=jnp.float32
    )
    normed_mine, normed_other = halves(grad_normed)
    grad_normed = normed_mine + swap_cores(normed_other.astype(jnp.bfloat16)).astype(jnp.float32)
    unit_mine, rms_mine = halves(unit_first)[0], halves(rms_first)[0]
    grad_first, attn_gain_grad = norm_backward(grad_normed, attn_gain, unit_mine, rms_mine)
    grad_tokens = grad_middle + grad_first
    tokens_grad = in_order(grad_tokens, swap_cores(grad_tokens))

    all_bits = dp_bits + owner_bits
    all_shape = (2,) * len(all_bits)
    pieces = chunks * owners

    def reduce_whole(values):
        columns = values.shape[1]
        out = []
        for part in range(2):
            order = (dp_bits if part == 0 else dp_bits[::-1]) + owner_bits[::-1]
            out.append(
                halving(
                    jnp.split(values, 2, axis=1)[part].reshape(
                        all_shape + (feat_width // pieces, columns // 2)
                    ),
                    order,
                    all_bits,
                )
            )
        return jnp.concatenate(out, axis=1)

    def reduce_small(values):
        values = values + swap_cores(values)
        values = values.reshape(values.shape[0], pieces, -1).transpose(1, 0, 2)
        return halving(values.reshape(all_shape + values.shape[1:]), all_bits[::-1], all_bits)

    output_total = reduce_whole(output_weight_grad).T
    first_total = reduce_whole(first_grad)
    small = reduce_small(jnp.concatenate([router_grad, expert_gain_grad[None]], axis=0))
    attn_gain_total = reduce_small(attn_gain_grad[None])[0]
    query_width = query_weight.shape[1]
    key_width = key_value_weight.shape[2]
    keyvalue_total = jnp.stack(
        [
            first_total[:, query_width : query_width + key_width],
            first_total[:, query_width + key_width :],
        ],
        axis=0,
    )
    return (
        output,
        tokens_grad,
        attn_gain_total,
        first_total[:, :query_width],
        keyvalue_total,
        output_total,
        small[expert_count],
        small[:expert_count].T,
        gateup_total,
        down_total,
    )


def solution(mesh):
    placed = (
        P(("dp", "expert"), None),
        P(("dp", "expert"), None),
        P(),
        P(None, "tensor"),
        P(None, None, "tensor"),
        P("tensor", None),
        P(),
        P(),
        P("expert", None, None, "tensor"),
        P("expert", "tensor", None),
        P(("dp", "expert"), None),
    )
    return jax.shard_map(
        per_device,
        mesh=mesh,
        in_specs=placed,
        out_specs=(
            P(("dp", "expert"), None),
            P(("dp", "expert"), None),
            P(("dp", "expert")),
            P(("dp", "expert"), "tensor"),
            P(None, ("dp", "expert"), "tensor"),
            P("tensor", ("dp", "expert")),
            P(("dp", "expert")),
            P(("dp", "expert"), None),
            P("expert", None, "dp", "tensor"),
            P("expert", "tensor", "dp"),
        ),
        check_vma=False,
    )
```

```python
import functools

import jax
import jax.numpy as jnp
from jax import lax
from jax.experimental import pallas as pl
from jax.experimental.pallas import tpu as pltpu
from jax.sharding import PartitionSpec as P

HEAD_SIZE = 64
TOPK = 8
SEQUENCE_LENGTH = 512


EPSILON = 1e-06
RESIDUAL = 0.22
ATTN_SCALE = 0.015625
ROPE_BASE = 10000.0
NEGATIVE = -1e30


def rotary_tables(length):
    half_dim = HEAD_SIZE // 2
    frequency = ROPE_BASE ** (-jnp.arange(half_dim, dtype=jnp.float32) * 2.0 / HEAD_SIZE)
    angles = jnp.arange(length, dtype=jnp.float32)[:, None] * frequency[None, :]
    return (jnp.cos(angles)[:, None, :], jnp.sin(angles)[:, None, :])


def rotate(value_rows, cosine, sine_table):
    half_dim = value_rows.shape[-1] // 2
    first = value_rows[..., :half_dim]
    second = value_rows[..., half_dim:]
    return jnp.concatenate(
        [first * cosine - second * sine_table, second * cosine + first * sine_table], axis=-1
    )


def norm_forward(value_rows):
    inv_rms = lax.rsqrt(jnp.mean(value_rows * value_rows, axis=-1, keepdims=True) + EPSILON)
    return (value_rows * inv_rms, inv_rms)


def block_scores(query_block, key_block, row_start):
    scores = (
        jnp.einsum("sqjgd,skjd->sjgqk", query_block, key_block, preferred_element_type=jnp.float32)
        * ATTN_SCALE
    )
    row_ids = row_start + jnp.arange(query_block.shape[1])[:, None]
    col_ids = jnp.arange(key_block.shape[1])[None, :]
    return jnp.where(row_ids >= col_ids, scores, NEGATIVE)


def contract(left, right, left_dim, right_dim):
    return lax.dot_general(
        left, right, (((left_dim,), (right_dim,)), ((), ())), preferred_element_type=jnp.float32
    )


def split_two(values):
    lane = lax.broadcasted_iota(jnp.int32, values.shape, 1)
    high = values.astype(jnp.bfloat16).astype(jnp.float32)
    low = values - high
    half_lanes = values.shape[1] // 2
    moved = jnp.concatenate([low[:, half_lanes:], low[:, :half_lanes]], axis=1)
    return jnp.where(lane < half_lanes, high, moved).astype(jnp.bfloat16)


def block_order(me, count, turn):
    left, right = me, count - 1 - me
    near = jnp.minimum(left, right)
    sign = jnp.where(left <= right, -1, 1)
    paired = turn <= 2 * near
    distance = jnp.where(paired, (turn + 1) // 2, turn - near)
    toward = jnp.where(paired & (turn % 2 == 1), sign, -sign)
    return me + toward * distance


def expert_kernel(
    owners,
    local,
    chunks,
    rows_hbm,
    cot_hbm,
    router_ref,
    gateup_hbm,
    down_hbm,
    parts_hbm,
    comb_hbm,
    gates_out,
    grads_hbm,
    act_hbm,
    hidden_hbm,
    rows_all,
    cot_all,
    gateup_ref,
    down_ref,
    gates_ref,
    send_grad,
    send_comb,
    recv_grad,
    recv_comb,
    load_sem,
    weight_sem,
    chain_send,
    chain_recv,
    swap_send,
    swap_recv,
    sums_send,
    grad_recv,
    comb_recv,
    back_send,
    back_recv,
    comb_sem,
    stage_sem,
):
    me = lax.axis_index("expert")
    core = lax.axis_index("tensor")
    sibling = {"tensor": 1 - core}
    total, feat_width = rows_all.shape[1], rows_all.shape[2]
    half = total // 2
    units = down_ref.shape[1]
    lanes = gates_ref.shape[1]
    mine = pl.ds(pl.multiple_of(core * half, half), half)
    others = pl.ds(pl.multiple_of((1 - core) * half, half), half)

    barrier = pltpu.get_barrier_semaphore()
    pl.semaphore_signal(barrier, inc=1, device_id=sibling, device_id_type=pl.DeviceIdType.MESH)
    for shift in range(1, owners):
        pl.semaphore_signal(
            barrier,
            inc=1,
            device_id={"expert": lax.rem(me + shift, owners)},
            device_id_type=pl.DeviceIdType.MESH,
        )

    def remote(src, dst, send, recv, device):
        return pltpu.make_async_remote_copy(
            src_ref=src,
            dst_ref=dst,
            send_sem=send,
            recv_sem=recv,
            device_id=device,
            device_id_type=pl.DeviceIdType.MESH,
        )

    own_rows = pltpu.make_async_copy(rows_hbm, rows_all.at[me, mine], load_sem.at[0])
    own_cot = pltpu.make_async_copy(cot_hbm, cot_all.at[me], load_sem.at[1])
    own_rows.start()
    own_cot.start()
    for expert in range(local):
        pltpu.make_async_copy(
            gateup_hbm.at[expert], gateup_ref.at[expert], weight_sem.at[0, expert]
        ).start()
        pltpu.make_async_copy(
            down_hbm.at[expert], down_ref.at[expert], weight_sem.at[1, expert]
        ).start()
    pl.semaphore_wait(barrier, owners)
    own_rows.wait()
    own_cot.wait()

    buffers = (rows_all, cot_all)

    def chain(step, what, side):
        block = me - side * (step - 1)
        to = me + side
        there = (block >= 0) & (block < owners) & (to >= 0) & (to < owners)
        safe = jnp.clip(block, 0, owners - 1)
        at = 0 if side == 1 else 1
        copy = remote(
            buffers[what].at[safe, mine],
            buffers[what].at[safe, mine],
            chain_send.at[what, step - 1, at],
            chain_recv.at[what, safe],
            {"expert": jnp.clip(to, 0, owners - 1)},
        )
        return there, copy

    def swap(what, block):
        return remote(
            buffers[what].at[block, mine],
            buffers[what].at[block, mine],
            swap_send.at[what, block],
            swap_recv.at[what, block],
            sibling,
        )

    def swap_arrival(what, block):
        return remote(
            buffers[what].at[block, others],
            buffers[what].at[block, others],
            swap_send.at[what, block],
            swap_recv.at[what, block],
            sibling,
        )

    def send_step(step):
        for what in range(2):
            for side in (1, -1):
                there, copy = chain(step, what, side)

                @pl.when(there)
                def _():
                    copy.start()

    def arrivals(step):
        for what in range(2):
            for side in (1, -1):
                block = me - side * step
                there = (block >= 0) & (block < owners)
                safe = jnp.clip(block, 0, owners - 1)

                @pl.when(there)
                def _():
                    chain_copy = remote(
                        buffers[what].at[safe, mine],
                        buffers[what].at[safe, mine],
                        chain_send.at[what, step - 1, 0],
                        chain_recv.at[what, safe],
                        sibling,
                    )
                    chain_copy.wait_recv()
                    swap(what, safe).start()

    swap(0, me).start()
    send_step(1)

    def expert_phase(comb_sum, grad_sum, dot_sum, hold_comb, hold_grad, hold_dot, act_stage, hidden_stage):
        lane = lax.broadcasted_iota(jnp.int32, (total, lanes), 1)

        def stage_copies(slot, expert, block):
            return (
                pltpu.make_async_copy(
                    act_stage.at[slot], act_hbm.at[expert, block], stage_sem.at[0, slot]
                ),
                pltpu.make_async_copy(
                    hidden_stage.at[slot], hidden_hbm.at[expert, block], stage_sem.at[1, slot]
                ),
            )

        def sums_copies(turn):
            return (
                remote(send_grad, recv_grad.at[turn], sums_send.at[0], grad_recv.at[turn], sibling),
                remote(send_comb, recv_comb.at[turn], sums_send.at[1], comb_recv.at[turn], sibling),
            )

        def back_copy(turn, block):
            return remote(
                recv_grad.at[turn],
                parts_hbm.at[me],
                back_send.at[turn],
                back_recv.at[me],
                {"expert": block},
            )

        def own_back():
            return pltpu.make_async_copy(recv_grad.at[0], parts_hbm.at[me], back_send.at[0])

        def comb_copy(turn, block):
            return pltpu.make_async_copy(
                recv_comb.at[turn],
                comb_hbm.at[lax.rem(block - me + owners, owners)],
                comb_sem.at[turn],
            )

        def settle(turn):
            block = block_order(me, owners, turn)
            copy_grad, copy_comb = sums_copies(turn)
            copy_grad.wait_recv()
            got = recv_grad[turn].astype(jnp.float32)
            recv_grad[turn, :, :feat_width] = (hold_grad[...] + got[:, :feat_width]).astype(
                jnp.bfloat16
            )
            dots = hold_dot[...] + got[:, feat_width:]
            lower = lanes // 2
            dots = dots + jnp.concatenate([dots[:, lower:], dots[:, :lower]], axis=1)
            low_lane = lax.broadcasted_iota(jnp.int32, (half, lanes), 1) < lower
            recv_grad[turn, :, feat_width:] = split_two(jnp.where(low_lane, dots, 0.0))

            @pl.when(turn > 0)
            def _():
                back_copy(turn, block).start()

            @pl.when(turn == 0)
            def _():
                own_back().start()

            copy_comb.wait_recv()
            recv_comb[turn] = (hold_comb[...] + recv_comb[turn].astype(jnp.float32)).astype(
                jnp.bfloat16
            )
            comb_copy(turn, block).start()

        def body(number, carry):
            turn = number // local
            expert = number % local
            block = block_order(me, owners, turn)
            slot = number % 2

            @pl.when(expert == 0)
            def _():
                swap_arrival_needed = turn > 0

                @pl.when(swap_arrival_needed)
                def _():
                    swap_arrival(1, block).wait_recv()

                swap_arrival(0, block).wait_recv()
                hits = cot_all[block, :, feat_width:].astype(jnp.float32) > 0.5
                logits = jnp.dot(
                    rows_all[block], router_ref[...], preferred_element_type=jnp.float32
                )
                logits = jnp.where(hits, logits, NEGATIVE)
                raised = jnp.where(
                    hits, jnp.exp(logits - jnp.max(logits, axis=1, keepdims=True)), 0.0
                )
                gates_ref[...] = raised / jnp.sum(raised, axis=1, keepdims=True)

                @pl.when(turn == 0)
                def _():
                    gates_out[...] = gates_ref[mine]

            @pl.when(number < local)
            def _():
                pltpu.make_async_copy(
                    gateup_hbm.at[expert], gateup_ref.at[expert], weight_sem.at[0, expert]
                ).wait()
                pltpu.make_async_copy(
                    down_hbm.at[expert], down_ref.at[expert], weight_sem.at[1, expert]
                ).wait()

            @pl.when(number >= 2)
            def _():
                for copy in stage_copies(slot, expert, block):
                    copy.wait()

            rows = rows_all[block]
            gate_weight, up_weight, down = (
                gateup_ref[expert, 0],
                gateup_ref[expert, 1],
                down_ref[expert],
            )
            gate_part = jnp.dot(rows, gate_weight, preferred_element_type=jnp.float32)
            up_part = jnp.dot(rows, up_weight, preferred_element_type=jnp.float32)
            raw = contract(cot_all[block, :, :feat_width], down, 1, 1)
            here = lane == me * local + expert
            weight = jnp.sum(jnp.where(here, gates_ref[...], 0.0), axis=1, keepdims=True)
            sigmoid_gate = jax.nn.sigmoid(gate_part)
            silu_gate = gate_part * sigmoid_gate
            activation = silu_gate * up_part
            dots = jnp.where(here, jnp.sum(activation * raw, axis=1, keepdims=True), 0.0)
            weighted = (activation * weight).astype(jnp.bfloat16)
            act_stage[slot] = weighted
            grad_act = raw * (RESIDUAL * weight)
            grad_gatepart = (
                grad_act * up_part * (sigmoid_gate * (1.0 + gate_part * (1.0 - sigmoid_gate)))
            ).astype(jnp.bfloat16)
            grad_uppart = (grad_act * silu_gate).astype(jnp.bfloat16)
            hidden_stage[slot, :, :units] = grad_gatepart
            hidden_stage[slot, :, units:] = grad_uppart
            for copy in stage_copies(slot, expert, block):
                copy.start()
            comb = jnp.dot(weighted, down, preferred_element_type=jnp.float32)
            grad = contract(grad_gatepart, gate_weight, 1, 1) + contract(
                grad_uppart, up_weight, 1, 1
            )

            @pl.when(expert == 0)
            def _():
                comb_sum[...] = comb
                grad_sum[...] = grad
                dot_sum[...] = dots

            @pl.when(expert > 0)
            def _():
                comb_sum[...] += comb
                grad_sum[...] += grad
                dot_sum[...] += dots

            @pl.when((expert == 1) & (turn > 0))
            def _():
                settle(turn - 1)

            for step in range(1, owners):

                @pl.when(number == step * local - 2)
                def _():
                    arrivals(step)
                    if step + 1 < owners:
                        send_step(step + 1)

            @pl.when(expert == local - 1)
            def _():
                @pl.when(turn > 0)
                def _():
                    for copy in sums_copies(turn):
                        copy.wait_send()

                send_grad[:, :feat_width] = grad_sum[others].astype(jnp.bfloat16)
                send_grad[:, feat_width:] = split_two(dot_sum[others])
                send_comb[...] = comb_sum[others].astype(jnp.bfloat16)
                for copy in sums_copies(turn):
                    copy.start()
                hold_grad[...] = grad_sum[mine]
                hold_comb[...] = comb_sum[mine]
                hold_dot[...] = dot_sum[mine]

            return carry

        lax.fori_loop(0, owners * local, body, 0)
        settle(owners - 1)
        for copy in sums_copies(owners - 1):
            copy.wait_send()
        for slot in range(2):
            for copy in stage_copies(slot, 0, 0):
                copy.wait()
        for turn in range(owners):
            block = block_order(me, owners, turn)
            comb_copy(turn, block).wait()

    pl.run_scoped(
        expert_phase,
        pltpu.VMEM((total, feat_width), jnp.float32),
        pltpu.VMEM((total, feat_width), jnp.float32),
        pltpu.VMEM((total, lanes), jnp.float32),
        pltpu.VMEM((half, feat_width), jnp.float32),
        pltpu.VMEM((half, feat_width), jnp.float32),
        pltpu.VMEM((half, lanes), jnp.float32),
        pltpu.VMEM((2, total, units), jnp.bfloat16),
        pltpu.VMEM((2, total, 2 * units), jnp.bfloat16),
    )

    width = feat_width // chunks

    def weights_body(act_ref, hidden_ref, grads_out):
        up_sum = sum(contract(rows_all[b], hidden_ref[0, b], 0, 0) for b in range(owners))
        up_sum = up_sum.astype(jnp.bfloat16)
        down_sum = sum(
            contract(act_ref[0, b], cot_all[b, :, :feat_width], 0, 0) for b in range(owners)
        )
        down_sum = (RESIDUAL * down_sum).T.astype(jnp.bfloat16)
        for chunk in range(chunks):
            for part in range(2):
                grads_out[chunk, 0, part, :width] = up_sum[
                    chunk * width : (chunk + 1) * width, part * units : (part + 1) * units
                ]
                start = chunk * width + part * (width // 2)
                grads_out[chunk, 0, part, width:] = down_sum[start : start + width // 2]

    pltpu.emit_pipeline(
        weights_body,
        grid=(local,),
        in_specs=[
            pl.BlockSpec((1, owners, total, units), lambda e: (e, 0, 0, 0)),
            pl.BlockSpec((1, owners, total, 2 * units), lambda e: (e, 0, 0, 0)),
        ],
        out_specs=[
            pl.BlockSpec((chunks, 1, 2, width + width // 2, units), lambda e: (0, e, 0, 0, 0)),
        ],
    )(act_hbm, hidden_hbm, grads_hbm)

    swap(0, me).wait_send()
    for step in range(1, owners):
        for what in range(2):
            for side in (1, -1):
                there, copy = chain(step, what, side)

                @pl.when(there)
                def _():
                    copy.wait_send()

                block = me - side * step
                arrived = (block >= 0) & (block < owners)
                safe = jnp.clip(block, 0, owners - 1)

                @pl.when(arrived)
                def _():
                    swap(what, safe).wait_send()

    pltpu.make_async_copy(recv_grad.at[0], parts_hbm.at[me], back_send.at[0]).wait()
    for turn in range(1, owners):
        block = block_order(me, owners, turn)
        remote(
            recv_grad.at[turn],
            parts_hbm.at[me],
            back_send.at[turn],
            back_recv.at[me],
            {"expert": block},
        ).wait_send()
        source = lax.rem(me + turn, owners)
        remote(
            recv_grad.at[turn],
            parts_hbm.at[source],
            back_send.at[turn],
            back_recv.at[source],
            {"expert": source},
        ).wait_recv()


def experts(rows, cot, router, gateup, down, owners, chunks):
    half, feat_width = rows.shape
    total = 2 * half
    local, units = down.shape[0], down.shape[1]
    lanes = router.shape[1]
    wide = feat_width + lanes
    any_space = pl.BlockSpec(memory_space=pl.ANY)
    in_vmem = pl.BlockSpec(memory_space=pltpu.VMEM)
    bf16 = jnp.bfloat16
    return pl.pallas_call(
        functools.partial(expert_kernel, owners, local, chunks),
        in_specs=[any_space, any_space, in_vmem, any_space, any_space],
        out_specs=[any_space, any_space, in_vmem, any_space, any_space, any_space],
        out_shape=[
            jax.ShapeDtypeStruct((owners, half, wide), bf16),
            jax.ShapeDtypeStruct((owners, half, feat_width), bf16),
            jax.ShapeDtypeStruct((half, lanes), jnp.float32),
            jax.ShapeDtypeStruct((chunks, local, 2, 3 * feat_width // chunks // 2, units), bf16),
            jax.ShapeDtypeStruct((local, owners, total, units), bf16),
            jax.ShapeDtypeStruct((local, owners, total, 2 * units), bf16),
        ],
        scratch_shapes=[
            pltpu.VMEM((owners, total, feat_width), bf16),
            pltpu.VMEM((owners, total, wide), bf16),
            pltpu.VMEM((local, 2, feat_width, units), bf16),
            pltpu.VMEM((local, units, feat_width), bf16),
            pltpu.VMEM((total, lanes), jnp.float32),
            pltpu.VMEM((half, wide), bf16),
            pltpu.VMEM((half, feat_width), bf16),
            pltpu.VMEM((owners, half, wide), bf16),
            pltpu.VMEM((owners, half, feat_width), bf16),
            pltpu.SemaphoreType.DMA((2,)),
            pltpu.SemaphoreType.DMA((2, local)),
            pltpu.SemaphoreType.DMA((2, owners - 1, 2)),
            pltpu.SemaphoreType.DMA((2, owners)),
            pltpu.SemaphoreType.DMA((2, owners)),
            pltpu.SemaphoreType.DMA((2, owners)),
            pltpu.SemaphoreType.DMA((2,)),
            pltpu.SemaphoreType.DMA((owners,)),
            pltpu.SemaphoreType.DMA((owners,)),
            pltpu.SemaphoreType.DMA((owners,)),
            pltpu.SemaphoreType.DMA((owners,)),
            pltpu.SemaphoreType.DMA((owners,)),
            pltpu.SemaphoreType.DMA((2, 2)),
        ],
        compiler_params=pltpu.CompilerParams(
            vmem_limit_bytes=60 * 2**20, collective_id=0, has_side_effects=True
        ),
        cost_estimate=pl.CostEstimate(
            flops=2 * owners * total * feat_width * units * 9 * local,
            bytes_accessed=80 * 2**20,
            transcendentals=owners * total * units * local,
        ),
    )(rows, cot, router, gateup, down)


def swap_cores(values):
    return lax.ppermute(values, "tensor", [(0, 1), (1, 0)])


def factors(count):
    low = 1 << ((count.bit_length() - 1) // 2)
    return count // low, low


class Place:
    def __init__(self, rows, columns, owners):
        self.sizes = {"y": rows, "x": columns, "z": owners}
        index = lax.axis_index("dp")
        self.at = {"y": index // columns, "x": index % columns, "z": lax.axis_index("expert")}

    def peer(self, axis, shift):
        return lax.rem(self.at[axis] + shift, self.sizes[axis])

    def device(self, axis, to):
        if axis == "z":
            return {"expert": to}
        if axis == "x":
            return {"dp": self.at["y"] * self.sizes["x"] + to}
        return {"dp": to * self.sizes["x"] + self.at["x"]}


def picked(ref, position, index):
    return ref.at[(slice(None),) * position + (index,)]


class Summing:
    def __init__(self, place, source, axes, order, landing, send, recv):
        self.place, self.order, self.landing = place, order, landing
        self.send, self.recv = send, recv
        self.sources, self.positions = [source], []
        left = list(axes)
        for step, axis in enumerate(order):
            self.positions.append(left.index(axis))
            left.pop(self.positions[-1])
            self.sources.append(landing[step].at[0])

    def copies(self, step):
        axis = self.order[step]
        found = []
        for shift in range(1, self.place.sizes[axis]):
            to = self.place.peer(axis, shift)
            found.append(
                pltpu.make_async_remote_copy(
                    src_ref=picked(self.sources[step], self.positions[step], to),
                    dst_ref=self.landing[step].at[shift - 1],
                    send_sem=self.send.at[step, shift - 1],
                    recv_sem=self.recv.at[step, shift - 1],
                    device_id=self.place.device(axis, to),
                    device_id_type=pl.DeviceIdType.MESH,
                )
            )
        return found

    def start(self, step):
        for copy in self.copies(step):
            copy.start()

    def total(self, step):
        axis = self.order[step]
        for copy in self.copies(step):
            copy.wait_recv()
        own = picked(self.sources[step], self.positions[step], self.place.at[axis])
        value = own[...].astype(jnp.float32)
        for shift in range(1, self.place.sizes[axis]):
            value = value + self.landing[step][shift - 1].astype(jnp.float32)
        return value

    def forward(self, step):
        self.landing[step][0] = self.total(step).astype(self.landing[step].dtype)
        self.start(step + 1)

    def close(self):
        for step in range(len(self.order)):
            for copy in self.copies(step):
                copy.wait_send()


def norm_parts(values):
    inv_rms = lax.rsqrt(jnp.mean(values * values, axis=-1, keepdims=True) + EPSILON)
    return values * inv_rms, inv_rms


def norm_grad(grad, gain, unit, inv_rms):
    grad_unit = grad * gain
    return inv_rms * (grad_unit - unit * jnp.mean(grad_unit * unit, axis=-1, keepdims=True))


def back_kernel(
    rows,
    columns,
    owners,
    parts_hbm,
    comb_hbm,
    grads_hbm,
    gates_ref,
    middle_hbm,
    cot_ref,
    tokens_ref,
    expert_gain_ref,
    attn_gain_ref,
    router_ref,
    out_weight_ref,
    heads_ref,
    query_ref,
    key_ref,
    value_ref,
    normed_ref,
    query_weight_hbm,
    keyvalue_weight_hbm,
    cosine_ref,
    sine_ref,
    mixed_hbm,
    tokens_grad_hbm,
    gateup_out,
    down_out,
    first_out,
    output_out,
    small_out,
    own_a,
    own_b,
    first_a,
    first_b,
    second_a,
    second_b,
    comb_land,
    out_stage,
    out_z,
    out_x,
    out_y,
    qkv_a,
    qkv_ax,
    qkv_ay,
    qkv_az,
    qkv_b,
    qkv_by,
    qkv_bx,
    qkv_bz,
    small_sum,
    small_swap,
    small_stage,
    small_z,
    small_x,
    small_y,
    grad_attn,
    grad_middle,
    grad_query,
    grad_keyvalue,
    half_send,
    half_land,
    mixed_stage,
    load_sem,
    own_sem,
    first_send,
    first_recv,
    second_send,
    second_recv,
    comb_send,
    comb_recv,
    sum_send,
    sum_recv,
    swap_send,
    swap_recv,
    store_sem,
):
    place = Place(rows, columns, owners)
    core = lax.axis_index("tensor")
    sibling = {"tensor": 1 - core}
    half, feat_width = middle_hbm.shape
    local = grads_hbm.shape[2]
    width = gateup_out.shape[2]
    lanes = gates_ref.shape[1]
    heads, length, head_size = query_ref.shape
    kv_heads = key_ref.shape[0]
    groups = heads // kv_heads
    query_width = heads * head_size
    key_width = kv_heads * head_size
    tile = 64
    mine = pl.ds(pl.multiple_of(core * half, half), half)
    others = pl.ds(pl.multiple_of((1 - core) * half, half), half)

    barrier = pltpu.get_barrier_semaphore()
    peers = [sibling]
    for axis in ("x", "y", "z"):
        for shift in range(1, place.sizes[axis]):
            peers.append(place.device(axis, place.peer(axis, shift)))
    for peer in peers:
        pl.semaphore_signal(barrier, inc=1, device_id=peer, device_id_type=pl.DeviceIdType.MESH)
    pl.semaphore_wait(barrier, len(peers))

    def to_sibling(src, dst, at):
        return pltpu.make_async_remote_copy(
            src_ref=src,
            dst_ref=dst,
            send_sem=swap_send.at[at],
            recv_sem=swap_recv.at[at],
            device_id=sibling,
            device_id_type=pl.DeviceIdType.MESH,
        )

    plans = (
        (0, "x", "y", own_a, first_a, second_a),
        (1, "y", "x", own_b, first_b, second_b),
    )

    def grads_of(part, axis, index, expert):
        if axis == "x":
            return grads_hbm.at[:, index, expert, part]
        return grads_hbm.at[index, :, expert, part]

    def own_load(plan, expert):
        part, axis, _, own, _, _ = plan
        return pltpu.make_async_copy(
            grads_of(part, axis, place.at[axis], expert),
            own.at[expert % 2],
            own_sem.at[part, expert],
        )

    def first_copies(plan, expert):
        part, axis, _, _, first, _ = plan
        found = []
        for shift in range(1, place.sizes[axis]):
            to = place.peer(axis, shift)
            found.append(
                pltpu.make_async_remote_copy(
                    src_ref=grads_of(part, axis, to, expert),
                    dst_ref=first.at[shift - 1, expert],
                    send_sem=first_send.at[part, shift - 1, expert],
                    recv_sem=first_recv.at[part, shift - 1, expert],
                    device_id=place.device(axis, to),
                    device_id_type=pl.DeviceIdType.MESH,
                )
            )
        return found

    def second_copies(plan, expert):
        part, _, axis, _, first, second = plan
        found = []
        for shift in range(1, place.sizes[axis]):
            to = place.peer(axis, shift)
            found.append(
                pltpu.make_async_remote_copy(
                    src_ref=first.at[0, expert, to],
                    dst_ref=second.at[shift - 1, expert],
                    send_sem=second_send.at[part, shift - 1, expert],
                    recv_sem=second_recv.at[part, shift - 1, expert],
                    device_id=place.device(axis, to),
                    device_id_type=pl.DeviceIdType.MESH,
                )
            )
        return found

    def first_sum(expert):
        for plan in plans:
            _, axis, after, own, first, _ = plan
            own_load(plan, expert).wait()
            for copy in first_copies(plan, expert):
                copy.wait_recv()
            for index in range(place.sizes[after]):
                value = own[expert % 2, index].astype(jnp.float32)
                for shift in range(1, place.sizes[axis]):
                    value = value + first[shift - 1, expert, index].astype(jnp.float32)
                first[0, expert, index] = value.astype(first.dtype)
            for copy in second_copies(plan, expert):
                copy.start()

            @pl.when(expert + 2 < local)
            def _():
                own_load(plan, expert + 2).start()

    def second_sum(expert):
        for plan in plans:
            part, _, axis, _, first, second = plan
            for copy in second_copies(plan, expert):
                copy.wait_recv()
            value = first[0, expert, place.at[axis]].astype(jnp.float32)
            for shift in range(1, place.sizes[axis]):
                value = value + second[shift - 1, expert].astype(jnp.float32)
            gateup_out[expert, part] = value[:width]
            down_out[expert, part] = value[width:]

    def start_first(expert, carry):
        for plan in plans:
            for copy in first_copies(plan, expert):
                copy.start()
        return carry

    for plan in plans:
        for expert in range(min(2, local)):
            own_load(plan, expert).start()

    lax.fori_loop(0, local, start_first, 0)

    def comb_copy(shift):
        to = place.peer("z", shift)
        return pltpu.make_async_remote_copy(
            src_ref=comb_hbm.at[shift],
            dst_ref=comb_land.at[shift],
            send_sem=comb_send.at[shift - 1],
            recv_sem=comb_recv.at[shift - 1],
            device_id=place.device("z", to),
            device_id_type=pl.DeviceIdType.MESH,
        )

    own_comb = pltpu.make_async_copy(comb_hbm.at[0], comb_land.at[0], load_sem.at[0])
    own_comb.start()
    for shift in range(1, owners):
        comb_copy(shift).start()

    def job(source, order, landing, at):
        return Summing(
            place, source, ("y", "x", "z"), order, landing, sum_send.at[at], sum_recv.at[at]
        )

    output_job = job(out_stage, ("z", "x", "y"), (out_z, out_x, out_y), 0)
    first_job_a = job(qkv_a, ("x", "y", "z"), (qkv_ax, qkv_ay, qkv_az), 1)
    first_job_b = job(qkv_b, ("y", "x", "z"), (qkv_by, qkv_bx, qkv_bz), 2)
    small_job = job(small_stage, ("z", "x", "y"), (small_z, small_x, small_y), 3)

    def weight_grad(stage, left, right):
        count = stage.shape[3]
        band = feat_width // 4
        for start in range(0, feat_width, band):
            value = contract(left[:, start : start + band], right, 0, 0).astype(jnp.bfloat16)
            for at in range(start, start + band, count):
                index = at // count
                y, x, z = (
                    index // (columns * owners),
                    index // owners % columns,
                    index % owners,
                )
                stage[y, x, z] = value[at - start : at - start + count]

    def middle_phase(parts, middle):
        loads = (
            pltpu.make_async_copy(parts_hbm, parts, load_sem.at[1]),
            pltpu.make_async_copy(middle_hbm, middle, load_sem.at[2]),
        )
        for copy in loads:
            copy.start()
        for copy in loads:
            copy.wait()
        small_sum[...] = jnp.zeros_like(small_sum)

        def body(step, carry):
            at = pl.ds(pl.multiple_of(step * tile, tile), tile)
            grad = sum(parts[b, at, :feat_width].astype(jnp.float32) for b in range(owners))
            dots = sum(parts[b, at, feat_width:].astype(jnp.float32) for b in range(owners))
            lower = lanes // 2
            dots = dots + jnp.concatenate([dots[:, lower:], dots[:, :lower]], axis=1)
            gates = gates_ref[at]
            grad_gate = RESIDUAL * dots
            grad_logits = (
                gates * (grad_gate - jnp.sum(gates * grad_gate, axis=-1, keepdims=True))
            ).astype(jnp.bfloat16)
            grad = grad + contract(grad_logits, router_ref[...], 1, 1)
            unit, inv_rms = norm_parts(middle[at])
            expert_in = (unit * expert_gain_ref[...]).astype(jnp.bfloat16)
            after = cot_ref[at].astype(jnp.float32) + norm_grad(
                grad, expert_gain_ref[...], unit, inv_rms
            )
            grad_middle[at] = after
            to = pl.ds(pl.multiple_of(core * half + step * tile, tile), tile)
            grad_attn[to] = (RESIDUAL * after).astype(jnp.bfloat16)
            count = small_sum.shape[0]
            small_sum[...] += contract(grad_logits, expert_in, 0, 0)[:count]
            small_sum[count - 2 : count - 1] += jnp.sum(grad * unit, axis=0, keepdims=True)
            return carry

        lax.fori_loop(0, half // tile, body, 0)

    pl.run_scoped(
        middle_phase,
        pltpu.VMEM(parts_hbm.shape, parts_hbm.dtype),
        pltpu.VMEM(middle_hbm.shape, middle_hbm.dtype),
    )
    attn_swap = to_sibling(grad_attn.at[mine], grad_attn.at[mine], 0)
    attn_swap.start()
    to_sibling(grad_attn.at[others], grad_attn.at[others], 0).wait_recv()

    weight_grad(out_stage, grad_attn, heads_ref[...])
    output_job.start(0)
    causal = length // 2

    def attention_phase(key_sum, value_sum):
        def turned_back(grads):
            swapped = jnp.concatenate(
                [grads[:, head_size // 2 :], grads[:, : head_size // 2]], axis=1
            )
            return (grads * cosine_ref[...] + swapped * sine_ref[...]).astype(jnp.bfloat16)

        def body(group, carry):
            grad_heads = contract(grad_attn[...], out_weight_ref[group], 1, 1).astype(jnp.bfloat16)
            keys, values = key_ref[group], value_ref[group]
            key_sum[...] = jnp.zeros_like(key_sum)
            value_sum[...] = jnp.zeros_like(value_sum)
            turned = []
            for member in range(groups):
                query = query_ref[group * groups + member]
                grad_head = grad_heads[:, member * head_size : (member + 1) * head_size]
                pieces = []
                for start in (0, causal):
                    stop = start + causal
                    some_q, some_g = query[start:stop], grad_head[start:stop]
                    some_k, some_v = keys[:stop], values[:stop]
                    scores = contract(some_q, some_k, 1, 1) * ATTN_SCALE
                    row = start + lax.broadcasted_iota(jnp.int32, scores.shape, 0)
                    col = lax.broadcasted_iota(jnp.int32, scores.shape, 1)
                    scores = jnp.where(row >= col, scores, NEGATIVE)
                    raised = jnp.exp(scores - jnp.max(scores, axis=1, keepdims=True))
                    probs = raised / jnp.sum(raised, axis=1, keepdims=True)
                    grad_probs = contract(some_g, some_v, 1, 1)
                    value_sum[:stop] += contract(probs.astype(jnp.bfloat16), some_g, 0, 0)
                    grad_scores = (
                        probs
                        * (grad_probs - jnp.sum(probs * grad_probs, axis=1, keepdims=True))
                    ).astype(jnp.bfloat16)
                    pieces.append(
                        jnp.dot(grad_scores, some_k, preferred_element_type=jnp.float32)
                    )
                    key_sum[:stop] += contract(grad_scores, some_q, 0, 0)
                turned.append(turned_back(ATTN_SCALE * jnp.concatenate(pieces, axis=0)))
            grad_query[group] = jnp.concatenate(turned, axis=1)
            grad_keyvalue[0, group] = turned_back(ATTN_SCALE * key_sum[...])
            grad_keyvalue[1, group] = value_sum[...].astype(jnp.bfloat16)

            @pl.when(group < local)
            def _():
                first_sum(group)

            return carry

        lax.fori_loop(0, kv_heads, body, 0)

    pl.run_scoped(
        attention_phase,
        pltpu.VMEM((length, head_size), jnp.float32),
        pltpu.VMEM((length, head_size), jnp.float32),
    )
    for expert in range(kv_heads, local):
        first_sum(expert)

    def tokens_phase(query_weight, keyvalue_weight, grad_normed):
        loads = (
            pltpu.make_async_copy(query_weight_hbm, query_weight, load_sem.at[1]),
            pltpu.make_async_copy(keyvalue_weight_hbm, keyvalue_weight, load_sem.at[2]),
        )
        for copy in loads:
            copy.start()
        queries = jnp.concatenate([grad_query[g] for g in range(kv_heads)], axis=1)
        keyvalue = [
            jnp.concatenate([grad_keyvalue[what, g] for g in range(kv_heads)], axis=1)
            for what in range(2)
        ]
        cut = (query_width + 2 * key_width) // 2
        left = queries[:, :cut]
        right = jnp.concatenate([queries[:, cut:]] + keyvalue, axis=1)
        weight_grad(qkv_a, normed_ref, left)
        first_job_a.start(0)
        weight_grad(qkv_b, normed_ref, right)
        first_job_b.start(0)
        for copy in loads:
            copy.wait()
        grad_normed[...] = (
            contract(queries, query_weight[...], 1, 1)
            + contract(keyvalue[0], keyvalue_weight[0], 1, 1)
            + contract(keyvalue[1], keyvalue_weight[1], 1, 1)
        )
        half_send[...] = grad_normed[others].astype(jnp.bfloat16)
        swap = to_sibling(half_send, half_land, 1)
        swap.start()
        swap.wait_recv()

        def body(step, carry):
            at = pl.ds(pl.multiple_of(step * tile, tile), tile)
            to = pl.ds(pl.multiple_of(core * half + step * tile, tile), tile)
            grad = grad_normed[to] + half_land[at].astype(jnp.float32)
            unit, inv_rms = norm_parts(tokens_ref[at].astype(jnp.float32))
            grad_middle[at] += norm_grad(grad, attn_gain_ref[...], unit, inv_rms)
            count = small_sum.shape[0]
            small_sum[count - 1 : count] += jnp.sum(grad * unit, axis=0, keepdims=True)
            return carry

        lax.fori_loop(0, half // tile, body, 0)

    pl.run_scoped(
        tokens_phase,
        pltpu.VMEM(query_weight_hbm.shape, query_weight_hbm.dtype),
        pltpu.VMEM(keyvalue_weight_hbm.shape, keyvalue_weight_hbm.dtype),
        pltpu.VMEM((2 * half, feat_width), jnp.float32),
    )
    tokens_store = pltpu.make_async_copy(grad_middle, tokens_grad_hbm.at[mine], store_sem.at[0])
    tokens_store.start()
    tokens_swap = to_sibling(grad_middle, tokens_grad_hbm.at[mine], 2)
    tokens_swap.start()
    small_exchange = to_sibling(small_sum, small_swap, 3)
    small_exchange.start()

    output_job.forward(0)

    small_exchange.wait()
    small_sum[...] += small_swap[...]
    piece = feat_width // (rows * columns * owners)
    small_stage[...] = jnp.zeros_like(small_stage)
    for y in range(rows):
        for x in range(columns):
            for z in range(owners):
                at = ((y * columns + x) * owners + z) * piece
                small_stage[y, x, z, :, :piece] = small_sum[:, at : at + piece]
    small_job.start(0)

    own_comb.wait()
    for shift in range(1, owners):
        comb_copy(shift).wait_recv()

    def mixed_phase(middle):
        load = pltpu.make_async_copy(middle_hbm, middle, load_sem.at[1])
        load.start()
        load.wait()

        def body(step, carry):
            at = pl.ds(pl.multiple_of(step * tile, tile), tile)
            comb = sum(comb_land[b, at].astype(jnp.float32) for b in range(owners))
            mixed_stage[at] = (middle[at] + RESIDUAL * comb).astype(jnp.bfloat16)
            return carry

        lax.fori_loop(0, half // tile, body, 0)

    pl.run_scoped(mixed_phase, pltpu.VMEM(middle_hbm.shape, middle_hbm.dtype))
    mixed_store = pltpu.make_async_copy(mixed_stage, mixed_hbm.at[mine], store_sem.at[1])
    mixed_store.start()
    mixed_swap = to_sibling(mixed_stage, mixed_hbm.at[mine], 4)
    mixed_swap.start()

    small_job.forward(0)
    output_job.forward(1)
    small_job.forward(1)

    def finish(expert, carry):
        second_sum(expert)
        return carry

    lax.fori_loop(0, local, finish, 0)
    first_job_a.forward(0)
    first_job_b.forward(0)
    output_out[...] = output_job.total(2)
    small_out[...] = small_job.total(2)
    first_job_a.forward(1)
    first_job_b.forward(1)
    cut = qkv_a.shape[4]
    first_out[:, :cut] = first_job_a.total(2)
    first_out[:, cut:] = first_job_b.total(2)

    def close(expert, carry):
        for plan in plans:
            for copy in first_copies(plan, expert) + second_copies(plan, expert):
                copy.wait_send()
        return carry

    lax.fori_loop(0, local, close, 0)
    for shift in range(1, owners):
        comb_copy(shift).wait_send()
    for which in (output_job, first_job_a, first_job_b, small_job):
        which.close()
    attn_swap.wait_send()
    to_sibling(half_send, half_land, 1).wait_send()
    tokens_store.wait()
    mixed_store.wait()
    tokens_swap.wait_send()
    mixed_swap.wait_send()
    to_sibling(grad_middle, tokens_grad_hbm.at[others], 2).wait_recv()
    to_sibling(mixed_stage, mixed_hbm.at[others], 4).wait_recv()


def backward(
    parts,
    combs,
    grads,
    gates,
    middle,
    cot,
    tokens,
    expert_gain,
    attn_gain,
    router,
    out_weight,
    heads_out,
    query,
    keys,
    values,
    normed,
    query_weight,
    keyvalue_weight,
    cosine,
    sine,
):
    owners = lax.axis_size("expert")
    chunks = lax.axis_size("dp")
    rows, columns = factors(chunks)
    half, feat_width = middle.shape
    local, _, height, units = grads.shape[1:]
    width = feat_width // chunks
    grads = grads.reshape((rows, columns) + grads.shape[1:])
    piece = feat_width // (chunks * owners)
    heads, length, head_size = query.shape
    kv_heads = keys.shape[0]
    query_width, key_width = heads * head_size, kv_heads * head_size
    cut = (query_width + 2 * key_width) // 2
    lanes = gates.shape[1]
    count = 24
    out_weight = out_weight.reshape(kv_heads, query_width // kv_heads, feat_width)
    bf16, f32 = jnp.bfloat16, jnp.float32
    hbm = pl.BlockSpec(memory_space=pl.ANY)
    vmem = pl.BlockSpec(memory_space=pltpu.VMEM)
    dma = pltpu.SemaphoreType.DMA
    most = max(rows, columns, owners) - 1

    def landings(tail, order, dtype):
        sizes = {"y": rows, "x": columns, "z": owners}
        left = ["y", "x", "z"]
        found = []
        for axis in order:
            left.remove(axis)
            found.append(
                pltpu.VMEM((sizes[axis] - 1,) + tuple(sizes[a] for a in left) + tail, dtype)
            )
        return found

    whole = (rows, columns, owners)
    return pl.pallas_call(
        functools.partial(back_kernel, rows, columns, owners),
        in_specs=[hbm, hbm, hbm, vmem, hbm] + [vmem] * 11 + [hbm, hbm, vmem, vmem],
        out_specs=[hbm, hbm, vmem, vmem, vmem, vmem, vmem],
        out_shape=[
            jax.ShapeDtypeStruct((2 * half, feat_width), bf16),
            jax.ShapeDtypeStruct((2 * half, feat_width), f32),
            jax.ShapeDtypeStruct((local, 2, width, units), f32),
            jax.ShapeDtypeStruct((local, 2, width // 2, units), f32),
            jax.ShapeDtypeStruct((piece, 2 * cut), f32),
            jax.ShapeDtypeStruct((piece, query_width), f32),
            jax.ShapeDtypeStruct((count, lanes), f32),
        ],
        scratch_shapes=[
            pltpu.VMEM((2, rows, height, units), bf16),
            pltpu.VMEM((2, columns, height, units), bf16),
            pltpu.VMEM((columns - 1, local, rows, height, units), bf16),
            pltpu.VMEM((rows - 1, local, columns, height, units), bf16),
            pltpu.VMEM((rows - 1, local, height, units), bf16),
            pltpu.VMEM((columns - 1, local, height, units), bf16),
            pltpu.VMEM((owners, half, feat_width), bf16),
            pltpu.VMEM(whole + (piece, query_width), bf16),
            *landings((piece, query_width), "zxy", bf16),
            pltpu.VMEM(whole + (piece, cut), bf16),
            *landings((piece, cut), "xyz", bf16),
            pltpu.VMEM(whole + (piece, cut), bf16),
            *landings((piece, cut), "yxz", bf16),
            pltpu.VMEM((count, feat_width), f32),
            pltpu.VMEM((count, feat_width), f32),
            pltpu.VMEM(whole + (count, lanes), f32),
            *landings((count, lanes), "zxy", f32),
            pltpu.VMEM((2 * half, feat_width), bf16),
            pltpu.VMEM((half, feat_width), f32),
            pltpu.VMEM((kv_heads, length, query_width // kv_heads), bf16),
            pltpu.VMEM((2, kv_heads, length, head_size), bf16),
            pltpu.VMEM((half, feat_width), bf16),
            pltpu.VMEM((half, feat_width), bf16),
            pltpu.VMEM((half, feat_width), bf16),
            dma((3,)),
            dma((2, local)),
            dma((2, most, local)),
            dma((2, most, local)),
            dma((2, most, local)),
            dma((2, most, local)),
            dma((owners - 1,)),
            dma((owners - 1,)),
            dma((4, 3, most)),
            dma((4, 3, most)),
            dma((5,)),
            dma((5,)),
            dma((2,)),
        ],
        compiler_params=pltpu.CompilerParams(
            vmem_limit_bytes=60 * 2**20, collective_id=1, has_side_effects=True
        ),
        cost_estimate=pl.CostEstimate(
            flops=12 * 2**30, bytes_accessed=60 * 2**20, transcendentals=heads * length * length
        ),
    )(
        parts,
        combs,
        grads,
        gates,
        middle,
        cot,
        tokens,
        expert_gain,
        attn_gain,
        router,
        out_weight,
        heads_out,
        query,
        keys,
        values,
        normed,
        query_weight,
        keyvalue_weight,
        cosine,
        sine,
    )


def per_device(
    tokens,
    out_grad,
    attn_gain,
    query_weight,
    key_value_weight,
    output_weight,
    expert_gain,
    router_weight,
    gateup_weight,
    down_weight,
    routes,
):
    tok_count, feat_width = tokens.shape
    expert_count = router_weight.shape[1]
    owners = lax.axis_size("expert")
    chunks = lax.axis_size("dp")
    core = lax.axis_index("tensor")
    local_experts = gateup_weight.shape[0]
    kv_heads = key_value_weight.shape[2] // HEAD_SIZE
    query_heads = query_weight.shape[1] // HEAD_SIZE
    groups = query_heads // kv_heads
    sequence_count = tok_count // SEQUENCE_LENGTH
    half = tok_count // 2
    lanes = 128

    def halves(values):
        return (
            lax.dynamic_slice_in_dim(values, core * half, half, 0),
            lax.dynamic_slice_in_dim(values, (1 - core) * half, half, 0),
        )

    cot_mine, _ = halves(out_grad)
    hit_table = jnp.any(
        routes[:, :, None] == jnp.arange(lanes, dtype=jnp.int32)[None, None, :], axis=1
    ).astype(jnp.bfloat16)
    cot_wide = jnp.concatenate([out_grad, hit_table], axis=1)
    router_wide = jnp.pad(router_weight, ((0, 0), (0, lanes - expert_count)))

    cosine, sine_table = rotary_tables(SEQUENCE_LENGTH)
    inputs = tokens.astype(jnp.float32)
    unit_first, rms_first = norm_forward(inputs)
    normed = (unit_first * attn_gain).astype(jnp.bfloat16)
    queries = jnp.dot(normed, query_weight, preferred_element_type=jnp.float32)
    key_value = jnp.einsum(
        "td,cde->cte", normed, key_value_weight, preferred_element_type=jnp.float32
    )
    query_rot = (
        rotate(
            queries.reshape(sequence_count, SEQUENCE_LENGTH, query_heads, HEAD_SIZE),
            cosine,
            sine_table,
        )
        .astype(jnp.bfloat16)
        .reshape(sequence_count, SEQUENCE_LENGTH, kv_heads, groups, HEAD_SIZE)
    )
    keys_rot = rotate(
        key_value[0].reshape(sequence_count, SEQUENCE_LENGTH, kv_heads, HEAD_SIZE),
        cosine,
        sine_table,
    ).astype(jnp.bfloat16)
    value_rows = (
        key_value[1]
        .astype(jnp.bfloat16)
        .reshape(sequence_count, SEQUENCE_LENGTH, kv_heads, HEAD_SIZE)
    )
    scores = block_scores(query_rot, keys_rot, 0)
    row_max = jnp.max(scores, axis=-1, keepdims=True)
    exp_scores = jnp.exp(scores - row_max)
    row_sum = jnp.sum(exp_scores, axis=-1, keepdims=True)
    prob_block = (exp_scores / row_sum).astype(jnp.bfloat16)
    outputs = jnp.einsum(
        "sjgqk,skjd->sqjgd", prob_block, value_rows, preferred_element_type=jnp.float32
    )
    heads_out = outputs.astype(jnp.bfloat16).reshape(tok_count, query_heads * HEAD_SIZE)
    partial_value = jnp.dot(heads_out, output_weight, preferred_element_type=jnp.float32)

    part_mine, part_other = halves(partial_value)
    inputs_mine = halves(inputs)[0]
    middle = inputs_mine + RESIDUAL * (part_mine + swap_cores(part_other))
    unit_second, rms_second = norm_forward(middle)
    expert_in = (unit_second * expert_gain).astype(jnp.bfloat16)

    parts, combs, gates, grads, _, _ = experts(
        expert_in, cot_wide, router_wide, gateup_weight, down_weight, owners, chunks
    )

    cosine_whole = jnp.concatenate([cosine[:, 0], cosine[:, 0]], axis=1)
    sine_whole = jnp.concatenate([sine_table[:, 0], -sine_table[:, 0]], axis=1)
    mixed, tokens_grad, gateup_total, down_total, first_total, output_total, small = backward(
        parts,
        combs,
        grads,
        gates,
        middle,
        cot_mine,
        halves(tokens)[0],
        expert_gain[None],
        attn_gain[None],
        router_wide,
        output_weight,
        heads_out,
        query_rot.reshape(tok_count, query_heads, HEAD_SIZE).transpose(1, 0, 2),
        keys_rot.reshape(tok_count, kv_heads, HEAD_SIZE).transpose(1, 0, 2),
        value_rows.reshape(tok_count, kv_heads, HEAD_SIZE).transpose(1, 0, 2),
        normed,
        query_weight,
        key_value_weight,
        cosine_whole,
        sine_whole,
    )
    query_width = query_weight.shape[1]
    key_width = key_value_weight.shape[2]
    piece = feat_width // (chunks * owners)
    down_total = down_total.reshape(local_experts, -1, down_weight.shape[1]).transpose(0, 2, 1)
    return (
        mixed,
        tokens_grad,
        small[23, :piece],
        first_total[:, :query_width],
        jnp.stack(
            [
                first_total[:, query_width : query_width + key_width],
                first_total[:, query_width + key_width :],
            ],
            axis=0,
        ),
        output_total.T,
        small[22, :piece],
        small[:expert_count, :piece].T,
        gateup_total,
        down_total,
    )


def solution(mesh):
    placed = (
        P(("dp", "expert"), None),
        P(("dp", "expert"), None),
        P(),
        P(None, "tensor"),
        P(None, None, "tensor"),
        P("tensor", None),
        P(),
        P(),
        P("expert", None, None, "tensor"),
        P("expert", "tensor", None),
        P(("dp", "expert"), None),
    )
    return jax.shard_map(
        per_device,
        mesh=mesh,
        in_specs=placed,
        out_specs=(
            P(("dp", "expert"), None),
            P(("dp", "expert"), None),
            P(("dp", "expert")),
            P(("dp", "expert"), "tensor"),
            P(None, ("dp", "expert"), "tensor"),
            P("tensor", ("dp", "expert")),
            P(("dp", "expert")),
            P(("dp", "expert"), None),
            P("expert", None, "dp", "tensor"),
            P("expert", "tensor", "dp"),
        ),
        check_vma=False,
    )
```

```python
import functools

import jax
import jax.numpy as jnp
import numpy as np
from jax import lax
from jax.experimental import pallas as pl
from jax.experimental.pallas import tpu as pltpu
from jax.sharding import PartitionSpec as P

HEAD_SIZE = 64
TOPK = 8
SEQUENCE_LENGTH = 512


EPSILON = 1e-06
RESIDUAL = 0.22
ATTN_SCALE = 0.015625
ROPE_BASE = 10000.0
NEGATIVE = -1e30


def rotary_tables():
    half_dim = HEAD_SIZE // 2
    frequency = ROPE_BASE ** (-np.arange(half_dim, dtype=np.float32) * 2.0 / HEAD_SIZE)
    angles = np.arange(SEQUENCE_LENGTH, dtype=np.float32)[:, None] * frequency[None, :]
    angles = angles.astype(np.float32)
    cosine, sine = np.cos(angles), np.sin(angles)
    return (
        jnp.asarray(np.concatenate([cosine, cosine], axis=1), jnp.float32),
        jnp.asarray(np.concatenate([sine, -sine], axis=1), jnp.float32),
    )


def norm_parts(values):
    inv_rms = lax.rsqrt(jnp.mean(values * values, axis=-1, keepdims=True) + EPSILON)
    return values * inv_rms, inv_rms


def contract(left, right, left_dim, right_dim):
    return lax.dot_general(
        left, right, (((left_dim,), (right_dim,)), ((), ())), preferred_element_type=jnp.float32
    )


def split_two(values):
    lane = lax.broadcasted_iota(jnp.int32, values.shape, 1)
    high = values.astype(jnp.bfloat16).astype(jnp.float32)
    low = values - high
    half_lanes = values.shape[1] // 2
    moved = jnp.concatenate([low[:, half_lanes:], low[:, :half_lanes]], axis=1)
    return jnp.where(lane < half_lanes, high, moved).astype(jnp.bfloat16)


def block_order(me, count, turn):
    left, right = me, count - 1 - me
    near = jnp.minimum(left, right)
    sign = jnp.where(left <= right, -1, 1)
    paired = turn <= 2 * near
    distance = jnp.where(paired, (turn + 1) // 2, turn - near)
    toward = jnp.where(paired & (turn % 2 == 1), sign, -sign)
    return me + toward * distance


def expert_kernel(
    owners,
    local,
    chunks,
    tokens_hbm,
    cot_hbm,
    routes_ref,
    attn_gain_ref,
    expert_gain_ref,
    cosine_ref,
    sine_ref,
    router_ref,
    query_weight_hbm,
    keyvalue_weight_hbm,
    out_weight_hbm,
    gateup_hbm,
    down_hbm,
    parts_hbm,
    comb_hbm,
    gates_out,
    grads_hbm,
    act_hbm,
    hidden_hbm,
    normed_hbm,
    query_hbm,
    key_hbm,
    value_hbm,
    heads_hbm,
    middle_hbm,
    rows_all,
    cot_all,
    gateup_ref,
    down_ref,
    router_wide,
    half_send,
    half_land,
    gates_ref,
    send_grad,
    send_comb,
    recv_grad,
    recv_comb,
    load_sem,
    keep_sem,
    half_sem,
    weight_sem,
    chain_send,
    chain_recv,
    swap_send,
    swap_recv,
    sums_send,
    grad_recv,
    comb_recv,
    back_send,
    back_recv,
    comb_sem,
    stage_sem,
):
    me = lax.axis_index("expert")
    core = lax.axis_index("tensor")
    sibling = {"tensor": 1 - core}
    total, feat_width = rows_all.shape[1], rows_all.shape[2]
    half = total // 2
    units = down_ref.shape[1]
    lanes = gates_ref.shape[1]
    mine = pl.ds(pl.multiple_of(core * half, half), half)
    others = pl.ds(pl.multiple_of((1 - core) * half, half), half)

    barrier = pltpu.get_barrier_semaphore()
    pl.semaphore_signal(barrier, inc=1, device_id=sibling, device_id_type=pl.DeviceIdType.MESH)
    for shift in range(1, owners):
        pl.semaphore_signal(
            barrier,
            inc=1,
            device_id={"expert": lax.rem(me + shift, owners)},
            device_id_type=pl.DeviceIdType.MESH,
        )

    def remote(src, dst, send, recv, device):
        return pltpu.make_async_remote_copy(
            src_ref=src,
            dst_ref=dst,
            send_sem=send,
            recv_sem=recv,
            device_id=device,
            device_id_type=pl.DeviceIdType.MESH,
        )

    own_cot = pltpu.make_async_copy(
        cot_hbm, cot_all.at[me, :, pl.ds(0, feat_width)], load_sem.at[0]
    )
    own_cot.start()
    lane_of = lax.broadcasted_iota(jnp.int32, (total, lanes), 1)
    hits = lane_of == routes_ref[:, 0:1]
    for pick in range(1, routes_ref.shape[1]):
        hits = hits | (lane_of == routes_ref[:, pick : pick + 1])
    cot_all[me, :, feat_width:] = jnp.where(hits, 1.0, 0.0).astype(jnp.bfloat16)
    experts_named = router_ref.shape[1]
    router_wide[...] = jnp.concatenate(
        [router_ref[...], jnp.zeros((feat_width, lanes - experts_named), jnp.bfloat16)], axis=1
    )

    buffers = (rows_all, cot_all)

    def chain(step, what, side):
        block = me - side * (step - 1)
        to = me + side
        there = (block >= 0) & (block < owners) & (to >= 0) & (to < owners)
        safe = jnp.clip(block, 0, owners - 1)
        at = 0 if side == 1 else 1
        copy = remote(
            buffers[what].at[safe, mine],
            buffers[what].at[safe, mine],
            chain_send.at[what, step - 1, at],
            chain_recv.at[what, safe],
            {"expert": jnp.clip(to, 0, owners - 1)},
        )
        return there, copy

    def swap(what, block):
        return remote(
            buffers[what].at[block, mine],
            buffers[what].at[block, mine],
            swap_send.at[what, block],
            swap_recv.at[what, block],
            sibling,
        )

    def swap_arrival(what, block):
        return remote(
            buffers[what].at[block, others],
            buffers[what].at[block, others],
            swap_send.at[what, block],
            swap_recv.at[what, block],
            sibling,
        )

    def send_step(step, what):
        for side in (1, -1):
            there, copy = chain(step, what, side)

            @pl.when(there)
            def _():
                copy.start()

    def arrivals(step, what):
        for side in (1, -1):
            block = me - side * step
            there = (block >= 0) & (block < owners)
            safe = jnp.clip(block, 0, owners - 1)

            @pl.when(there)
            def _():
                chain_copy = remote(
                    buffers[what].at[safe, mine],
                    buffers[what].at[safe, mine],
                    chain_send.at[what, step - 1, 0],
                    chain_recv.at[what, safe],
                    sibling,
                )
                chain_copy.wait_recv()

        if step + 1 < owners:
            send_step(step + 1, what)
        for side in (1, -1):
            block = me - side * step
            there = (block >= 0) & (block < owners)
            safe = jnp.clip(block, 0, owners - 1)

            @pl.when(there)
            def _():
                swap(what, safe).start()

    heads, length, head_size = query_hbm.shape
    kv_heads = key_hbm.shape[0]
    groups = heads // kv_heads
    tile = 64

    def attention_phase(
        tokens, query_weight, keyvalue_weight, out_weight, normed, query, key, value, group_out, heads_out, partial, middle
    ):
        load_tokens = pltpu.make_async_copy(tokens_hbm, tokens, load_sem.at[1])
        loads = (
            pltpu.make_async_copy(query_weight_hbm, query_weight, load_sem.at[2]),
            pltpu.make_async_copy(keyvalue_weight_hbm, keyvalue_weight, load_sem.at[3]),
            pltpu.make_async_copy(out_weight_hbm, out_weight, load_sem.at[4]),
        )
        keeps = (
            pltpu.make_async_copy(normed, normed_hbm, keep_sem.at[0]),
            pltpu.make_async_copy(query, query_hbm, keep_sem.at[1]),
            pltpu.make_async_copy(key, key_hbm, keep_sem.at[2]),
            pltpu.make_async_copy(value, value_hbm, keep_sem.at[3]),
            pltpu.make_async_copy(heads_out, heads_hbm, keep_sem.at[4]),
            pltpu.make_async_copy(middle, middle_hbm, keep_sem.at[5]),
        )
        load_tokens.start()
        for copy in loads:
            copy.start()
        for expert in range(local):
            pltpu.make_async_copy(
                gateup_hbm.at[expert], gateup_ref.at[expert], weight_sem.at[0, expert]
            ).start()
            pltpu.make_async_copy(
                down_hbm.at[expert], down_ref.at[expert], weight_sem.at[1, expert]
            ).start()
        own_cot.wait()
        pl.semaphore_wait(barrier, owners)
        send_step(1, 1)
        load_tokens.wait()

        def first_norm(step, carry):
            at = pl.ds(pl.multiple_of(step * tile, tile), tile)
            unit, _ = norm_parts(tokens[at].astype(jnp.float32))
            normed[at] = (unit * attn_gain_ref[...]).astype(jnp.bfloat16)
            return carry

        lax.fori_loop(0, total // tile, first_norm, 0)
        keeps[0].start()

        def turned(values):
            swapped = jnp.concatenate(
                [values[:, head_size // 2 :], values[:, : head_size // 2]], axis=1
            )
            return (values * cosine_ref[...] - swapped * sine_ref[...]).astype(jnp.bfloat16)

        loads[0].wait()
        projected = jnp.dot(normed[...], query_weight[...], preferred_element_type=jnp.float32)
        for head in range(heads):
            query[head] = turned(projected[:, head * head_size : (head + 1) * head_size])
        loads[1].wait()
        projected = jnp.dot(normed[...], keyvalue_weight[0], preferred_element_type=jnp.float32)
        for head in range(kv_heads):
            key[head] = turned(projected[:, head * head_size : (head + 1) * head_size])
        projected = jnp.dot(normed[...], keyvalue_weight[1], preferred_element_type=jnp.float32)
        for head in range(kv_heads):
            value[head] = projected[:, head * head_size : (head + 1) * head_size].astype(
                jnp.bfloat16
            )
        for copy in keeps[1:4]:
            copy.start()
        causal = length // 2

        def body(group, carry):
            keys, values = key[group], value[group]
            found = []
            for member in range(groups):
                some = query[group * groups + member]
                pieces = []
                for start in (0, causal):
                    stop = start + causal
                    scores = contract(some[start:stop], keys[:stop], 1, 1) * ATTN_SCALE
                    row = start + lax.broadcasted_iota(jnp.int32, scores.shape, 0)
                    col = lax.broadcasted_iota(jnp.int32, scores.shape, 1)
                    scores = jnp.where(row >= col, scores, NEGATIVE)
                    raised = jnp.exp(scores - jnp.max(scores, axis=1, keepdims=True))
                    probs = raised / jnp.sum(raised, axis=1, keepdims=True)
                    pieces.append(
                        jnp.dot(
                            probs.astype(jnp.bfloat16),
                            values[:stop],
                            preferred_element_type=jnp.float32,
                        )
                    )
                found.append(jnp.concatenate(pieces, axis=0))
            group_out[group] = jnp.concatenate(found, axis=1).astype(jnp.bfloat16)

            @pl.when(group == kv_heads - 1)
            def _():
                arrivals(1, 1)

            return carry

        lax.fori_loop(0, kv_heads, body, 0)
        heads_out[...] = jnp.concatenate([group_out[g] for g in range(kv_heads)], axis=1)
        keeps[4].start()
        loads[2].wait()
        partial[...] = jnp.dot(heads_out[...], out_weight[...], preferred_element_type=jnp.float32)
        half_send[...] = partial[others].astype(jnp.bfloat16)
        half_copy = remote(half_send, half_land, half_sem.at[0], half_sem.at[1], sibling)
        half_copy.start()
        half_copy.wait()

        def second_norm(step, carry):
            at = pl.ds(pl.multiple_of(step * tile, tile), tile)
            to = pl.ds(pl.multiple_of(core * half + step * tile, tile), tile)
            after = tokens[to].astype(jnp.float32) + RESIDUAL * (
                partial[to] + half_land[at].astype(jnp.float32)
            )
            middle[at] = after
            unit, _ = norm_parts(after)
            rows_all[me, to] = (unit * expert_gain_ref[...]).astype(jnp.bfloat16)
            return carry

        lax.fori_loop(0, half // tile, second_norm, 0)
        swap(0, me).start()
        send_step(1, 0)
        keeps[5].start()
        for copy in keeps:
            copy.wait()

    pl.run_scoped(
        attention_phase,
        pltpu.VMEM((total, feat_width), jnp.bfloat16),
        pltpu.VMEM(query_weight_hbm.shape, jnp.bfloat16),
        pltpu.VMEM(keyvalue_weight_hbm.shape, jnp.bfloat16),
        pltpu.VMEM(out_weight_hbm.shape, jnp.bfloat16),
        pltpu.VMEM((total, feat_width), jnp.bfloat16),
        pltpu.VMEM(query_hbm.shape, jnp.bfloat16),
        pltpu.VMEM(key_hbm.shape, jnp.bfloat16),
        pltpu.VMEM(value_hbm.shape, jnp.bfloat16),
        pltpu.VMEM((kv_heads, total, groups * head_size), jnp.bfloat16),
        pltpu.VMEM(heads_hbm.shape, jnp.bfloat16),
        pltpu.VMEM((total, feat_width), jnp.float32),
        pltpu.VMEM((half, feat_width), jnp.float32),
    )

    def expert_phase(comb_sum, grad_sum, dot_sum, hold_comb, hold_grad, hold_dot, act_stage, hidden_stage):
        lane = lax.broadcasted_iota(jnp.int32, (total, lanes), 1)

        def stage_copies(slot, expert, block):
            return (
                pltpu.make_async_copy(
                    act_stage.at[slot], act_hbm.at[expert, block], stage_sem.at[0, slot]
                ),
                pltpu.make_async_copy(
                    hidden_stage.at[slot], hidden_hbm.at[expert, block], stage_sem.at[1, slot]
                ),
            )

        def sums_copies(turn):
            return (
                remote(send_grad, recv_grad.at[turn], sums_send.at[0], grad_recv.at[turn], sibling),
                remote(send_comb, recv_comb.at[turn], sums_send.at[1], comb_recv.at[turn], sibling),
            )

        def back_copy(turn, block):
            return remote(
                recv_grad.at[turn],
                parts_hbm.at[me],
                back_send.at[turn],
                back_recv.at[me],
                {"expert": block},
            )

        def own_back():
            return pltpu.make_async_copy(recv_grad.at[0], parts_hbm.at[me], back_send.at[0])

        def comb_copy(turn, block):
            return pltpu.make_async_copy(
                recv_comb.at[turn],
                comb_hbm.at[lax.rem(block - me + owners, owners)],
                comb_sem.at[turn],
            )

        def settle(turn):
            block = block_order(me, owners, turn)
            copy_grad, copy_comb = sums_copies(turn)
            copy_grad.wait_recv()
            got = recv_grad[turn].astype(jnp.float32)
            recv_grad[turn, :, :feat_width] = (hold_grad[...] + got[:, :feat_width]).astype(
                jnp.bfloat16
            )
            dots = hold_dot[...] + got[:, feat_width:]
            lower = lanes // 2
            dots = dots + jnp.concatenate([dots[:, lower:], dots[:, :lower]], axis=1)
            low_lane = lax.broadcasted_iota(jnp.int32, (half, lanes), 1) < lower
            recv_grad[turn, :, feat_width:] = split_two(jnp.where(low_lane, dots, 0.0))

            @pl.when(turn > 0)
            def _():
                back_copy(turn, block).start()

            @pl.when(turn == 0)
            def _():
                own_back().start()

            copy_comb.wait_recv()
            recv_comb[turn] = (hold_comb[...] + recv_comb[turn].astype(jnp.float32)).astype(
                jnp.bfloat16
            )
            comb_copy(turn, block).start()

        def body(number, carry):
            turn = number // local
            expert = number % local
            block = block_order(me, owners, turn)
            slot = number % 2

            @pl.when(expert == 0)
            def _():
                swap_arrival_needed = turn > 0

                @pl.when(swap_arrival_needed)
                def _():
                    swap_arrival(1, block).wait_recv()

                swap_arrival(0, block).wait_recv()
                hits = cot_all[block, :, feat_width:].astype(jnp.float32) > 0.5
                logits = jnp.dot(
                    rows_all[block], router_wide[...], preferred_element_type=jnp.float32
                )
                logits = jnp.where(hits, logits, NEGATIVE)
                raised = jnp.where(
                    hits, jnp.exp(logits - jnp.max(logits, axis=1, keepdims=True)), 0.0
                )
                gates_ref[...] = raised / jnp.sum(raised, axis=1, keepdims=True)

                @pl.when(turn == 0)
                def _():
                    gates_out[...] = gates_ref[mine]

            @pl.when(number < local)
            def _():
                pltpu.make_async_copy(
                    gateup_hbm.at[expert], gateup_ref.at[expert], weight_sem.at[0, expert]
                ).wait()
                pltpu.make_async_copy(
                    down_hbm.at[expert], down_ref.at[expert], weight_sem.at[1, expert]
                ).wait()

            @pl.when(number >= 2)
            def _():
                for copy in stage_copies(slot, expert, block):
                    copy.wait()

            rows = rows_all[block]
            gate_weight, up_weight, down = (
                gateup_ref[expert, 0],
                gateup_ref[expert, 1],
                down_ref[expert],
            )
            gate_part = jnp.dot(rows, gate_weight, preferred_element_type=jnp.float32)
            up_part = jnp.dot(rows, up_weight, preferred_element_type=jnp.float32)
            raw = contract(cot_all[block, :, :feat_width], down, 1, 1)
            here = lane == me * local + expert
            weight = jnp.sum(jnp.where(here, gates_ref[...], 0.0), axis=1, keepdims=True)
            sigmoid_gate = jax.nn.sigmoid(gate_part)
            silu_gate = gate_part * sigmoid_gate
            activation = silu_gate * up_part
            dots = jnp.where(here, jnp.sum(activation * raw, axis=1, keepdims=True), 0.0)
            weighted = (activation * weight).astype(jnp.bfloat16)
            act_stage[slot] = weighted
            grad_act = raw * (RESIDUAL * weight)
            grad_gatepart = (
                grad_act * up_part * (sigmoid_gate * (1.0 + gate_part * (1.0 - sigmoid_gate)))
            ).astype(jnp.bfloat16)
            grad_uppart = (grad_act * silu_gate).astype(jnp.bfloat16)
            hidden_stage[slot, :, :units] = grad_gatepart
            hidden_stage[slot, :, units:] = grad_uppart
            for copy in stage_copies(slot, expert, block):
                copy.start()
            comb = jnp.dot(weighted, down, preferred_element_type=jnp.float32)
            grad = contract(grad_gatepart, gate_weight, 1, 1) + contract(
                grad_uppart, up_weight, 1, 1
            )

            @pl.when(expert == 0)
            def _():
                comb_sum[...] = comb
                grad_sum[...] = grad
                dot_sum[...] = dots

            @pl.when(expert > 0)
            def _():
                comb_sum[...] += comb
                grad_sum[...] += grad
                dot_sum[...] += dots

            @pl.when((expert == 1) & (turn > 0))
            def _():
                settle(turn - 1)

            for step in range(1, owners):

                @pl.when(number == step * local - 2)
                def _():
                    arrivals(step, 0)

            for step in range(2, owners):

                @pl.when(number == (step - 2) * (local - 1) + 2)
                def _():
                    arrivals(step, 1)

            @pl.when(expert == local - 1)
            def _():
                @pl.when(turn > 0)
                def _():
                    for copy in sums_copies(turn):
                        copy.wait_send()

                send_grad[:, :feat_width] = grad_sum[others].astype(jnp.bfloat16)
                send_grad[:, feat_width:] = split_two(dot_sum[others])
                send_comb[...] = comb_sum[others].astype(jnp.bfloat16)
                for copy in sums_copies(turn):
                    copy.start()
                hold_grad[...] = grad_sum[mine]
                hold_comb[...] = comb_sum[mine]
                hold_dot[...] = dot_sum[mine]

            return carry

        lax.fori_loop(0, owners * local, body, 0)
        settle(owners - 1)
        for copy in sums_copies(owners - 1):
            copy.wait_send()
        for slot in range(2):
            for copy in stage_copies(slot, 0, 0):
                copy.wait()
        for turn in range(owners):
            block = block_order(me, owners, turn)
            comb_copy(turn, block).wait()

    pl.run_scoped(
        expert_phase,
        pltpu.VMEM((total, feat_width), jnp.float32),
        pltpu.VMEM((total, feat_width), jnp.float32),
        pltpu.VMEM((total, lanes), jnp.float32),
        pltpu.VMEM((half, feat_width), jnp.float32),
        pltpu.VMEM((half, feat_width), jnp.float32),
        pltpu.VMEM((half, lanes), jnp.float32),
        pltpu.VMEM((2, total, units), jnp.bfloat16),
        pltpu.VMEM((2, total, 2 * units), jnp.bfloat16),
    )

    width = feat_width // chunks

    def weights_body(act_ref, hidden_ref, grads_out):
        up_sum = sum(contract(rows_all[b], hidden_ref[0, b], 0, 0) for b in range(owners))
        up_sum = up_sum.astype(jnp.bfloat16)
        down_sum = sum(
            contract(act_ref[0, b], cot_all[b, :, :feat_width], 0, 0) for b in range(owners)
        )
        down_sum = (RESIDUAL * down_sum).T.astype(jnp.bfloat16)
        for chunk in range(chunks):
            for part in range(2):
                grads_out[chunk, 0, part, :width] = up_sum[
                    chunk * width : (chunk + 1) * width, part * units : (part + 1) * units
                ]
                start = chunk * width + part * (width // 2)
                grads_out[chunk, 0, part, width:] = down_sum[start : start + width // 2]

    pltpu.emit_pipeline(
        weights_body,
        grid=(local,),
        in_specs=[
            pl.BlockSpec((1, owners, total, units), lambda e: (e, 0, 0, 0)),
            pl.BlockSpec((1, owners, total, 2 * units), lambda e: (e, 0, 0, 0)),
        ],
        out_specs=[
            pl.BlockSpec((chunks, 1, 2, width + width // 2, units), lambda e: (0, e, 0, 0, 0)),
        ],
    )(act_hbm, hidden_hbm, grads_hbm)

    swap(0, me).wait_send()
    for step in range(1, owners):
        for what in range(2):
            for side in (1, -1):
                there, copy = chain(step, what, side)

                @pl.when(there)
                def _():
                    copy.wait_send()

                block = me - side * step
                arrived = (block >= 0) & (block < owners)
                safe = jnp.clip(block, 0, owners - 1)

                @pl.when(arrived)
                def _():
                    swap(what, safe).wait_send()

    pltpu.make_async_copy(recv_grad.at[0], parts_hbm.at[me], back_send.at[0]).wait()
    for turn in range(1, owners):
        block = block_order(me, owners, turn)
        remote(
            recv_grad.at[turn],
            parts_hbm.at[me],
            back_send.at[turn],
            back_recv.at[me],
            {"expert": block},
        ).wait_send()
        source = lax.rem(me + turn, owners)
        remote(
            recv_grad.at[turn],
            parts_hbm.at[source],
            back_send.at[turn],
            back_recv.at[source],
            {"expert": source},
        ).wait_recv()


def experts(
    tokens,
    cot,
    routes,
    attn_gain,
    expert_gain,
    cosine,
    sine,
    router,
    query_weight,
    keyvalue_weight,
    out_weight,
    gateup,
    down,
):
    owners = lax.axis_size("expert")
    chunks = lax.axis_size("dp")
    total, feat_width = tokens.shape
    half = total // 2
    local, units = down.shape[0], down.shape[1]
    lanes = 128
    wide = feat_width + lanes
    heads = query_weight.shape[1] // HEAD_SIZE
    kv_heads = keyvalue_weight.shape[2] // HEAD_SIZE
    hbm = pl.BlockSpec(memory_space=pl.ANY)
    vmem = pl.BlockSpec(memory_space=pltpu.VMEM)
    bf16, f32 = jnp.bfloat16, jnp.float32
    dma = pltpu.SemaphoreType.DMA
    return pl.pallas_call(
        functools.partial(expert_kernel, owners, local, chunks),
        in_specs=[hbm, hbm] + [vmem] * 6 + [hbm] * 5,
        out_specs=[hbm, hbm, vmem] + [hbm] * 9,
        out_shape=[
            jax.ShapeDtypeStruct((owners, half, wide), bf16),
            jax.ShapeDtypeStruct((owners, half, feat_width), bf16),
            jax.ShapeDtypeStruct((half, lanes), f32),
            jax.ShapeDtypeStruct((chunks, local, 2, 3 * feat_width // chunks // 2, units), bf16),
            jax.ShapeDtypeStruct((local, owners, total, units), bf16),
            jax.ShapeDtypeStruct((local, owners, total, 2 * units), bf16),
            jax.ShapeDtypeStruct((total, feat_width), bf16),
            jax.ShapeDtypeStruct((heads, total, HEAD_SIZE), bf16),
            jax.ShapeDtypeStruct((kv_heads, total, HEAD_SIZE), bf16),
            jax.ShapeDtypeStruct((kv_heads, total, HEAD_SIZE), bf16),
            jax.ShapeDtypeStruct((total, heads * HEAD_SIZE), bf16),
            jax.ShapeDtypeStruct((half, feat_width), f32),
        ],
        scratch_shapes=[
            pltpu.VMEM((owners, total, feat_width), bf16),
            pltpu.VMEM((owners, total, wide), bf16),
            pltpu.VMEM((local, 2, feat_width, units), bf16),
            pltpu.VMEM((local, units, feat_width), bf16),
            pltpu.VMEM((feat_width, lanes), bf16),
            pltpu.VMEM((half, feat_width), bf16),
            pltpu.VMEM((half, feat_width), bf16),
            pltpu.VMEM((total, lanes), f32),
            pltpu.VMEM((half, wide), bf16),
            pltpu.VMEM((half, feat_width), bf16),
            pltpu.VMEM((owners, half, wide), bf16),
            pltpu.VMEM((owners, half, feat_width), bf16),
            dma((5,)),
            dma((6,)),
            dma((2,)),
            dma((2, local)),
            dma((2, owners - 1, 2)),
            dma((2, owners)),
            dma((2, owners)),
            dma((2, owners)),
            dma((2,)),
            dma((owners,)),
            dma((owners,)),
            dma((owners,)),
            dma((owners,)),
            dma((owners,)),
            dma((2, 2)),
        ],
        compiler_params=pltpu.CompilerParams(
            vmem_limit_bytes=62 * 2**20, collective_id=0, has_side_effects=True
        ),
        cost_estimate=pl.CostEstimate(
            flops=2 * owners * total * feat_width * units * 9 * local,
            bytes_accessed=80 * 2**20,
            transcendentals=owners * total * units * local,
        ),
    )(
        tokens,
        cot,
        routes,
        attn_gain,
        expert_gain,
        cosine,
        sine,
        router,
        query_weight,
        keyvalue_weight,
        out_weight,
        gateup,
        down,
    )


def factors(count):
    low = 1 << ((count.bit_length() - 1) // 2)
    return count // low, low


class Place:
    def __init__(self, rows, columns, owners):
        self.sizes = {"y": rows, "x": columns, "z": owners}
        index = lax.axis_index("dp")
        self.at = {"y": index // columns, "x": index % columns, "z": lax.axis_index("expert")}

    def peer(self, axis, shift):
        return lax.rem(self.at[axis] + shift, self.sizes[axis])

    def device(self, axis, to):
        if axis == "z":
            return {"expert": to}
        if axis == "x":
            return {"dp": self.at["y"] * self.sizes["x"] + to}
        return {"dp": to * self.sizes["x"] + self.at["x"]}


def picked(ref, position, index):
    return ref.at[(slice(None),) * position + (index,)]


class Summing:
    def __init__(self, place, source, axes, order, landing, send, recv):
        self.place, self.order, self.landing = place, order, landing
        self.send, self.recv = send, recv
        self.sources, self.positions = [source], []
        left = list(axes)
        for step, axis in enumerate(order):
            self.positions.append(left.index(axis))
            left.pop(self.positions[-1])
            self.sources.append(landing[step].at[0])

    def copies(self, step):
        axis = self.order[step]
        found = []
        for shift in range(1, self.place.sizes[axis]):
            to = self.place.peer(axis, shift)
            found.append(
                pltpu.make_async_remote_copy(
                    src_ref=picked(self.sources[step], self.positions[step], to),
                    dst_ref=self.landing[step].at[shift - 1],
                    send_sem=self.send.at[step, shift - 1],
                    recv_sem=self.recv.at[step, shift - 1],
                    device_id=self.place.device(axis, to),
                    device_id_type=pl.DeviceIdType.MESH,
                )
            )
        return found

    def start(self, step):
        for copy in self.copies(step):
            copy.start()

    def total(self, step):
        axis = self.order[step]
        for copy in self.copies(step):
            copy.wait_recv()
        own = picked(self.sources[step], self.positions[step], self.place.at[axis])
        value = own[...].astype(jnp.float32)
        for shift in range(1, self.place.sizes[axis]):
            value = value + self.landing[step][shift - 1].astype(jnp.float32)
        return value

    def forward(self, step):
        self.landing[step][0] = self.total(step).astype(self.landing[step].dtype)
        self.start(step + 1)

    def close(self):
        for step in range(len(self.order)):
            for copy in self.copies(step):
                copy.wait_send()


def norm_grad(grad, gain, unit, inv_rms):
    grad_unit = grad * gain
    return inv_rms * (grad_unit - unit * jnp.mean(grad_unit * unit, axis=-1, keepdims=True))


def back_kernel(
    rows,
    columns,
    owners,
    parts_hbm,
    comb_hbm,
    grads_hbm,
    gates_ref,
    middle_hbm,
    cot_hbm,
    tokens_hbm,
    expert_gain_ref,
    attn_gain_ref,
    router_ref,
    out_weight_ref,
    heads_ref,
    query_ref,
    key_ref,
    value_ref,
    normed_ref,
    query_weight_hbm,
    keyvalue_weight_hbm,
    cosine_ref,
    sine_ref,
    mixed_hbm,
    tokens_grad_hbm,
    gateup_out,
    down_out,
    first_out,
    output_out,
    small_out,
    own_a,
    own_b,
    first_a,
    first_b,
    second_a,
    second_b,
    comb_land,
    out_stage,
    out_z,
    out_x,
    out_y,
    qkv_a,
    qkv_ax,
    qkv_ay,
    qkv_az,
    qkv_b,
    qkv_by,
    qkv_bx,
    qkv_bz,
    small_sum,
    small_swap,
    small_stage,
    small_z,
    small_x,
    small_y,
    grad_attn,
    grad_middle,
    grad_query,
    grad_keyvalue,
    half_send,
    half_land,
    mixed_stage,
    load_sem,
    own_sem,
    first_send,
    first_recv,
    second_send,
    second_recv,
    comb_send,
    comb_recv,
    sum_send,
    sum_recv,
    swap_send,
    swap_recv,
    store_sem,
):
    place = Place(rows, columns, owners)
    core = lax.axis_index("tensor")
    sibling = {"tensor": 1 - core}
    half, feat_width = middle_hbm.shape
    local = grads_hbm.shape[2]
    width = gateup_out.shape[2]
    lanes = gates_ref.shape[1]
    heads, length, head_size = query_ref.shape
    kv_heads = key_ref.shape[0]
    groups = heads // kv_heads
    query_width = heads * head_size
    key_width = kv_heads * head_size
    tile = 64
    mine = pl.ds(pl.multiple_of(core * half, half), half)
    others = pl.ds(pl.multiple_of((1 - core) * half, half), half)

    barrier = pltpu.get_barrier_semaphore()
    peers = [sibling]
    for axis in ("x", "y", "z"):
        for shift in range(1, place.sizes[axis]):
            peers.append(place.device(axis, place.peer(axis, shift)))
    for peer in peers:
        pl.semaphore_signal(barrier, inc=1, device_id=peer, device_id_type=pl.DeviceIdType.MESH)
    pl.semaphore_wait(barrier, len(peers))

    def to_sibling(src, dst, at):
        return pltpu.make_async_remote_copy(
            src_ref=src,
            dst_ref=dst,
            send_sem=swap_send.at[at],
            recv_sem=swap_recv.at[at],
            device_id=sibling,
            device_id_type=pl.DeviceIdType.MESH,
        )

    plans = (
        (0, "x", "y", own_a, first_a, second_a),
        (1, "y", "x", own_b, first_b, second_b),
    )

    def grads_of(part, axis, index, expert):
        if axis == "x":
            return grads_hbm.at[:, index, expert, part]
        return grads_hbm.at[index, :, expert, part]

    def own_load(plan, expert):
        part, axis, _, own, _, _ = plan
        return pltpu.make_async_copy(
            grads_of(part, axis, place.at[axis], expert),
            own.at[expert % 2],
            own_sem.at[part, expert],
        )

    def first_copies(plan, expert):
        part, axis, _, _, first, _ = plan
        found = []
        for shift in range(1, place.sizes[axis]):
            to = place.peer(axis, shift)
            found.append(
                pltpu.make_async_remote_copy(
                    src_ref=grads_of(part, axis, to, expert),
                    dst_ref=first.at[shift - 1, expert],
                    send_sem=first_send.at[part, shift - 1, expert],
                    recv_sem=first_recv.at[part, shift - 1, expert],
                    device_id=place.device(axis, to),
                    device_id_type=pl.DeviceIdType.MESH,
                )
            )
        return found

    def second_copies(plan, expert):
        part, _, axis, _, first, second = plan
        found = []
        for shift in range(1, place.sizes[axis]):
            to = place.peer(axis, shift)
            found.append(
                pltpu.make_async_remote_copy(
                    src_ref=first.at[0, expert, to],
                    dst_ref=second.at[shift - 1, expert],
                    send_sem=second_send.at[part, shift - 1, expert],
                    recv_sem=second_recv.at[part, shift - 1, expert],
                    device_id=place.device(axis, to),
                    device_id_type=pl.DeviceIdType.MESH,
                )
            )
        return found

    def first_sum(expert):
        for plan in plans:
            _, axis, after, own, first, _ = plan
            own_load(plan, expert).wait()
            for copy in first_copies(plan, expert):
                copy.wait_recv()
            for index in range(place.sizes[after]):
                value = own[expert % 2, index].astype(jnp.float32)
                for shift in range(1, place.sizes[axis]):
                    value = value + first[shift - 1, expert, index].astype(jnp.float32)
                first[0, expert, index] = value.astype(first.dtype)
            for copy in second_copies(plan, expert):
                copy.start()

            @pl.when(expert + 2 < local)
            def _():
                own_load(plan, expert + 2).start()

    def second_sum(expert):
        for plan in plans:
            part, _, axis, _, first, second = plan
            for copy in second_copies(plan, expert):
                copy.wait_recv()
            value = first[0, expert, place.at[axis]].astype(jnp.float32)
            for shift in range(1, place.sizes[axis]):
                value = value + second[shift - 1, expert].astype(jnp.float32)
            gateup_out[expert, part] = value[:width]
            down_out[expert, part] = value[width:]

    def start_first(expert, carry):
        for plan in plans:
            for copy in first_copies(plan, expert):
                copy.start()
        return carry

    for plan in plans:
        for expert in range(min(2, local)):
            own_load(plan, expert).start()

    lax.fori_loop(0, local, start_first, 0)

    def comb_copy(shift):
        to = place.peer("z", shift)
        return pltpu.make_async_remote_copy(
            src_ref=comb_hbm.at[shift],
            dst_ref=comb_land.at[shift],
            send_sem=comb_send.at[shift - 1],
            recv_sem=comb_recv.at[shift - 1],
            device_id=place.device("z", to),
            device_id_type=pl.DeviceIdType.MESH,
        )

    own_comb = pltpu.make_async_copy(comb_hbm.at[0], comb_land.at[0], load_sem.at[0])
    own_comb.start()
    for shift in range(1, owners):
        comb_copy(shift).start()

    def job(source, order, landing, at):
        return Summing(
            place, source, ("y", "x", "z"), order, landing, sum_send.at[at], sum_recv.at[at]
        )

    output_job = job(out_stage, ("z", "x", "y"), (out_z, out_x, out_y), 0)
    first_job_a = job(qkv_a, ("x", "y", "z"), (qkv_ax, qkv_ay, qkv_az), 1)
    first_job_b = job(qkv_b, ("y", "x", "z"), (qkv_by, qkv_bx, qkv_bz), 2)
    small_job = job(small_stage, ("z", "x", "y"), (small_z, small_x, small_y), 3)

    def weight_grad(stage, left, right):
        count = stage.shape[3]
        band = feat_width // 4
        for start in range(0, feat_width, band):
            value = contract(left[:, start : start + band], right, 0, 0).astype(jnp.bfloat16)
            for at in range(start, start + band, count):
                index = at // count
                y, x, z = (
                    index // (columns * owners),
                    index // owners % columns,
                    index % owners,
                )
                stage[y, x, z] = value[at - start : at - start + count]

    def middle_phase(parts, middle, cot_ref):
        loads = (
            pltpu.make_async_copy(cot_hbm.at[mine], cot_ref, load_sem.at[3]),
            pltpu.make_async_copy(parts_hbm, parts, load_sem.at[1]),
            pltpu.make_async_copy(middle_hbm, middle, load_sem.at[2]),
        )
        for copy in loads:
            copy.start()
        for copy in loads:
            copy.wait()
        small_sum[...] = jnp.zeros_like(small_sum)

        def body(step, carry):
            at = pl.ds(pl.multiple_of(step * tile, tile), tile)
            grad = sum(parts[b, at, :feat_width].astype(jnp.float32) for b in range(owners))
            dots = sum(parts[b, at, feat_width:].astype(jnp.float32) for b in range(owners))
            lower = lanes // 2
            dots = dots + jnp.concatenate([dots[:, lower:], dots[:, :lower]], axis=1)
            gates = gates_ref[at]
            grad_gate = RESIDUAL * dots
            grad_logits = (
                gates * (grad_gate - jnp.sum(gates * grad_gate, axis=-1, keepdims=True))
            ).astype(jnp.bfloat16)
            grad = grad + contract(
                grad_logits[:, : router_ref.shape[1]], router_ref[...], 1, 1
            )
            unit, inv_rms = norm_parts(middle[at])
            expert_in = (unit * expert_gain_ref[...]).astype(jnp.bfloat16)
            after = cot_ref[at].astype(jnp.float32) + norm_grad(
                grad, expert_gain_ref[...], unit, inv_rms
            )
            grad_middle[at] = after
            to = pl.ds(pl.multiple_of(core * half + step * tile, tile), tile)
            grad_attn[to] = (RESIDUAL * after).astype(jnp.bfloat16)
            count = small_sum.shape[0]
            small_sum[...] += contract(grad_logits, expert_in, 0, 0)[:count]
            small_sum[count - 2 : count - 1] += jnp.sum(grad * unit, axis=0, keepdims=True)
            return carry

        lax.fori_loop(0, half // tile, body, 0)

    pl.run_scoped(
        middle_phase,
        pltpu.VMEM(parts_hbm.shape, parts_hbm.dtype),
        pltpu.VMEM(middle_hbm.shape, middle_hbm.dtype),
        pltpu.VMEM(middle_hbm.shape, cot_hbm.dtype),
    )
    attn_swap = to_sibling(grad_attn.at[mine], grad_attn.at[mine], 0)
    attn_swap.start()
    to_sibling(grad_attn.at[others], grad_attn.at[others], 0).wait_recv()

    weight_grad(out_stage, grad_attn, heads_ref[...])
    output_job.start(0)
    causal = length // 2

    def attention_phase(key_sum, value_sum):
        def turned_back(grads):
            swapped = jnp.concatenate(
                [grads[:, head_size // 2 :], grads[:, : head_size // 2]], axis=1
            )
            return (grads * cosine_ref[...] + swapped * sine_ref[...]).astype(jnp.bfloat16)

        def body(group, carry):
            grad_heads = contract(grad_attn[...], out_weight_ref[group], 1, 1).astype(jnp.bfloat16)
            keys, values = key_ref[group], value_ref[group]
            key_sum[...] = jnp.zeros_like(key_sum)
            value_sum[...] = jnp.zeros_like(value_sum)
            turned = []
            for member in range(groups):
                query = query_ref[group * groups + member]
                grad_head = grad_heads[:, member * head_size : (member + 1) * head_size]
                pieces = []
                for start in (0, causal):
                    stop = start + causal
                    some_q, some_g = query[start:stop], grad_head[start:stop]
                    some_k, some_v = keys[:stop], values[:stop]
                    scores = contract(some_q, some_k, 1, 1) * ATTN_SCALE
                    row = start + lax.broadcasted_iota(jnp.int32, scores.shape, 0)
                    col = lax.broadcasted_iota(jnp.int32, scores.shape, 1)
                    scores = jnp.where(row >= col, scores, NEGATIVE)
                    raised = jnp.exp(scores - jnp.max(scores, axis=1, keepdims=True))
                    probs = raised / jnp.sum(raised, axis=1, keepdims=True)
                    grad_probs = contract(some_g, some_v, 1, 1)
                    value_sum[:stop] += contract(probs.astype(jnp.bfloat16), some_g, 0, 0)
                    grad_scores = (
                        probs
                        * (grad_probs - jnp.sum(probs * grad_probs, axis=1, keepdims=True))
                    ).astype(jnp.bfloat16)
                    pieces.append(
                        jnp.dot(grad_scores, some_k, preferred_element_type=jnp.float32)
                    )
                    key_sum[:stop] += contract(grad_scores, some_q, 0, 0)
                turned.append(turned_back(ATTN_SCALE * jnp.concatenate(pieces, axis=0)))
            grad_query[group] = jnp.concatenate(turned, axis=1)
            grad_keyvalue[0, group] = turned_back(ATTN_SCALE * key_sum[...])
            grad_keyvalue[1, group] = value_sum[...].astype(jnp.bfloat16)

            @pl.when(group < local)
            def _():
                first_sum(group)

            return carry

        lax.fori_loop(0, kv_heads, body, 0)

    pl.run_scoped(
        attention_phase,
        pltpu.VMEM((length, head_size), jnp.float32),
        pltpu.VMEM((length, head_size), jnp.float32),
    )
    for expert in range(kv_heads, local):
        first_sum(expert)

    def tokens_phase(query_weight, keyvalue_weight, grad_normed, tokens_ref):
        loads = (
            pltpu.make_async_copy(tokens_hbm.at[mine], tokens_ref, load_sem.at[3]),
            pltpu.make_async_copy(query_weight_hbm, query_weight, load_sem.at[1]),
            pltpu.make_async_copy(keyvalue_weight_hbm, keyvalue_weight, load_sem.at[2]),
        )
        for copy in loads:
            copy.start()
        queries = jnp.concatenate([grad_query[g] for g in range(kv_heads)], axis=1)
        keyvalue = [
            jnp.concatenate([grad_keyvalue[what, g] for g in range(kv_heads)], axis=1)
            for what in range(2)
        ]
        cut = (query_width + 2 * key_width) // 2
        left = queries[:, :cut]
        right = jnp.concatenate([queries[:, cut:]] + keyvalue, axis=1)
        weight_grad(qkv_a, normed_ref, left)
        first_job_a.start(0)
        weight_grad(qkv_b, normed_ref, right)
        first_job_b.start(0)
        for copy in loads:
            copy.wait()
        grad_normed[...] = (
            contract(queries, query_weight[...], 1, 1)
            + contract(keyvalue[0], keyvalue_weight[0], 1, 1)
            + contract(keyvalue[1], keyvalue_weight[1], 1, 1)
        )
        half_send[...] = grad_normed[others].astype(jnp.bfloat16)
        swap = to_sibling(half_send, half_land, 1)
        swap.start()
        swap.wait_recv()

        def body(step, carry):
            at = pl.ds(pl.multiple_of(step * tile, tile), tile)
            to = pl.ds(pl.multiple_of(core * half + step * tile, tile), tile)
            grad = grad_normed[to] + half_land[at].astype(jnp.float32)
            unit, inv_rms = norm_parts(tokens_ref[at].astype(jnp.float32))
            grad_middle[at] += norm_grad(grad, attn_gain_ref[...], unit, inv_rms)
            count = small_sum.shape[0]
            small_sum[count - 1 : count] += jnp.sum(grad * unit, axis=0, keepdims=True)
            return carry

        lax.fori_loop(0, half // tile, body, 0)

    pl.run_scoped(
        tokens_phase,
        pltpu.VMEM(query_weight_hbm.shape, query_weight_hbm.dtype),
        pltpu.VMEM(keyvalue_weight_hbm.shape, keyvalue_weight_hbm.dtype),
        pltpu.VMEM((2 * half, feat_width), jnp.float32),
        pltpu.VMEM((half, feat_width), tokens_hbm.dtype),
    )
    tokens_store = pltpu.make_async_copy(grad_middle, tokens_grad_hbm.at[mine], store_sem.at[0])
    tokens_store.start()
    tokens_swap = to_sibling(grad_middle, tokens_grad_hbm.at[mine], 2)
    tokens_swap.start()
    small_exchange = to_sibling(small_sum, small_swap, 3)
    small_exchange.start()

    output_job.forward(0)

    small_exchange.wait()
    small_sum[...] += small_swap[...]
    piece = feat_width // (rows * columns * owners)
    small_stage[...] = jnp.zeros_like(small_stage)
    for y in range(rows):
        for x in range(columns):
            for z in range(owners):
                at = ((y * columns + x) * owners + z) * piece
                small_stage[y, x, z, :, :piece] = small_sum[:, at : at + piece]
    small_job.start(0)

    own_comb.wait()
    for shift in range(1, owners):
        comb_copy(shift).wait_recv()

    def mixed_phase(middle):
        load = pltpu.make_async_copy(middle_hbm, middle, load_sem.at[1])
        load.start()
        load.wait()

        def body(step, carry):
            at = pl.ds(pl.multiple_of(step * tile, tile), tile)
            comb = sum(comb_land[b, at].astype(jnp.float32) for b in range(owners))
            mixed_stage[at] = (middle[at] + RESIDUAL * comb).astype(jnp.bfloat16)
            return carry

        lax.fori_loop(0, half // tile, body, 0)

    pl.run_scoped(mixed_phase, pltpu.VMEM(middle_hbm.shape, middle_hbm.dtype))
    mixed_store = pltpu.make_async_copy(mixed_stage, mixed_hbm.at[mine], store_sem.at[1])
    mixed_store.start()
    mixed_swap = to_sibling(mixed_stage, mixed_hbm.at[mine], 4)
    mixed_swap.start()

    small_job.forward(0)
    output_job.forward(1)
    small_job.forward(1)

    def finish(expert, carry):
        second_sum(expert)
        return carry

    lax.fori_loop(0, local, finish, 0)
    first_job_a.forward(0)
    first_job_b.forward(0)
    output_out[...] = output_job.total(2)
    small_out[...] = small_job.total(2)
    first_job_a.forward(1)
    first_job_b.forward(1)
    cut = qkv_a.shape[4]
    first_out[:, :cut] = first_job_a.total(2)
    first_out[:, cut:] = first_job_b.total(2)

    def close(expert, carry):
        for plan in plans:
            for copy in first_copies(plan, expert) + second_copies(plan, expert):
                copy.wait_send()
        return carry

    lax.fori_loop(0, local, close, 0)
    for shift in range(1, owners):
        comb_copy(shift).wait_send()
    for which in (output_job, first_job_a, first_job_b, small_job):
        which.close()
    attn_swap.wait_send()
    to_sibling(half_send, half_land, 1).wait_send()
    tokens_store.wait()
    mixed_store.wait()
    tokens_swap.wait_send()
    mixed_swap.wait_send()
    to_sibling(grad_middle, tokens_grad_hbm.at[others], 2).wait_recv()
    to_sibling(mixed_stage, mixed_hbm.at[others], 4).wait_recv()


def backward(
    parts,
    combs,
    grads,
    gates,
    middle,
    cot,
    tokens,
    expert_gain,
    attn_gain,
    router,
    out_weight,
    heads_out,
    query,
    keys,
    values,
    normed,
    query_weight,
    keyvalue_weight,
    cosine,
    sine,
):
    owners = lax.axis_size("expert")
    chunks = lax.axis_size("dp")
    rows, columns = factors(chunks)
    half, feat_width = middle.shape
    local, _, height, units = grads.shape[1:]
    width = feat_width // chunks
    grads = grads.reshape((rows, columns) + grads.shape[1:])
    piece = feat_width // (chunks * owners)
    heads, length, head_size = query.shape
    kv_heads = keys.shape[0]
    query_width, key_width = heads * head_size, kv_heads * head_size
    cut = (query_width + 2 * key_width) // 2
    lanes = gates.shape[1]
    count = 24
    out_weight = out_weight.reshape(kv_heads, query_width // kv_heads, feat_width)
    bf16, f32 = jnp.bfloat16, jnp.float32
    hbm = pl.BlockSpec(memory_space=pl.ANY)
    vmem = pl.BlockSpec(memory_space=pltpu.VMEM)
    dma = pltpu.SemaphoreType.DMA
    most = max(rows, columns, owners) - 1

    def landings(tail, order, dtype):
        sizes = {"y": rows, "x": columns, "z": owners}
        left = ["y", "x", "z"]
        found = []
        for axis in order:
            left.remove(axis)
            found.append(
                pltpu.VMEM((sizes[axis] - 1,) + tuple(sizes[a] for a in left) + tail, dtype)
            )
        return found

    whole = (rows, columns, owners)
    return pl.pallas_call(
        functools.partial(back_kernel, rows, columns, owners),
        in_specs=[hbm, hbm, hbm, vmem, hbm, hbm, hbm] + [vmem] * 9 + [hbm, hbm, vmem, vmem],
        out_specs=[hbm, hbm, vmem, vmem, vmem, vmem, vmem],
        out_shape=[
            jax.ShapeDtypeStruct((2 * half, feat_width), bf16),
            jax.ShapeDtypeStruct((2 * half, feat_width), f32),
            jax.ShapeDtypeStruct((local, 2, width, units), f32),
            jax.ShapeDtypeStruct((local, 2, width // 2, units), f32),
            jax.ShapeDtypeStruct((piece, 2 * cut), f32),
            jax.ShapeDtypeStruct((piece, query_width), f32),
            jax.ShapeDtypeStruct((count, lanes), f32),
        ],
        scratch_shapes=[
            pltpu.VMEM((2, rows, height, units), bf16),
            pltpu.VMEM((2, columns, height, units), bf16),
            pltpu.VMEM((columns - 1, local, rows, height, units), bf16),
            pltpu.VMEM((rows - 1, local, columns, height, units), bf16),
            pltpu.VMEM((rows - 1, local, height, units), bf16),
            pltpu.VMEM((columns - 1, local, height, units), bf16),
            pltpu.VMEM((owners, half, feat_width), bf16),
            pltpu.VMEM(whole + (piece, query_width), bf16),
            *landings((piece, query_width), "zxy", bf16),
            pltpu.VMEM(whole + (piece, cut), bf16),
            *landings((piece, cut), "xyz", bf16),
            pltpu.VMEM(whole + (piece, cut), bf16),
            *landings((piece, cut), "yxz", bf16),
            pltpu.VMEM((count, feat_width), f32),
            pltpu.VMEM((count, feat_width), f32),
            pltpu.VMEM(whole + (count, lanes), f32),
            *landings((count, lanes), "zxy", f32),
            pltpu.VMEM((2 * half, feat_width), bf16),
            pltpu.VMEM((half, feat_width), f32),
            pltpu.VMEM((kv_heads, length, query_width // kv_heads), bf16),
            pltpu.VMEM((2, kv_heads, length, head_size), bf16),
            pltpu.VMEM((half, feat_width), bf16),
            pltpu.VMEM((half, feat_width), bf16),
            pltpu.VMEM((half, feat_width), bf16),
            dma((4,)),
            dma((2, local)),
            dma((2, most, local)),
            dma((2, most, local)),
            dma((2, most, local)),
            dma((2, most, local)),
            dma((owners - 1,)),
            dma((owners - 1,)),
            dma((4, 3, most)),
            dma((4, 3, most)),
            dma((5,)),
            dma((5,)),
            dma((2,)),
        ],
        compiler_params=pltpu.CompilerParams(
            vmem_limit_bytes=60 * 2**20, collective_id=1, has_side_effects=True
        ),
        cost_estimate=pl.CostEstimate(
            flops=12 * 2**30, bytes_accessed=60 * 2**20, transcendentals=heads * length * length
        ),
    )(
        parts,
        combs,
        grads,
        gates,
        middle,
        cot,
        tokens,
        expert_gain,
        attn_gain,
        router,
        out_weight,
        heads_out,
        query,
        keys,
        values,
        normed,
        query_weight,
        keyvalue_weight,
        cosine,
        sine,
    )


def per_device(
    tokens,
    out_grad,
    attn_gain,
    query_weight,
    key_value_weight,
    output_weight,
    expert_gain,
    router_weight,
    gateup_weight,
    down_weight,
    routes,
):
    feat_width = tokens.shape[1]
    expert_count = router_weight.shape[1]
    owners = lax.axis_size("expert")
    chunks = lax.axis_size("dp")
    local_experts = gateup_weight.shape[0]
    cosine, sine = rotary_tables()
    parts, combs, gates, grads, _, _, normed, query, keys, values, heads_out, middle = experts(
        tokens,
        out_grad,
        routes,
        attn_gain[None],
        expert_gain[None],
        cosine,
        sine,
        router_weight,
        query_weight,
        key_value_weight,
        output_weight,
        gateup_weight,
        down_weight,
    )
    mixed, tokens_grad, gateup_total, down_total, first_total, output_total, small = backward(
        parts,
        combs,
        grads,
        gates,
        middle,
        out_grad,
        tokens,
        expert_gain[None],
        attn_gain[None],
        router_weight,
        output_weight,
        heads_out,
        query,
        keys,
        values,
        normed,
        query_weight,
        key_value_weight,
        cosine,
        sine,
    )
    query_width = query_weight.shape[1]
    key_width = key_value_weight.shape[2]
    piece = feat_width // (chunks * owners)
    down_total = down_total.reshape(local_experts, -1, down_weight.shape[1]).transpose(0, 2, 1)
    return (
        mixed,
        tokens_grad,
        small[23, :piece],
        first_total[:, :query_width],
        jnp.stack(
            [
                first_total[:, query_width : query_width + key_width],
                first_total[:, query_width + key_width :],
            ],
            axis=0,
        ),
        output_total.T,
        small[22, :piece],
        small[:expert_count, :piece].T,
        gateup_total,
        down_total,
    )


def solution(mesh):
    placed = (
        P(("dp", "expert"), None),
        P(("dp", "expert"), None),
        P(),
        P(None, "tensor"),
        P(None, None, "tensor"),
        P("tensor", None),
        P(),
        P(),
        P("expert", None, None, "tensor"),
        P("expert", "tensor", None),
        P(("dp", "expert"), None),
    )
    return jax.shard_map(
        per_device,
        mesh=mesh,
        in_specs=placed,
        out_specs=(
            P(("dp", "expert"), None),
            P(("dp", "expert"), None),
            P(("dp", "expert")),
            P(("dp", "expert"), "tensor"),
            P(None, ("dp", "expert"), "tensor"),
            P("tensor", ("dp", "expert")),
            P(("dp", "expert")),
            P(("dp", "expert"), None),
            P("expert", None, "dp", "tensor"),
            P("expert", "tensor", "dp"),
        ),
        check_vma=False,
    )
```

```python
import functools

import jax
import jax.numpy as jnp
import numpy as np
from jax import lax
from jax.experimental import pallas as pl
from jax.experimental.pallas import tpu as pltpu
from jax.sharding import PartitionSpec as P

HEAD_SIZE = 64
TOPK = 8
SEQUENCE_LENGTH = 512


EPSILON = 1e-06
RESIDUAL = 0.22
ATTN_SCALE = 0.015625
ROPE_BASE = 10000.0
NEGATIVE = -1e30
EARLY = 2


def rotary_tables():
    half_dim = HEAD_SIZE // 2
    frequency = ROPE_BASE ** (-np.arange(half_dim, dtype=np.float32) * 2.0 / HEAD_SIZE)
    angles = np.arange(SEQUENCE_LENGTH, dtype=np.float32)[:, None] * frequency[None, :]
    angles = angles.astype(np.float32)
    cosine, sine = np.cos(angles), np.sin(angles)
    return (
        jnp.asarray(np.concatenate([cosine, cosine], axis=1), jnp.float32),
        jnp.asarray(np.concatenate([sine, -sine], axis=1), jnp.float32),
    )


def norm_parts(values):
    inv_rms = lax.rsqrt(jnp.mean(values * values, axis=-1, keepdims=True) + EPSILON)
    return values * inv_rms, inv_rms


def factors(count):
    low = 1 << ((count.bit_length() - 1) // 2)
    return count // low, low


class Place:
    def __init__(self, rows, columns, owners):
        self.sizes = {"y": rows, "x": columns, "z": owners}
        index = lax.axis_index("dp")
        self.at = {"y": index // columns, "x": index % columns, "z": lax.axis_index("expert")}

    def peer(self, axis, shift):
        return lax.rem(self.at[axis] + shift, self.sizes[axis])

    def device(self, axis, to):
        if axis == "z":
            return {"expert": to}
        if axis == "x":
            return {"dp": self.at["y"] * self.sizes["x"] + to}
        return {"dp": to * self.sizes["x"] + self.at["x"]}


def picked(ref, position, index):
    return ref.at[(slice(None),) * position + (index,)]


def contract(left, right, left_dim, right_dim):
    return lax.dot_general(
        left, right, (((left_dim,), (right_dim,)), ((), ())), preferred_element_type=jnp.float32
    )


def split_two(values):
    lane = lax.broadcasted_iota(jnp.int32, values.shape, 1)
    high = values.astype(jnp.bfloat16).astype(jnp.float32)
    low = values - high
    half_lanes = values.shape[1] // 2
    moved = jnp.concatenate([low[:, half_lanes:], low[:, :half_lanes]], axis=1)
    return jnp.where(lane < half_lanes, high, moved).astype(jnp.bfloat16)


def block_order(me, count, turn):
    left, right = me, count - 1 - me
    near = jnp.minimum(left, right)
    sign = jnp.where(left <= right, -1, 1)
    paired = turn <= 2 * near
    distance = jnp.where(paired, (turn + 1) // 2, turn - near)
    toward = jnp.where(paired & (turn % 2 == 1), sign, -sign)
    return me + toward * distance


def expert_kernel(
    rows,
    columns,
    owners,
    local,
    early,
    tokens_hbm,
    cot_hbm,
    routes_ref,
    attn_gain_ref,
    expert_gain_ref,
    cosine_ref,
    sine_ref,
    router_ref,
    query_weight_hbm,
    keyvalue_weight_hbm,
    out_weight_hbm,
    gateup_hbm,
    down_hbm,
    parts_hbm,
    comb_hbm,
    gates_out,
    grads_hbm,
    early_a,
    early_b,
    act_hbm,
    hidden_hbm,
    normed_hbm,
    query_hbm,
    key_hbm,
    value_hbm,
    heads_hbm,
    middle_hbm,
    rows_all,
    cot_all,
    gateup_ref,
    down_ref,
    router_wide,
    half_send,
    half_land,
    gates_ref,
    send_grad,
    send_comb,
    recv_grad,
    recv_comb,
    load_sem,
    keep_sem,
    half_sem,
    weight_sem,
    chain_send,
    chain_recv,
    swap_send,
    swap_recv,
    sums_send,
    grad_recv,
    comb_recv,
    back_send,
    back_recv,
    comb_sem,
    stage_sem,
    early_send,
    early_recv,
    dots_sem,
    grads_sem,
):
    place = Place(rows, columns, owners)
    me = lax.axis_index("expert")
    core = lax.axis_index("tensor")
    sibling = {"tensor": 1 - core}
    total, feat_width = rows_all.shape[1], rows_all.shape[2]
    half = total // 2
    units = down_ref.shape[1]
    lanes = gates_ref.shape[1]
    mine = pl.ds(pl.multiple_of(core * half, half), half)
    others = pl.ds(pl.multiple_of((1 - core) * half, half), half)

    barrier = pltpu.get_barrier_semaphore()
    pl.semaphore_signal(barrier, inc=1, device_id=sibling, device_id_type=pl.DeviceIdType.MESH)
    peers = 1
    for axis in ("x", "y", "z"):
        for shift in range(1, place.sizes[axis]):
            pl.semaphore_signal(
                barrier,
                inc=1,
                device_id=place.device(axis, place.peer(axis, shift)),
                device_id_type=pl.DeviceIdType.MESH,
            )
            peers += 1

    def remote(src, dst, send, recv, device):
        return pltpu.make_async_remote_copy(
            src_ref=src,
            dst_ref=dst,
            send_sem=send,
            recv_sem=recv,
            device_id=device,
            device_id_type=pl.DeviceIdType.MESH,
        )

    own_cot = pltpu.make_async_copy(
        cot_hbm, cot_all.at[me, :, pl.ds(0, feat_width)], load_sem.at[0]
    )
    own_cot.start()
    number_of = lax.broadcasted_iota(jnp.int32, (lanes, total), 0)
    hits = number_of == routes_ref[0:1]
    for pick in range(1, routes_ref.shape[0]):
        hits = hits | (number_of == routes_ref[pick : pick + 1])
    cot_all[me, :, feat_width:] = jnp.where(hits, 1.0, 0.0).T.astype(jnp.bfloat16)
    experts_named = router_ref.shape[0]
    router_wide[...] = jnp.concatenate(
        [
            router_ref[...].astype(jnp.float32),
            jnp.zeros((lanes - experts_named, feat_width), jnp.float32),
        ],
        axis=0,
    ).astype(jnp.bfloat16)

    buffers = (rows_all, cot_all)

    def chain(step, what, side):
        block = me - side * (step - 1)
        to = me + side
        there = (block >= 0) & (block < owners) & (to >= 0) & (to < owners)
        safe = jnp.clip(block, 0, owners - 1)
        at = 0 if side == 1 else 1
        copy = remote(
            buffers[what].at[safe, mine],
            buffers[what].at[safe, mine],
            chain_send.at[what, step - 1, at],
            chain_recv.at[what, safe],
            {"expert": jnp.clip(to, 0, owners - 1)},
        )
        return there, copy

    def swap(what, block):
        return remote(
            buffers[what].at[block, mine],
            buffers[what].at[block, mine],
            swap_send.at[what, block],
            swap_recv.at[what, block],
            sibling,
        )

    def swap_arrival(what, block):
        return remote(
            buffers[what].at[block, others],
            buffers[what].at[block, others],
            swap_send.at[what, block],
            swap_recv.at[what, block],
            sibling,
        )

    def send_step(step, what):
        for side in (1, -1):
            there, copy = chain(step, what, side)

            @pl.when(there)
            def _():
                copy.start()

    def arrivals(step, what):
        for side in (1, -1):
            block = me - side * step
            there = (block >= 0) & (block < owners)
            safe = jnp.clip(block, 0, owners - 1)

            @pl.when(there)
            def _():
                chain_copy = remote(
                    buffers[what].at[safe, mine],
                    buffers[what].at[safe, mine],
                    chain_send.at[what, step - 1, 0],
                    chain_recv.at[what, safe],
                    sibling,
                )
                chain_copy.wait_recv()

        if step + 1 < owners:
            send_step(step + 1, what)
        for side in (1, -1):
            block = me - side * step
            there = (block >= 0) & (block < owners)
            safe = jnp.clip(block, 0, owners - 1)

            @pl.when(there)
            def _():
                swap(what, safe).start()

    heads, length, head_size = query_hbm.shape
    kv_heads = key_hbm.shape[0]
    groups = heads // kv_heads
    tile = 64

    def attention_phase(
        tokens, query_weight, keyvalue_weight, out_weight, normed, query, key, value, group_out, heads_out, partial, middle
    ):
        load_tokens = pltpu.make_async_copy(tokens_hbm, tokens, load_sem.at[1])
        loads = (
            pltpu.make_async_copy(query_weight_hbm, query_weight, load_sem.at[2]),
            pltpu.make_async_copy(keyvalue_weight_hbm, keyvalue_weight, load_sem.at[3]),
            pltpu.make_async_copy(out_weight_hbm, out_weight, load_sem.at[4]),
        )
        keeps = (
            pltpu.make_async_copy(normed, normed_hbm, keep_sem.at[0]),
            pltpu.make_async_copy(query, query_hbm, keep_sem.at[1]),
            pltpu.make_async_copy(key, key_hbm, keep_sem.at[2]),
            pltpu.make_async_copy(value, value_hbm, keep_sem.at[3]),
            pltpu.make_async_copy(heads_out, heads_hbm, keep_sem.at[4]),
            pltpu.make_async_copy(middle, middle_hbm, keep_sem.at[5]),
        )
        load_tokens.start()
        for copy in loads:
            copy.start()
        for expert in range(local):
            pltpu.make_async_copy(
                gateup_hbm.at[expert], gateup_ref.at[expert], weight_sem.at[0, expert]
            ).start()
            pltpu.make_async_copy(
                down_hbm.at[expert], down_ref.at[expert], weight_sem.at[1, expert]
            ).start()
        own_cot.wait()
        pl.semaphore_wait(barrier, peers)
        send_step(1, 1)
        load_tokens.wait()

        def first_norm(step, carry):
            at = pl.ds(pl.multiple_of(step * tile, tile), tile)
            unit, _ = norm_parts(tokens[at].astype(jnp.float32))
            normed[at] = (unit * attn_gain_ref[...]).astype(jnp.bfloat16)
            return carry

        lax.fori_loop(0, total // tile, first_norm, 0)
        keeps[0].start()

        def turned(values):
            swapped = jnp.concatenate(
                [values[:, head_size // 2 :], values[:, : head_size // 2]], axis=1
            )
            return (values * cosine_ref[...] - swapped * sine_ref[...]).astype(jnp.bfloat16)

        loads[0].wait()
        projected = jnp.dot(normed[...], query_weight[...], preferred_element_type=jnp.float32)
        for head in range(heads):
            query[head] = turned(projected[:, head * head_size : (head + 1) * head_size])
        loads[1].wait()
        projected = jnp.dot(normed[...], keyvalue_weight[0], preferred_element_type=jnp.float32)
        for head in range(kv_heads):
            key[head] = turned(projected[:, head * head_size : (head + 1) * head_size])
        projected = jnp.dot(normed[...], keyvalue_weight[1], preferred_element_type=jnp.float32)
        for head in range(kv_heads):
            value[head] = projected[:, head * head_size : (head + 1) * head_size].astype(
                jnp.bfloat16
            )
        for copy in keeps[1:4]:
            copy.start()
        causal = length // 2

        def body(group, carry):
            keys, values = key[group], value[group]
            found = []
            for member in range(groups):
                some = query[group * groups + member]
                pieces = []
                for start in (0, causal):
                    stop = start + causal
                    scores = contract(some[start:stop], keys[:stop], 1, 1) * ATTN_SCALE
                    row = start + lax.broadcasted_iota(jnp.int32, scores.shape, 0)
                    col = lax.broadcasted_iota(jnp.int32, scores.shape, 1)
                    scores = jnp.where(row >= col, scores, NEGATIVE)
                    raised = jnp.exp(scores - jnp.max(scores, axis=1, keepdims=True))
                    probs = raised / jnp.sum(raised, axis=1, keepdims=True)
                    pieces.append(
                        jnp.dot(
                            probs.astype(jnp.bfloat16),
                            values[:stop],
                            preferred_element_type=jnp.float32,
                        )
                    )
                found.append(jnp.concatenate(pieces, axis=0))
            group_out[group] = jnp.concatenate(found, axis=1).astype(jnp.bfloat16)

            @pl.when(group == kv_heads - 1)
            def _():
                arrivals(1, 1)

            return carry

        lax.fori_loop(0, kv_heads, body, 0)
        heads_out[...] = jnp.concatenate([group_out[g] for g in range(kv_heads)], axis=1)
        keeps[4].start()
        loads[2].wait()
        partial[...] = jnp.dot(heads_out[...], out_weight[...], preferred_element_type=jnp.float32)
        half_send[...] = partial[others].astype(jnp.bfloat16)
        half_copy = remote(half_send, half_land, half_sem.at[0], half_sem.at[1], sibling)
        half_copy.start()
        half_copy.wait()

        def second_norm(step, carry):
            at = pl.ds(pl.multiple_of(step * tile, tile), tile)
            to = pl.ds(pl.multiple_of(core * half + step * tile, tile), tile)
            after = tokens[to].astype(jnp.float32) + RESIDUAL * (
                partial[to] + half_land[at].astype(jnp.float32)
            )
            middle[at] = after
            unit, _ = norm_parts(after)
            rows_all[me, to] = (unit * expert_gain_ref[...]).astype(jnp.bfloat16)
            return carry

        lax.fori_loop(0, half // tile, second_norm, 0)
        swap(0, me).start()
        send_step(1, 0)
        keeps[5].start()
        for copy in keeps:
            copy.wait()

    pl.run_scoped(
        attention_phase,
        pltpu.VMEM((total, feat_width), jnp.bfloat16),
        pltpu.VMEM(query_weight_hbm.shape, jnp.bfloat16),
        pltpu.VMEM(keyvalue_weight_hbm.shape, jnp.bfloat16),
        pltpu.VMEM(out_weight_hbm.shape, jnp.bfloat16),
        pltpu.VMEM((total, feat_width), jnp.bfloat16),
        pltpu.VMEM(query_hbm.shape, jnp.bfloat16),
        pltpu.VMEM(key_hbm.shape, jnp.bfloat16),
        pltpu.VMEM(value_hbm.shape, jnp.bfloat16),
        pltpu.VMEM((kv_heads, total, groups * head_size), jnp.bfloat16),
        pltpu.VMEM(heads_hbm.shape, jnp.bfloat16),
        pltpu.VMEM((total, feat_width), jnp.float32),
        pltpu.VMEM((half, feat_width), jnp.float32),
    )

    def expert_phase(comb_sum, grad_sum, dot_sum, hold_comb, hold_grad, hold_dot, act_stage, hidden_stage):
        lane = lax.broadcasted_iota(jnp.int32, (total, lanes), 1)

        def stage_copies(slot, expert, block):
            return (
                pltpu.make_async_copy(
                    act_stage.at[slot], act_hbm.at[expert, block], stage_sem.at[0, slot]
                ),
                pltpu.make_async_copy(
                    hidden_stage.at[slot], hidden_hbm.at[expert, block], stage_sem.at[1, slot]
                ),
            )

        def sums_copies(turn):
            return (
                remote(send_grad, recv_grad.at[turn], sums_send.at[0], grad_recv.at[turn], sibling),
                remote(send_comb, recv_comb.at[turn], sums_send.at[1], comb_recv.at[turn], sibling),
            )

        def back_copy(turn, block):
            return remote(
                recv_grad.at[turn],
                parts_hbm.at[me],
                back_send.at[turn],
                back_recv.at[me],
                {"expert": block},
            )

        def own_back():
            return pltpu.make_async_copy(recv_grad.at[0], parts_hbm.at[me], back_send.at[0])

        def comb_copy(turn, block):
            return pltpu.make_async_copy(
                recv_comb.at[turn],
                comb_hbm.at[lax.rem(block - me + owners, owners)],
                comb_sem.at[turn],
            )

        def settle(turn):
            block = block_order(me, owners, turn)
            copy_grad, copy_comb = sums_copies(turn)
            copy_grad.wait_recv()
            got = recv_grad[turn].astype(jnp.float32)
            recv_grad[turn, :, :feat_width] = (hold_grad[...] + got[:, :feat_width]).astype(
                jnp.bfloat16
            )
            dots = hold_dot[...] + got[:, feat_width:]
            lower = lanes // 2
            dots = dots + jnp.concatenate([dots[:, lower:], dots[:, :lower]], axis=1)
            low_lane = lax.broadcasted_iota(jnp.int32, (half, lanes), 1) < lower
            recv_grad[turn, :, feat_width:] = split_two(jnp.where(low_lane, dots, 0.0))

            @pl.when(turn > 0)
            def _():
                back_copy(turn, block).start()

            @pl.when(turn == 0)
            def _():
                own_back().start()

            copy_comb.wait_recv()
            recv_comb[turn] = (hold_comb[...] + recv_comb[turn].astype(jnp.float32)).astype(
                jnp.bfloat16
            )
            comb_copy(turn, block).start()

        def body(number, carry):
            turn = number // local
            expert = number % local
            block = block_order(me, owners, turn)
            slot = number % 2

            @pl.when(expert == 0)
            def _():
                swap_arrival_needed = turn > 0

                @pl.when(swap_arrival_needed)
                def _():
                    swap_arrival(1, block).wait_recv()

                swap_arrival(0, block).wait_recv()
                hits = cot_all[block, :, feat_width:].astype(jnp.float32) > 0.5
                logits = contract(rows_all[block], router_wide[...], 1, 1)
                logits = jnp.where(hits, logits, NEGATIVE)
                raised = jnp.where(
                    hits, jnp.exp(logits - jnp.max(logits, axis=1, keepdims=True)), 0.0
                )
                gates_ref[...] = raised / jnp.sum(raised, axis=1, keepdims=True)

                @pl.when(turn == 0)
                def _():
                    gates_out[...] = gates_ref[mine]

            @pl.when(number < local)
            def _():
                pltpu.make_async_copy(
                    gateup_hbm.at[expert], gateup_ref.at[expert], weight_sem.at[0, expert]
                ).wait()
                pltpu.make_async_copy(
                    down_hbm.at[expert], down_ref.at[expert], weight_sem.at[1, expert]
                ).wait()

            @pl.when(number >= 2)
            def _():
                for copy in stage_copies(slot, expert, block):
                    copy.wait()

            rows = rows_all[block]
            gate_weight, up_weight, down = (
                gateup_ref[expert, 0],
                gateup_ref[expert, 1],
                down_ref[expert],
            )
            gate_part = jnp.dot(rows, gate_weight, preferred_element_type=jnp.float32)
            up_part = jnp.dot(rows, up_weight, preferred_element_type=jnp.float32)
            raw = contract(cot_all[block, :, :feat_width], down, 1, 1)
            here = lane == me * local + expert
            weight = jnp.sum(jnp.where(here, gates_ref[...], 0.0), axis=1, keepdims=True)
            sigmoid_gate = jax.nn.sigmoid(gate_part)
            silu_gate = gate_part * sigmoid_gate
            activation = silu_gate * up_part
            dots = jnp.where(here, jnp.sum(activation * raw, axis=1, keepdims=True), 0.0)
            weighted = (activation * weight).astype(jnp.bfloat16)
            act_stage[slot] = weighted
            grad_act = raw * (RESIDUAL * weight)
            grad_gatepart = (
                grad_act * up_part * (sigmoid_gate * (1.0 + gate_part * (1.0 - sigmoid_gate)))
            ).astype(jnp.bfloat16)
            grad_uppart = (grad_act * silu_gate).astype(jnp.bfloat16)
            hidden_stage[slot, :, :units] = grad_gatepart
            hidden_stage[slot, :, units:] = grad_uppart
            for copy in stage_copies(slot, expert, block):
                copy.start()
            comb = jnp.dot(weighted, down, preferred_element_type=jnp.float32)
            grad = contract(grad_gatepart, gate_weight, 1, 1) + contract(
                grad_uppart, up_weight, 1, 1
            )

            @pl.when(expert == 0)
            def _():
                comb_sum[...] = comb
                grad_sum[...] = grad
                dot_sum[...] = dots

            @pl.when(expert > 0)
            def _():
                comb_sum[...] += comb
                grad_sum[...] += grad
                dot_sum[...] += dots

            @pl.when((expert == 1) & (turn > 0))
            def _():
                settle(turn - 1)

            for step in range(1, owners):

                @pl.when(number == step * local - 2)
                def _():
                    arrivals(step, 0)

            for step in range(2, owners):

                @pl.when(number == (step - 2) * (local - 1) + 2)
                def _():
                    arrivals(step, 1)

            @pl.when(expert == local - 1)
            def _():
                @pl.when(turn > 0)
                def _():
                    for copy in sums_copies(turn):
                        copy.wait_send()

                send_grad[:, :feat_width] = grad_sum[others].astype(jnp.bfloat16)
                send_grad[:, feat_width:] = split_two(dot_sum[others])
                send_comb[...] = comb_sum[others].astype(jnp.bfloat16)
                for copy in sums_copies(turn):
                    copy.start()
                hold_grad[...] = grad_sum[mine]
                hold_comb[...] = comb_sum[mine]
                hold_dot[...] = dot_sum[mine]

            return carry

        lax.fori_loop(0, owners * local, body, 0)
        settle(owners - 1)
        for copy in sums_copies(owners - 1):
            copy.wait_send()
        for slot in range(2):
            for copy in stage_copies(slot, 0, 0):
                copy.wait()
        for turn in range(owners):
            block = block_order(me, owners, turn)
            comb_copy(turn, block).wait()

    pl.run_scoped(
        expert_phase,
        pltpu.VMEM((total, feat_width), jnp.float32),
        pltpu.VMEM((total, feat_width), jnp.float32),
        pltpu.VMEM((total, lanes), jnp.float32),
        pltpu.VMEM((half, feat_width), jnp.float32),
        pltpu.VMEM((half, feat_width), jnp.float32),
        pltpu.VMEM((half, lanes), jnp.float32),
        pltpu.VMEM((2, total, units), jnp.bfloat16),
        pltpu.VMEM((2, total, 2 * units), jnp.bfloat16),
    )

    width = feat_width // (rows * columns)

    def early_copies(expert):
        found = []
        for part, axis, landing in ((0, "x", early_a), (1, "y", early_b)):
            for shift in range(1, place.sizes[axis]):
                to = place.peer(axis, shift)
                source = (
                    grads_hbm.at[:, to, expert, part]
                    if axis == "x"
                    else grads_hbm.at[to, :, expert, part]
                )
                found.append(
                    remote(
                        source,
                        landing.at[shift - 1, expert],
                        early_send.at[part, shift - 1, expert],
                        early_recv.at[part, shift - 1, expert],
                        place.device(axis, to),
                    )
                )
        return found

    def weights_phase(act, hidden, grads):
        def loads(expert):
            slot = expert % 2
            return (
                pltpu.make_async_copy(act_hbm.at[expert], act.at[slot], dots_sem.at[0, slot]),
                pltpu.make_async_copy(
                    hidden_hbm.at[expert], hidden.at[slot], dots_sem.at[1, slot]
                ),
            )

        def store(expert):
            slot = expert % 2
            return pltpu.make_async_copy(
                grads.at[slot], grads_hbm.at[:, :, expert], grads_sem.at[slot]
            )

        def stored(expert):
            store(expert).wait()

            @pl.when(expert < early)
            def _():
                for copy in early_copies(expert):
                    copy.start()

        for copy in loads(0):
            copy.start()

        def body(expert, carry):
            slot = expert % 2

            @pl.when(expert + 1 < local)
            def _():
                for copy in loads(expert + 1):
                    copy.start()

            for copy in loads(expert):
                copy.wait()
            up_sum = sum(contract(rows_all[b], hidden[slot, b], 0, 0) for b in range(owners))
            up_sum = up_sum.astype(jnp.bfloat16)
            for y in range(rows):
                for x in range(columns):
                    start = (y * columns + x) * width
                    for part in range(2):
                        grads[slot, y, x, part, :width] = up_sum[
                            start : start + width, part * units : (part + 1) * units
                        ]
            down_sum = sum(
                contract(act[slot, b], cot_all[b, :, :feat_width], 0, 0) for b in range(owners)
            )
            down_sum = (RESIDUAL * down_sum).T.astype(jnp.bfloat16)
            for y in range(rows):
                for x in range(columns):
                    for part in range(2):
                        start = (y * columns + x) * width + part * (width // 2)
                        grads[slot, y, x, part, width:] = down_sum[start : start + width // 2]

            @pl.when(expert > 0)
            def _():
                stored(expert - 1)

            store(expert).start()
            return carry

        lax.fori_loop(0, local, body, 0)
        stored(local - 1)

    pl.run_scoped(
        weights_phase,
        pltpu.VMEM((2, owners, total, units), jnp.bfloat16),
        pltpu.VMEM((2, owners, total, 2 * units), jnp.bfloat16),
        pltpu.VMEM((2, rows, columns, 2, width + width // 2, units), jnp.bfloat16),
    )

    swap(0, me).wait_send()
    for step in range(1, owners):
        for what in range(2):
            for side in (1, -1):
                there, copy = chain(step, what, side)

                @pl.when(there)
                def _():
                    copy.wait_send()

                block = me - side * step
                arrived = (block >= 0) & (block < owners)
                safe = jnp.clip(block, 0, owners - 1)

                @pl.when(arrived)
                def _():
                    swap(what, safe).wait_send()

    pltpu.make_async_copy(recv_grad.at[0], parts_hbm.at[me], back_send.at[0]).wait()
    for turn in range(1, owners):
        block = block_order(me, owners, turn)
        remote(
            recv_grad.at[turn],
            parts_hbm.at[me],
            back_send.at[turn],
            back_recv.at[me],
            {"expert": block},
        ).wait_send()
        source = lax.rem(me + turn, owners)
        remote(
            recv_grad.at[turn],
            parts_hbm.at[source],
            back_send.at[turn],
            back_recv.at[source],
            {"expert": source},
        ).wait_recv()
    for expert in range(early):
        for copy in early_copies(expert):
            copy.wait()


def experts(
    tokens,
    cot,
    routes,
    attn_gain,
    expert_gain,
    cosine,
    sine,
    router,
    query_weight,
    keyvalue_weight,
    out_weight,
    gateup,
    down,
):
    owners = lax.axis_size("expert")
    rows, columns = factors(lax.axis_size("dp"))
    total, feat_width = tokens.shape
    half = total // 2
    local, units = down.shape[0], down.shape[1]
    height = 3 * feat_width // (rows * columns) // 2
    early = min(EARLY, local)
    most = max(rows, columns) - 1
    lanes = 128
    wide = feat_width + lanes
    heads = query_weight.shape[1] // HEAD_SIZE
    kv_heads = keyvalue_weight.shape[2] // HEAD_SIZE
    hbm = pl.BlockSpec(memory_space=pl.ANY)
    vmem = pl.BlockSpec(memory_space=pltpu.VMEM)
    bf16, f32 = jnp.bfloat16, jnp.float32
    dma = pltpu.SemaphoreType.DMA
    return pl.pallas_call(
        functools.partial(expert_kernel, rows, columns, owners, local, early),
        in_specs=[hbm, hbm] + [vmem] * 6 + [hbm] * 5,
        out_specs=[hbm, hbm, vmem] + [hbm] * 11,
        out_shape=[
            jax.ShapeDtypeStruct((owners, half, wide), bf16),
            jax.ShapeDtypeStruct((owners, half, feat_width), bf16),
            jax.ShapeDtypeStruct((half, lanes), f32),
            jax.ShapeDtypeStruct((rows, columns, local, 2, height, units), bf16),
            jax.ShapeDtypeStruct((columns - 1, early, rows, height, units), bf16),
            jax.ShapeDtypeStruct((rows - 1, early, columns, height, units), bf16),
            jax.ShapeDtypeStruct((local, owners, total, units), bf16),
            jax.ShapeDtypeStruct((local, owners, total, 2 * units), bf16),
            jax.ShapeDtypeStruct((total, feat_width), bf16),
            jax.ShapeDtypeStruct((heads, total, HEAD_SIZE), bf16),
            jax.ShapeDtypeStruct((kv_heads, total, HEAD_SIZE), bf16),
            jax.ShapeDtypeStruct((kv_heads, total, HEAD_SIZE), bf16),
            jax.ShapeDtypeStruct((total, heads * HEAD_SIZE), bf16),
            jax.ShapeDtypeStruct((half, feat_width), f32),
        ],
        scratch_shapes=[
            pltpu.VMEM((owners, total, feat_width), bf16),
            pltpu.VMEM((owners, total, wide), bf16),
            pltpu.VMEM((local, 2, feat_width, units), bf16),
            pltpu.VMEM((local, units, feat_width), bf16),
            pltpu.VMEM((lanes, feat_width), bf16),
            pltpu.VMEM((half, feat_width), bf16),
            pltpu.VMEM((half, feat_width), bf16),
            pltpu.VMEM((total, lanes), f32),
            pltpu.VMEM((half, wide), bf16),
            pltpu.VMEM((half, feat_width), bf16),
            pltpu.VMEM((owners, half, wide), bf16),
            pltpu.VMEM((owners, half, feat_width), bf16),
            dma((5,)),
            dma((6,)),
            dma((2,)),
            dma((2, local)),
            dma((2, owners - 1, 2)),
            dma((2, owners)),
            dma((2, owners)),
            dma((2, owners)),
            dma((2,)),
            dma((owners,)),
            dma((owners,)),
            dma((owners,)),
            dma((owners,)),
            dma((owners,)),
            dma((2, 2)),
            dma((2, most, early)),
            dma((2, most, early)),
            dma((2, 2)),
            dma((2,)),
        ],
        compiler_params=pltpu.CompilerParams(
            vmem_limit_bytes=62 * 2**20, collective_id=0, has_side_effects=True
        ),
        cost_estimate=pl.CostEstimate(
            flops=2 * owners * total * feat_width * units * 9 * local,
            bytes_accessed=80 * 2**20,
            transcendentals=owners * total * units * local,
        ),
    )(
        tokens,
        cot,
        routes,
        attn_gain,
        expert_gain,
        cosine,
        sine,
        router,
        query_weight,
        keyvalue_weight,
        out_weight,
        gateup,
        down,
    )


class Summing:
    def __init__(self, place, source, axes, order, landing, send, recv):
        self.place, self.order, self.landing = place, order, landing
        self.send, self.recv = send, recv
        self.sources, self.positions = [source], []
        left = list(axes)
        for step, axis in enumerate(order):
            self.positions.append(left.index(axis))
            left.pop(self.positions[-1])
            self.sources.append(landing[step].at[0])

    def copies(self, step):
        axis = self.order[step]
        found = []
        for shift in range(1, self.place.sizes[axis]):
            to = self.place.peer(axis, shift)
            found.append(
                pltpu.make_async_remote_copy(
                    src_ref=picked(self.sources[step], self.positions[step], to),
                    dst_ref=self.landing[step].at[shift - 1],
                    send_sem=self.send.at[step, shift - 1],
                    recv_sem=self.recv.at[step, shift - 1],
                    device_id=self.place.device(axis, to),
                    device_id_type=pl.DeviceIdType.MESH,
                )
            )
        return found

    def start(self, step):
        for copy in self.copies(step):
            copy.start()

    def total(self, step):
        axis = self.order[step]
        for copy in self.copies(step):
            copy.wait_recv()
        own = picked(self.sources[step], self.positions[step], self.place.at[axis])
        value = own[...].astype(jnp.float32)
        for shift in range(1, self.place.sizes[axis]):
            value = value + self.landing[step][shift - 1].astype(jnp.float32)
        return value

    def forward(self, step):
        self.landing[step][0] = self.total(step).astype(self.landing[step].dtype)
        self.start(step + 1)

    def close(self):
        for step in range(len(self.order)):
            for copy in self.copies(step):
                copy.wait_send()


def norm_grad(grad, gain, unit, inv_rms):
    grad_unit = grad * gain
    return inv_rms * (grad_unit - unit * jnp.mean(grad_unit * unit, axis=-1, keepdims=True))


def back_kernel(
    rows,
    columns,
    owners,
    parts_hbm,
    comb_hbm,
    grads_hbm,
    early_a,
    early_b,
    gates_ref,
    middle_hbm,
    cot_hbm,
    tokens_hbm,
    expert_gain_ref,
    attn_gain_ref,
    router_ref,
    out_weight_hbm,
    heads_hbm,
    query_hbm,
    key_hbm,
    value_hbm,
    normed_hbm,
    query_weight_hbm,
    keyvalue_weight_hbm,
    cosine_ref,
    sine_ref,
    mixed_hbm,
    tokens_grad_hbm,
    gateup_out,
    down_out,
    query_out,
    keyvalue_out,
    output_out,
    router_out,
    expert_gain_out,
    attn_gain_out,
    own_a,
    own_b,
    first_a,
    first_b,
    second_a,
    second_b,
    comb_own,
    comb_left,
    comb_right,
    out_a,
    out_az,
    out_ax,
    out_ay,
    out_b,
    out_by,
    out_bx,
    out_bz,
    near_q,
    near_qx,
    near_qy,
    near_qz,
    near_kv,
    near_kvy,
    near_kvx,
    near_kvz,
    far_q,
    far_qy,
    far_qx,
    far_qz,
    far_kv,
    far_kvx,
    far_kvy,
    far_kvz,
    small_sum,
    small_swap,
    small_stage,
    small_z,
    small_x,
    small_y,
    grad_attn,
    grad_middle,
    grad_query,
    grad_keyvalue,
    half_send,
    half_land,
    mixed_stage,
    load_sem,
    own_sem,
    early_sem,
    first_send,
    first_recv,
    second_send,
    second_recv,
    comb_sem,
    comb_send,
    comb_recv,
    sum_send,
    sum_recv,
    swap_send,
    swap_recv,
    store_sem,
):
    place = Place(rows, columns, owners)
    core = lax.axis_index("tensor")
    sibling = {"tensor": 1 - core}
    half, feat_width = middle_hbm.shape
    local = grads_hbm.shape[2]
    width = gateup_out.shape[2]
    lanes = gates_ref.shape[1]
    early = early_a.shape[1]
    heads, length, head_size = query_hbm.shape
    kv_heads = key_hbm.shape[0]
    groups = heads // kv_heads
    query_width = heads * head_size
    key_width = kv_heads * head_size
    tile = 64
    mine = pl.ds(pl.multiple_of(core * half, half), half)
    others = pl.ds(pl.multiple_of((1 - core) * half, half), half)

    barrier = pltpu.get_barrier_semaphore()
    peers = [sibling]
    for axis in ("x", "y", "z"):
        for shift in range(1, place.sizes[axis]):
            peers.append(place.device(axis, place.peer(axis, shift)))
    for peer in peers:
        pl.semaphore_signal(barrier, inc=1, device_id=peer, device_id_type=pl.DeviceIdType.MESH)
    pl.semaphore_wait(barrier, len(peers))

    def to_sibling(src, dst, at):
        return pltpu.make_async_remote_copy(
            src_ref=src,
            dst_ref=dst,
            send_sem=swap_send.at[at],
            recv_sem=swap_recv.at[at],
            device_id=sibling,
            device_id_type=pl.DeviceIdType.MESH,
        )

    plans = (
        (0, "x", "y", own_a, first_a, second_a),
        (1, "y", "x", own_b, first_b, second_b),
    )

    def grads_of(part, axis, index, expert):
        if axis == "x":
            return grads_hbm.at[:, index, expert, part]
        return grads_hbm.at[index, :, expert, part]

    def own_load(plan, expert):
        part, axis, _, own, _, _ = plan
        return pltpu.make_async_copy(
            grads_of(part, axis, place.at[axis], expert),
            own.at[expert % 2],
            own_sem.at[part, expert],
        )

    def early_load(plan, expert):
        part, _, _, _, first, _ = plan
        source = (early_a, early_b)[part]
        return pltpu.make_async_copy(
            source.at[:, expert], first.at[:, expert], early_sem.at[part, expert]
        )

    def first_copies(plan, expert):
        part, axis, _, _, first, _ = plan
        found = []
        for shift in range(1, place.sizes[axis]):
            to = place.peer(axis, shift)
            found.append(
                pltpu.make_async_remote_copy(
                    src_ref=grads_of(part, axis, to, expert),
                    dst_ref=first.at[shift - 1, expert],
                    send_sem=first_send.at[part, shift - 1, expert],
                    recv_sem=first_recv.at[part, shift - 1, expert],
                    device_id=place.device(axis, to),
                    device_id_type=pl.DeviceIdType.MESH,
                )
            )
        return found

    def second_copies(plan, expert):
        part, _, axis, _, first, second = plan
        found = []
        for shift in range(1, place.sizes[axis]):
            to = place.peer(axis, shift)
            found.append(
                pltpu.make_async_remote_copy(
                    src_ref=first.at[0, expert, to],
                    dst_ref=second.at[shift - 1, expert],
                    send_sem=second_send.at[part, shift - 1, expert],
                    recv_sem=second_recv.at[part, shift - 1, expert],
                    device_id=place.device(axis, to),
                    device_id_type=pl.DeviceIdType.MESH,
                )
            )
        return found

    def first_sum(expert):
        for plan in plans:
            _, axis, after, own, first, _ = plan
            own_load(plan, expert).wait()

            @pl.when(expert < early)
            def _():
                early_load(plan, expert).wait()

            @pl.when(expert >= early)
            def _():
                for copy in first_copies(plan, expert):
                    copy.wait_recv()

            for index in range(place.sizes[after]):
                value = own[expert % 2, index].astype(jnp.float32)
                for shift in range(1, place.sizes[axis]):
                    value = value + first[shift - 1, expert, index].astype(jnp.float32)
                first[0, expert, index] = value.astype(first.dtype)

            @pl.when(expert + 2 < local)
            def _():
                own_load(plan, expert + 2).start()

    def second_sum(expert):
        turned = []
        for plan in plans:
            part, _, axis, _, first, second = plan
            for copy in second_copies(plan, expert):
                copy.wait_recv()
            value = first[0, expert, place.at[axis]].astype(jnp.float32)
            for shift in range(1, place.sizes[axis]):
                value = value + second[shift - 1, expert].astype(jnp.float32)
            gateup_out[expert, part] = value[:width]
            turned.append(value[width:])
        down_out[expert] = jnp.concatenate(turned, axis=0).T

    def start_first(expert, carry):
        for plan in plans:
            for copy in first_copies(plan, expert):
                copy.start()
        return carry

    held = local - 1
    lax.fori_loop(early, held, start_first, 0)
    for plan in plans:
        for expert in range(early):
            early_load(plan, expert).start()
        for expert in range(min(2, local)):
            own_load(plan, expert).start()

    me = place.at["z"]

    def comb_load(shift):
        return pltpu.make_async_copy(comb_hbm.at[shift], comb_own.at[shift], comb_sem.at[shift])

    def comb_copy(side, away):
        landing, at = (comb_right, 0) if side == 1 else (comb_left, 1)
        shift = away if side == 1 else owners - away
        to = jnp.clip(me + side, 0, owners - 1)
        return pltpu.make_async_remote_copy(
            src_ref=comb_own.at[shift],
            dst_ref=landing.at[away - 1],
            send_sem=comb_send.at[at, away],
            recv_sem=comb_recv.at[at, away - 1],
            device_id=place.device("z", to),
            device_id_type=pl.DeviceIdType.MESH,
        )

    def comb_arrival(side, away):
        landing, at = (comb_right, 0) if side == 1 else (comb_left, 1)
        from_ = jnp.clip(me - side, 0, owners - 1)
        return pltpu.make_async_remote_copy(
            src_ref=comb_own.at[0],
            dst_ref=landing.at[away],
            send_sem=comb_send.at[at, away],
            recv_sem=comb_recv.at[at, away],
            device_id=place.device("z", from_),
            device_id_type=pl.DeviceIdType.MESH,
        )

    def inside(at):
        return (at >= 0) & (at < owners)

    def comb_send_on(away):
        for side in (1, -1):

            @pl.when(inside(me + side * away))
            def _():
                comb_copy(side, away).start()

    def comb_add(away):
        for side in (1, -1):

            @pl.when(inside(me + side * away) & inside(me - side))
            def _():
                comb_arrival(side, away).wait_recv()
                landing = comb_right if side == 1 else comb_left
                shift = 0 if away == 0 else (away if side == 1 else owners - away)
                comb_own[shift] = (
                    comb_own[shift].astype(jnp.float32) + landing[away].astype(jnp.float32)
                ).astype(jnp.bfloat16)

    for shift in range(owners):
        comb_load(shift).start()
    for shift in range(owners):
        comb_load(shift).wait()
    comb_send_on(owners - 1)

    def comb_stage(away):
        comb_add(away)
        if away > 0:
            comb_send_on(away)

    def job(source, order, landing, at):
        return Summing(
            place, source, ("y", "x", "z"), order, landing, sum_send.at[at], sum_recv.at[at]
        )

    output_job_a = job(out_a, ("z", "x", "y"), (out_az, out_ax, out_ay), 0)
    output_job_b = job(out_b, ("y", "x", "z"), (out_by, out_bx, out_bz), 4)
    pair_jobs = (
        (
            job(near_q, ("x", "y", "z"), (near_qx, near_qy, near_qz), 1),
            job(near_kv, ("y", "x", "z"), (near_kvy, near_kvx, near_kvz), 2),
        ),
        (
            job(far_q, ("y", "x", "z"), (far_qy, far_qx, far_qz), 5),
            job(far_kv, ("x", "y", "z"), (far_kvx, far_kvy, far_kvz), 6),
        ),
    )
    pair_stages = ((near_q, near_kv), (far_q, far_kv))
    small_job = job(small_stage, ("z", "x", "y"), (small_z, small_x, small_y), 3)

    def weight_grad(stage, left, right):
        count = stage.shape[3]
        band = feat_width // 4
        for start in range(0, feat_width, band):
            value = contract(left[:, start : start + band], right, 0, 0).astype(jnp.bfloat16)
            for at in range(start, start + band, count):
                index = at // count
                y, x, z = (
                    index // (columns * owners),
                    index // owners % columns,
                    index % owners,
                )
                stage[y, x, z] = value[at - start : at - start + count]

    def middle_phase(parts, middle, cot_ref):
        loads = (
            pltpu.make_async_copy(cot_hbm.at[mine], cot_ref, load_sem.at[3]),
            pltpu.make_async_copy(parts_hbm, parts, load_sem.at[1]),
            pltpu.make_async_copy(middle_hbm, middle, load_sem.at[2]),
        )
        for copy in loads:
            copy.start()
        for copy in loads:
            copy.wait()
        small_sum[...] = jnp.zeros_like(small_sum)

        def body(step, carry):
            at = pl.ds(pl.multiple_of(step * tile, tile), tile)
            grad = sum(parts[b, at, :feat_width].astype(jnp.float32) for b in range(owners))
            dots = sum(parts[b, at, feat_width:].astype(jnp.float32) for b in range(owners))
            lower = lanes // 2
            dots = dots + jnp.concatenate([dots[:, lower:], dots[:, :lower]], axis=1)
            gates = gates_ref[at]
            grad_gate = RESIDUAL * dots
            grad_logits = (
                gates * (grad_gate - jnp.sum(gates * grad_gate, axis=-1, keepdims=True))
            ).astype(jnp.bfloat16)
            grad = grad + contract(
                grad_logits[:, : router_ref.shape[0]], router_ref[...], 1, 0
            )
            unit, inv_rms = norm_parts(middle[at])
            expert_in = (unit * expert_gain_ref[...]).astype(jnp.bfloat16)
            after = cot_ref[at].astype(jnp.float32) + norm_grad(
                grad, expert_gain_ref[...], unit, inv_rms
            )
            grad_middle[at] = after
            to = pl.ds(pl.multiple_of(core * half + step * tile, tile), tile)
            grad_attn[to] = (RESIDUAL * after).astype(jnp.bfloat16)
            count = small_sum.shape[0]
            small_sum[...] += contract(grad_logits, expert_in, 0, 0)[:count]
            small_sum[count - 2 : count - 1] += jnp.sum(grad * unit, axis=0, keepdims=True)
            return carry

        lax.fori_loop(0, half // tile, body, 0)

    pl.run_scoped(
        middle_phase,
        pltpu.VMEM(parts_hbm.shape, parts_hbm.dtype),
        pltpu.VMEM(middle_hbm.shape, middle_hbm.dtype),
        pltpu.VMEM(middle_hbm.shape, cot_hbm.dtype),
    )
    attn_swap = to_sibling(grad_attn.at[mine], grad_attn.at[mine], 0)
    attn_swap.start()
    to_sibling(grad_attn.at[others], grad_attn.at[others], 0).wait_recv()

    comb_stage(owners - 2)
    causal = length // 2

    def attention_phase(
        out_weight_ref, heads_ref, query_ref, key_ref, value_ref, key_sum, value_sum, normed_ref
    ):
        load_normed = pltpu.make_async_copy(normed_hbm, normed_ref, load_sem.at[0])
        loads = (
            pltpu.make_async_copy(heads_hbm, heads_ref, load_sem.at[4]),
            pltpu.make_async_copy(out_weight_hbm, out_weight_ref, load_sem.at[5]),
            pltpu.make_async_copy(query_hbm, query_ref, load_sem.at[6]),
            pltpu.make_async_copy(key_hbm, key_ref, load_sem.at[7]),
            pltpu.make_async_copy(value_hbm, value_ref, load_sem.at[8]),
        )
        for copy in loads:
            copy.start()
        load_normed.start()
        loads[0].wait()
        cut = heads_ref.shape[1] // 2
        weight_grad(out_a, grad_attn, heads_ref[:, :cut])
        output_job_a.start(0)
        weight_grad(out_b, grad_attn, heads_ref[:, cut:])
        output_job_b.start(0)
        for copy in loads[1:]:
            copy.wait()

        def turned_back(grads):
            swapped = jnp.concatenate(
                [grads[:, head_size // 2 :], grads[:, : head_size // 2]], axis=1
            )
            return (grads * cosine_ref[...] + swapped * sine_ref[...]).astype(jnp.bfloat16)

        def body(group, carry):
            grad_heads = contract(grad_attn[...], out_weight_ref[group], 1, 1).astype(jnp.bfloat16)
            keys, values = key_ref[group], value_ref[group]
            key_sum[...] = jnp.zeros_like(key_sum)
            value_sum[...] = jnp.zeros_like(value_sum)
            turned = []
            for member in range(groups):
                query = query_ref[group * groups + member]
                grad_head = grad_heads[:, member * head_size : (member + 1) * head_size]
                pieces = []
                for start in (0, causal):
                    stop = start + causal
                    some_q, some_g = query[start:stop], grad_head[start:stop]
                    some_k, some_v = keys[:stop], values[:stop]
                    scores = contract(some_q, some_k, 1, 1) * ATTN_SCALE
                    row = start + lax.broadcasted_iota(jnp.int32, scores.shape, 0)
                    col = lax.broadcasted_iota(jnp.int32, scores.shape, 1)
                    scores = jnp.where(row >= col, scores, NEGATIVE)
                    raised = jnp.exp(scores - jnp.max(scores, axis=1, keepdims=True))
                    probs = raised / jnp.sum(raised, axis=1, keepdims=True)
                    grad_probs = contract(some_g, some_v, 1, 1)
                    value_sum[:stop] += contract(probs.astype(jnp.bfloat16), some_g, 0, 0)
                    grad_scores = (
                        probs
                        * (grad_probs - jnp.sum(probs * grad_probs, axis=1, keepdims=True))
                    ).astype(jnp.bfloat16)
                    pieces.append(
                        jnp.dot(grad_scores, some_k, preferred_element_type=jnp.float32)
                    )
                    key_sum[:stop] += contract(grad_scores, some_q, 0, 0)
                turned.append(turned_back(ATTN_SCALE * jnp.concatenate(pieces, axis=0)))
            grad_query[group] = jnp.concatenate(turned, axis=1)
            grad_keyvalue[0, group] = turned_back(ATTN_SCALE * key_sum[...])
            grad_keyvalue[1, group] = value_sum[...].astype(jnp.bfloat16)

            @pl.when(group < local)
            def _():
                first_sum(group)

            return carry

        pairs = kv_heads // 2
        for pair, (jobs, stages) in enumerate(zip(pair_jobs, pair_stages)):
            chosen = range(pair * pairs, (pair + 1) * pairs)
            lax.fori_loop(chosen[0], chosen[-1] + 1, body, 0)
            queries = jnp.concatenate([grad_query[g] for g in chosen], axis=1)
            keyvalue = jnp.concatenate(
                [grad_keyvalue[what, g] for what in range(2) for g in chosen], axis=1
            )
            if pair == 0:
                load_normed.wait()
            weight_grad(stages[0], normed_ref, queries)
            jobs[0].start(0)
            weight_grad(stages[1], normed_ref, keyvalue)
            jobs[1].start(0)
            if pair == 0:
                lax.fori_loop(held, local, start_first, 0)

    pl.run_scoped(
        attention_phase,
        pltpu.VMEM(out_weight_hbm.shape, out_weight_hbm.dtype),
        pltpu.VMEM(heads_hbm.shape, heads_hbm.dtype),
        pltpu.VMEM(query_hbm.shape, query_hbm.dtype),
        pltpu.VMEM(key_hbm.shape, key_hbm.dtype),
        pltpu.VMEM(value_hbm.shape, value_hbm.dtype),
        pltpu.VMEM((length, head_size), jnp.float32),
        pltpu.VMEM((length, head_size), jnp.float32),
        pltpu.VMEM(normed_hbm.shape, normed_hbm.dtype),
    )
    def start_second(expert, carry):
        for plan in plans:
            for copy in second_copies(plan, expert):
                copy.start()
        return carry

    for away in range(owners - 3, 0, -1):
        comb_stage(away)

    def tokens_phase(query_weight, keyvalue_weight, grad_normed, tokens_ref):
        loads = (
            pltpu.make_async_copy(tokens_hbm.at[mine], tokens_ref, load_sem.at[3]),
            pltpu.make_async_copy(query_weight_hbm, query_weight, load_sem.at[1]),
            pltpu.make_async_copy(keyvalue_weight_hbm, keyvalue_weight, load_sem.at[2]),
        )
        for copy in loads:
            copy.start()
        queries = jnp.concatenate([grad_query[g] for g in range(kv_heads)], axis=1)
        keyvalue = [
            jnp.concatenate([grad_keyvalue[what, g] for g in range(kv_heads)], axis=1)
            for what in range(2)
        ]
        for copy in loads:
            copy.wait()
        grad_normed[...] = (
            contract(queries, query_weight[...], 1, 1)
            + contract(keyvalue[0], keyvalue_weight[0], 1, 1)
            + contract(keyvalue[1], keyvalue_weight[1], 1, 1)
        )
        half_send[...] = grad_normed[others].astype(jnp.bfloat16)
        swap = to_sibling(half_send, half_land, 1)
        swap.start()
        swap.wait_recv()

        def body(step, carry):
            at = pl.ds(pl.multiple_of(step * tile, tile), tile)
            to = pl.ds(pl.multiple_of(core * half + step * tile, tile), tile)
            grad = grad_normed[to] + half_land[at].astype(jnp.float32)
            unit, inv_rms = norm_parts(tokens_ref[at].astype(jnp.float32))
            grad_middle[at] += norm_grad(grad, attn_gain_ref[...], unit, inv_rms)
            count = small_sum.shape[0]
            small_sum[count - 1 : count] += jnp.sum(grad * unit, axis=0, keepdims=True)
            return carry

        lax.fori_loop(0, half // tile, body, 0)

    pl.run_scoped(
        tokens_phase,
        pltpu.VMEM(query_weight_hbm.shape, query_weight_hbm.dtype),
        pltpu.VMEM(keyvalue_weight_hbm.shape, keyvalue_weight_hbm.dtype),
        pltpu.VMEM((2 * half, feat_width), jnp.float32),
        pltpu.VMEM((half, feat_width), tokens_hbm.dtype),
    )
    tokens_store = pltpu.make_async_copy(grad_middle, tokens_grad_hbm.at[mine], store_sem.at[0])
    tokens_store.start()
    tokens_swap = to_sibling(grad_middle, tokens_grad_hbm.at[mine], 2)
    tokens_swap.start()
    small_exchange = to_sibling(small_sum, small_swap, 3)
    small_exchange.start()

    small_exchange.wait()
    small_sum[...] += small_swap[...]
    piece = feat_width // (rows * columns * owners)
    small_stage[...] = jnp.zeros_like(small_stage)
    for y in range(rows):
        for x in range(columns):
            for z in range(owners):
                at = ((y * columns + x) * owners + z) * piece
                small_stage[y, x, z, :, :piece] = small_sum[:, at : at + piece]
    small_job.start(0)

    for which in pair_jobs[0]:
        which.forward(0)
    output_job_b.forward(0)
    for expert in range(kv_heads, local):
        first_sum(expert)
    for which in pair_jobs[1]:
        which.forward(0)
    lax.fori_loop(0, local, start_second, 0)
    output_job_a.forward(0)
    for which in pair_jobs[0]:
        which.forward(1)
    output_job_b.forward(1)
    for which in pair_jobs[1]:
        which.forward(1)
    output_job_a.forward(1)
    small_job.forward(0)
    small_job.forward(1)

    def mixed_phase(middle):
        load = pltpu.make_async_copy(middle_hbm, middle, load_sem.at[1])
        load.start()
        comb_stage(0)
        load.wait()

        def body(step, carry):
            at = pl.ds(pl.multiple_of(step * tile, tile), tile)
            comb = comb_own[0, at].astype(jnp.float32)
            mixed_stage[at] = (middle[at] + RESIDUAL * comb).astype(jnp.bfloat16)
            return carry

        lax.fori_loop(0, half // tile, body, 0)

    pl.run_scoped(mixed_phase, pltpu.VMEM(middle_hbm.shape, middle_hbm.dtype))
    mixed_store = pltpu.make_async_copy(mixed_stage, mixed_hbm.at[mine], store_sem.at[1])
    mixed_store.start()
    mixed_swap = to_sibling(mixed_stage, mixed_hbm.at[mine], 4)
    mixed_swap.start()

    cut = out_a.shape[4]
    output_out[:, :cut] = output_job_a.total(2)
    output_out[:, cut:] = output_job_b.total(2)
    small = small_job.total(2)
    count = small.shape[0]
    router_out[...] = small[: router_out.shape[0], :piece]
    expert_gain_out[...] = small[count - 2 : count - 1, :piece]
    attn_gain_out[...] = small[count - 1 :, :piece]
    for pair, jobs in enumerate(pair_jobs):
        cut = near_q.shape[4]
        query_out[:, pair * cut : (pair + 1) * cut] = jobs[0].total(2)
        value = jobs[1].total(2)
        cut = near_kv.shape[4] // 2
        for what in range(2):
            keyvalue_out[what, :, pair * cut : (pair + 1) * cut] = value[
                :, what * cut : (what + 1) * cut
            ]

    def finish(expert, carry):
        second_sum(expert)
        return carry

    lax.fori_loop(0, local, finish, 0)

    def close(expert, carry):
        for plan in plans:

            @pl.when(expert >= early)
            def _():
                for copy in first_copies(plan, expert):
                    copy.wait_send()

            for copy in second_copies(plan, expert):
                copy.wait_send()
        return carry

    lax.fori_loop(0, local, close, 0)
    for away in range(1, owners):
        for side in (1, -1):

            @pl.when(inside(me + side * away))
            def _():
                comb_copy(side, away).wait_send()

    for which in (output_job_a, output_job_b, small_job) + pair_jobs[0] + pair_jobs[1]:
        which.close()
    attn_swap.wait_send()
    to_sibling(half_send, half_land, 1).wait_send()
    tokens_store.wait()
    mixed_store.wait()
    tokens_swap.wait_send()
    mixed_swap.wait_send()
    to_sibling(grad_middle, tokens_grad_hbm.at[others], 2).wait_recv()
    to_sibling(mixed_stage, mixed_hbm.at[others], 4).wait_recv()


def backward(
    parts,
    combs,
    grads,
    early_a,
    early_b,
    gates,
    middle,
    cot,
    tokens,
    expert_gain,
    attn_gain,
    router,
    out_weight,
    heads_out,
    query,
    keys,
    values,
    normed,
    query_weight,
    keyvalue_weight,
    cosine,
    sine,
):
    owners = lax.axis_size("expert")
    chunks = lax.axis_size("dp")
    rows, columns = factors(chunks)
    half, feat_width = middle.shape
    local, _, height, units = grads.shape[2:]
    width = feat_width // chunks
    early = early_a.shape[1]
    piece = feat_width // (chunks * owners)
    heads, length, head_size = query.shape
    kv_heads = keys.shape[0]
    query_width, key_width = heads * head_size, kv_heads * head_size
    lanes = gates.shape[1]
    count = 24
    out_weight = out_weight.reshape(kv_heads, query_width // kv_heads, feat_width)
    bf16, f32 = jnp.bfloat16, jnp.float32
    hbm = pl.BlockSpec(memory_space=pl.ANY)
    vmem = pl.BlockSpec(memory_space=pltpu.VMEM)
    dma = pltpu.SemaphoreType.DMA
    most = max(rows, columns, owners) - 1

    def landings(tail, order, dtype):
        sizes = {"y": rows, "x": columns, "z": owners}
        left = ["y", "x", "z"]
        found = []
        for axis in order:
            left.remove(axis)
            found.append(
                pltpu.VMEM((sizes[axis] - 1,) + tuple(sizes[a] for a in left) + tail, dtype)
            )
        return found

    whole = (rows, columns, owners)
    return pl.pallas_call(
        functools.partial(back_kernel, rows, columns, owners),
        in_specs=[hbm] * 5 + [vmem] + [hbm] * 3 + [vmem] * 3 + [hbm] * 8 + [vmem, vmem],
        out_specs=[hbm, hbm] + [vmem] * 8,
        out_shape=[
            jax.ShapeDtypeStruct((2 * half, feat_width), bf16),
            jax.ShapeDtypeStruct((2 * half, feat_width), f32),
            jax.ShapeDtypeStruct((local, 2, width, units), f32),
            jax.ShapeDtypeStruct((local, units, width), f32),
            jax.ShapeDtypeStruct((piece, query_width), f32),
            jax.ShapeDtypeStruct((2, piece, key_width), f32),
            jax.ShapeDtypeStruct((piece, query_width), f32),
            jax.ShapeDtypeStruct((router.shape[0], piece), f32),
            jax.ShapeDtypeStruct((1, piece), f32),
            jax.ShapeDtypeStruct((1, piece), f32),
        ],
        scratch_shapes=[
            pltpu.VMEM((2, rows, height, units), bf16),
            pltpu.VMEM((2, columns, height, units), bf16),
            pltpu.VMEM((columns - 1, local, rows, height, units), bf16),
            pltpu.VMEM((rows - 1, local, columns, height, units), bf16),
            pltpu.VMEM((rows - 1, local, height, units), bf16),
            pltpu.VMEM((columns - 1, local, height, units), bf16),
            pltpu.VMEM((owners, half, feat_width), bf16),
            pltpu.VMEM((owners - 1, half, feat_width), bf16),
            pltpu.VMEM((owners - 1, half, feat_width), bf16),
            pltpu.VMEM(whole + (piece, query_width // 2), bf16),
            *landings((piece, query_width // 2), "zxy", bf16),
            pltpu.VMEM(whole + (piece, query_width // 2), bf16),
            *landings((piece, query_width // 2), "yxz", bf16),
            pltpu.VMEM(whole + (piece, query_width // 2), bf16),
            *landings((piece, query_width // 2), "xyz", bf16),
            pltpu.VMEM(whole + (piece, key_width), bf16),
            *landings((piece, key_width), "yxz", bf16),
            pltpu.VMEM(whole + (piece, query_width // 2), bf16),
            *landings((piece, query_width // 2), "yxz", bf16),
            pltpu.VMEM(whole + (piece, key_width), bf16),
            *landings((piece, key_width), "xyz", bf16),
            pltpu.VMEM((count, feat_width), f32),
            pltpu.VMEM((count, feat_width), f32),
            pltpu.VMEM(whole + (count, lanes), f32),
            *landings((count, lanes), "zxy", f32),
            pltpu.VMEM((2 * half, feat_width), bf16),
            pltpu.VMEM((half, feat_width), f32),
            pltpu.VMEM((kv_heads, length, query_width // kv_heads), bf16),
            pltpu.VMEM((2, kv_heads, length, head_size), bf16),
            pltpu.VMEM((half, feat_width), bf16),
            pltpu.VMEM((half, feat_width), bf16),
            pltpu.VMEM((half, feat_width), bf16),
            dma((9,)),
            dma((2, local)),
            dma((2, early)),
            dma((2, most, local)),
            dma((2, most, local)),
            dma((2, most, local)),
            dma((2, most, local)),
            dma((owners,)),
            dma((2, owners)),
            dma((2, owners)),
            dma((7, 3, most)),
            dma((7, 3, most)),
            dma((5,)),
            dma((5,)),
            dma((2,)),
        ],
        compiler_params=pltpu.CompilerParams(
            vmem_limit_bytes=60 * 2**20, collective_id=1, has_side_effects=True
        ),
        cost_estimate=pl.CostEstimate(
            flops=12 * 2**30, bytes_accessed=60 * 2**20, transcendentals=heads * length * length
        ),
    )(
        parts,
        combs,
        grads,
        early_a,
        early_b,
        gates,
        middle,
        cot,
        tokens,
        expert_gain,
        attn_gain,
        router,
        out_weight,
        heads_out,
        query,
        keys,
        values,
        normed,
        query_weight,
        keyvalue_weight,
        cosine,
        sine,
    )


def per_device(
    tokens,
    out_grad,
    attn_gain,
    query_weight,
    key_value_weight,
    output_weight,
    expert_gain,
    router_weight,
    gateup_weight,
    down_weight,
    routes,
):
    cosine, sine = rotary_tables()
    parts, combs, gates, grads, early_a, early_b, _, _, normed, *kept = experts(
        tokens,
        out_grad,
        routes.T,
        attn_gain[None],
        expert_gain[None],
        cosine,
        sine,
        router_weight.T,
        query_weight,
        key_value_weight,
        output_weight,
        gateup_weight,
        down_weight,
    )
    query, keys, values, heads_out, middle = kept
    (
        mixed,
        tokens_grad,
        gateup_total,
        down_total,
        query_total,
        keyvalue_total,
        output_total,
        router_total,
        expert_gain_total,
        attn_gain_total,
    ) = backward(
        parts,
        combs,
        grads,
        early_a,
        early_b,
        gates,
        middle,
        out_grad,
        tokens,
        expert_gain[None],
        attn_gain[None],
        router_weight.T,
        output_weight,
        heads_out,
        query,
        keys,
        values,
        normed,
        query_weight,
        key_value_weight,
        cosine,
        sine,
    )
    return (
        mixed,
        tokens_grad,
        attn_gain_total[0],
        query_total,
        keyvalue_total,
        output_total.T,
        expert_gain_total[0],
        router_total.T,
        gateup_total,
        down_total,
    )


def solution(mesh):
    placed = (
        P(("dp", "expert"), None),
        P(("dp", "expert"), None),
        P(),
        P(None, "tensor"),
        P(None, None, "tensor"),
        P("tensor", None),
        P(),
        P(),
        P("expert", None, None, "tensor"),
        P("expert", "tensor", None),
        P(("dp", "expert"), None),
    )
    return jax.shard_map(
        per_device,
        mesh=mesh,
        in_specs=placed,
        out_specs=(
            P(("dp", "expert"), None),
            P(("dp", "expert"), None),
            P(("dp", "expert")),
            P(("dp", "expert"), "tensor"),
            P(None, ("dp", "expert"), "tensor"),
            P("tensor", ("dp", "expert")),
            P(("dp", "expert")),
            P(("dp", "expert"), None),
            P("expert", None, "dp", "tensor"),
            P("expert", "tensor", "dp"),
        ),
        check_vma=False,
    )
```

```python
import functools

import jax
import jax.numpy as jnp
import numpy as np
from jax import lax
from jax.experimental import pallas as pl
from jax.experimental.pallas import tpu as pltpu
from jax.sharding import PartitionSpec as P

HEAD_SIZE = 64
TOPK = 8
SEQUENCE_LENGTH = 512


EPSILON = 1e-06
RESIDUAL = 0.22
ATTN_SCALE = 0.015625
ROPE_BASE = 10000.0
NEGATIVE = -1e30
COT_STEPS = {1: (2,)}
EARLY = 2


def rotary_tables():
    half_dim = HEAD_SIZE // 2
    frequency = ROPE_BASE ** (-np.arange(half_dim, dtype=np.float32) * 2.0 / HEAD_SIZE)
    angles = np.arange(SEQUENCE_LENGTH, dtype=np.float32)[:, None] * frequency[None, :]
    angles = angles.astype(np.float32)
    cosine, sine = np.cos(angles), np.sin(angles)
    return (
        jnp.asarray(np.concatenate([cosine, cosine], axis=1), jnp.float32),
        jnp.asarray(np.concatenate([sine, -sine], axis=1), jnp.float32),
    )


def norm_parts(values):
    inv_rms = lax.rsqrt(jnp.mean(values * values, axis=-1, keepdims=True) + EPSILON)
    return values * inv_rms, inv_rms


def factors(count):
    low = 1 << ((count.bit_length() - 1) // 2)
    return count // low, low


class Place:
    def __init__(self, rows, columns, owners):
        self.sizes = {"y": rows, "x": columns, "z": owners}
        index = lax.axis_index("dp")
        self.at = {"y": index // columns, "x": index % columns, "z": lax.axis_index("expert")}

    def peer(self, axis, shift):
        return lax.rem(self.at[axis] + shift, self.sizes[axis])

    def device(self, axis, to):
        if axis == "z":
            return {"expert": to}
        if axis == "x":
            return {"dp": self.at["y"] * self.sizes["x"] + to}
        return {"dp": to * self.sizes["x"] + self.at["x"]}


def picked(ref, position, index):
    return ref.at[(slice(None),) * position + (index,)]


def contract(left, right, left_dim, right_dim):
    return lax.dot_general(
        left, right, (((left_dim,), (right_dim,)), ((), ())), preferred_element_type=jnp.float32
    )


def block_order(me, count, turn):
    block, unit = 0, 1
    while unit < count:
        block = block + unit * ((me // unit + turn // unit) % 2)
        unit *= 2
    return block


def expert_kernel(
    rows,
    columns,
    owners,
    local,
    early,
    tokens_hbm,
    cot_hbm,
    routes_ref,
    gains_ref,
    cosine_ref,
    sine_ref,
    router_ref,
    query_weight_hbm,
    keyvalue_weight_hbm,
    out_weight_hbm,
    gateup_hbm,
    down_hbm,
    parts_hbm,
    dots_hbm,
    comb_hbm,
    gates_out,
    grads_hbm,
    early_a,
    early_b,
    act_hbm,
    hidden_hbm,
    normed_hbm,
    query_hbm,
    key_hbm,
    value_hbm,
    heads_hbm,
    middle_hbm,
    rows_all,
    cot_all,
    hits_all,
    gateup_ref,
    down_ref,
    router_wide,
    half_send,
    half_land,
    gates_ref,
    send_grad,
    send_comb,
    send_dots,
    recv_grad,
    recv_comb,
    recv_dots,
    relay,
    load_sem,
    keep_sem,
    half_sem,
    weight_sem,
    chain_send,
    chain_recv,
    swap_send,
    swap_recv,
    sums_send,
    grad_recv,
    comb_recv,
    dots_recv,
    back_send,
    back_recv,
    dots_send,
    dots_back,
    hits_send,
    hits_recv,
    relay_sem,
    comb_sem,
    stage_sem,
    early_send,
    early_recv,
    dots_sem,
    grads_sem,
):
    place = Place(rows, columns, owners)
    me = lax.axis_index("expert")
    core = lax.axis_index("tensor")
    sibling = {"tensor": 1 - core}
    total, feat_width = rows_all.shape[1], rows_all.shape[2]
    half = total // 2
    units = down_ref.shape[0] // local
    lanes = gates_ref.shape[1]
    mine = pl.ds(pl.multiple_of(core * half, half), half)
    others = pl.ds(pl.multiple_of((1 - core) * half, half), half)

    barrier = pltpu.get_barrier_semaphore()
    pl.semaphore_signal(barrier, inc=1, device_id=sibling, device_id_type=pl.DeviceIdType.MESH)
    peers = 1
    for axis in ("x", "y", "z"):
        for shift in range(1, place.sizes[axis]):
            pl.semaphore_signal(
                barrier,
                inc=1,
                device_id=place.device(axis, place.peer(axis, shift)),
                device_id_type=pl.DeviceIdType.MESH,
            )
            peers += 1

    def remote(src, dst, send, recv, device):
        return pltpu.make_async_remote_copy(
            src_ref=src,
            dst_ref=dst,
            send_sem=send,
            recv_sem=recv,
            device_id=device,
            device_id_type=pl.DeviceIdType.MESH,
        )

    own_cot = pltpu.make_async_copy(cot_hbm, cot_all.at[me], load_sem.at[0])
    own_cot.start()
    number_of = lax.broadcasted_iota(jnp.int32, (lanes, total), 0)
    hits = number_of == routes_ref[0:1]
    for pick in range(1, routes_ref.shape[0]):
        hits = hits | (number_of == routes_ref[pick : pick + 1])
    hits_all[me] = jnp.where(hits, 1.0, 0.0).astype(jnp.bfloat16)
    experts_named = router_ref.shape[0]
    router_wide[...] = jnp.concatenate(
        [
            router_ref[...].astype(jnp.float32),
            jnp.zeros((lanes - experts_named, feat_width), jnp.float32),
        ],
        axis=0,
    ).astype(jnp.bfloat16)

    buffers = (rows_all, cot_all)

    def hits_copy(shift):
        return remote(
            hits_all.at[me],
            hits_all.at[me],
            hits_send.at[shift - 1],
            hits_recv.at[me],
            place.device("z", place.peer("z", shift)),
        )

    def hits_arrival(block):
        return remote(
            hits_all.at[block],
            hits_all.at[block],
            hits_send.at[0],
            hits_recv.at[block],
            sibling,
        )

    def chain(step, what, side):
        block = me - side * (step - 1)
        to = me + side
        there = (block >= 0) & (block < owners) & (to >= 0) & (to < owners)
        safe = jnp.clip(block, 0, owners - 1)
        at = 0 if side == 1 else 1
        copy = remote(
            buffers[what].at[safe, mine],
            buffers[what].at[safe, mine],
            chain_send.at[what, step - 1, at],
            chain_recv.at[what, safe],
            {"expert": jnp.clip(to, 0, owners - 1)},
        )
        return there, copy

    def swap(what, block):
        return remote(
            buffers[what].at[block, mine],
            buffers[what].at[block, mine],
            swap_send.at[what, block],
            swap_recv.at[what, block],
            sibling,
        )

    def swap_arrival(what, block):
        return remote(
            buffers[what].at[block, others],
            buffers[what].at[block, others],
            swap_send.at[what, block],
            swap_recv.at[what, block],
            sibling,
        )

    def send_step(step, what):
        for side in (1, -1):
            there, copy = chain(step, what, side)

            @pl.when(there)
            def _():
                copy.start()

    def arrivals(step, what):
        for side in (1, -1):
            block = me - side * step
            there = (block >= 0) & (block < owners)
            safe = jnp.clip(block, 0, owners - 1)

            @pl.when(there)
            def _():
                chain_copy = remote(
                    buffers[what].at[safe, mine],
                    buffers[what].at[safe, mine],
                    chain_send.at[what, step - 1, 0],
                    chain_recv.at[what, safe],
                    sibling,
                )
                chain_copy.wait_recv()

        if step + 1 < owners:
            send_step(step + 1, what)
        for side in (1, -1):
            block = me - side * step
            there = (block >= 0) & (block < owners)
            safe = jnp.clip(block, 0, owners - 1)

            @pl.when(there)
            def _():
                swap(what, safe).start()

    heads, length, head_size = query_hbm.shape
    kv_heads = key_hbm.shape[0]
    groups = heads // kv_heads
    tile = 64

    def part_of(expert, part):
        return pl.ds(pl.multiple_of((2 * expert + part) * units, units), units)

    def both_of(expert):
        return pl.ds(pl.multiple_of(2 * expert * units, 2 * units), 2 * units)

    def own_of(expert):
        return pl.ds(pl.multiple_of(expert * units, units), units)

    def weight_loads(expert):
        return [
            pltpu.make_async_copy(
                gateup_hbm.at[expert, part],
                gateup_ref.at[:, part_of(expert, part)],
                weight_sem.at[part, expert],
            )
            for part in range(2)
        ] + [
            pltpu.make_async_copy(
                down_hbm.at[expert], down_ref.at[own_of(expert)], weight_sem.at[2, expert]
            )
        ]

    def attention_phase(
        tokens, query_weight, keyvalue_weight, out_weight, normed, query, key, value, group_out, heads_out, partial, middle
    ):
        load_tokens = pltpu.make_async_copy(tokens_hbm, tokens, load_sem.at[1])
        loads = (
            pltpu.make_async_copy(query_weight_hbm, query_weight, load_sem.at[2]),
            pltpu.make_async_copy(keyvalue_weight_hbm, keyvalue_weight, load_sem.at[3]),
            pltpu.make_async_copy(out_weight_hbm, out_weight, load_sem.at[4]),
        )
        keeps = (
            pltpu.make_async_copy(normed, normed_hbm, keep_sem.at[0]),
            pltpu.make_async_copy(query, query_hbm, keep_sem.at[1]),
            pltpu.make_async_copy(key, key_hbm, keep_sem.at[2]),
            pltpu.make_async_copy(value, value_hbm, keep_sem.at[3]),
            pltpu.make_async_copy(heads_out, heads_hbm, keep_sem.at[4]),
            pltpu.make_async_copy(middle, middle_hbm, keep_sem.at[5]),
        )
        load_tokens.start()
        for copy in loads:
            copy.start()
        for expert in range(local):
            for copy in weight_loads(expert):
                copy.start()
        own_cot.wait()
        pl.semaphore_wait(barrier, peers)
        send_step(1, 1)
        for shift in range(1, owners):
            hits_copy(shift).start()
        load_tokens.wait()

        def first_norm(step, carry):
            at = pl.ds(pl.multiple_of(step * tile, tile), tile)
            unit, _ = norm_parts(tokens[at].astype(jnp.float32))
            normed[at] = (unit * gains_ref[0:1]).astype(jnp.bfloat16)
            return carry

        lax.fori_loop(0, total // tile, first_norm, 0)
        keeps[0].start()

        def turned(values):
            swapped = jnp.concatenate(
                [values[:, head_size // 2 :], values[:, : head_size // 2]], axis=1
            )
            return (values * cosine_ref[...] - swapped * sine_ref[...]).astype(jnp.bfloat16)

        loads[0].wait()
        projected = jnp.dot(normed[...], query_weight[...], preferred_element_type=jnp.float32)
        for head in range(heads):
            query[head] = turned(projected[:, head * head_size : (head + 1) * head_size])
        loads[1].wait()
        projected = jnp.dot(normed[...], keyvalue_weight[0], preferred_element_type=jnp.float32)
        for head in range(kv_heads):
            key[head] = turned(projected[:, head * head_size : (head + 1) * head_size])
        projected = jnp.dot(normed[...], keyvalue_weight[1], preferred_element_type=jnp.float32)
        for head in range(kv_heads):
            value[head] = projected[:, head * head_size : (head + 1) * head_size].astype(
                jnp.bfloat16
            )
        for copy in keeps[1:4]:
            copy.start()
        causal = length // 2

        def body(group, carry):
            keys, values = key[group], value[group]
            found = []
            for member in range(groups):
                some = query[group * groups + member]
                pieces = []
                for start in (0, causal):
                    stop = start + causal
                    scores = contract(some[start:stop], keys[:stop], 1, 1) * ATTN_SCALE
                    row = start + lax.broadcasted_iota(jnp.int32, scores.shape, 0)
                    col = lax.broadcasted_iota(jnp.int32, scores.shape, 1)
                    scores = jnp.where(row >= col, scores, NEGATIVE)
                    raised = jnp.exp(scores - jnp.max(scores, axis=1, keepdims=True))
                    probs = raised * (1.0 / jnp.sum(raised, axis=1, keepdims=True))
                    pieces.append(
                        jnp.dot(
                            probs.astype(jnp.bfloat16),
                            values[:stop],
                            preferred_element_type=jnp.float32,
                        )
                    )
                found.append(jnp.concatenate(pieces, axis=0))
            group_out[group] = jnp.concatenate(found, axis=1).astype(jnp.bfloat16)

            @pl.when(group == kv_heads - 1)
            def _():
                arrivals(1, 1)

            return carry

        lax.fori_loop(0, kv_heads, body, 0)
        heads_out[...] = jnp.concatenate([group_out[g] for g in range(kv_heads)], axis=1)
        keeps[4].start()
        loads[2].wait()
        half_send[...] = jnp.dot(
            heads_out[others], out_weight[...], preferred_element_type=jnp.float32
        ).astype(jnp.bfloat16)
        half_copy = remote(half_send, half_land, half_sem.at[0], half_sem.at[1], sibling)
        half_copy.start()
        partial[...] = jnp.dot(
            heads_out[mine], out_weight[...], preferred_element_type=jnp.float32
        )
        half_copy.wait()

        def second_norm(step, carry):
            at = pl.ds(pl.multiple_of(step * tile, tile), tile)
            to = pl.ds(pl.multiple_of(core * half + step * tile, tile), tile)
            after = tokens[to].astype(jnp.float32) + RESIDUAL * (
                partial[at] + half_land[at].astype(jnp.float32)
            )
            middle[at] = after
            unit, _ = norm_parts(after)
            rows_all[me, to] = (unit * gains_ref[1:2]).astype(jnp.bfloat16)
            return carry

        lax.fori_loop(0, half // tile, second_norm, 0)
        swap(0, me).start()
        send_step(1, 0)
        keeps[5].start()
        for copy in keeps:
            copy.wait()

    pl.run_scoped(
        attention_phase,
        pltpu.VMEM((total, feat_width), jnp.bfloat16),
        pltpu.VMEM(query_weight_hbm.shape, jnp.bfloat16),
        pltpu.VMEM(keyvalue_weight_hbm.shape, jnp.bfloat16),
        pltpu.VMEM(out_weight_hbm.shape, jnp.bfloat16),
        pltpu.VMEM((total, feat_width), jnp.bfloat16),
        pltpu.VMEM(query_hbm.shape, jnp.bfloat16),
        pltpu.VMEM(key_hbm.shape, jnp.bfloat16),
        pltpu.VMEM(value_hbm.shape, jnp.bfloat16),
        pltpu.VMEM((kv_heads, total, groups * head_size), jnp.bfloat16),
        pltpu.VMEM(heads_hbm.shape, jnp.bfloat16),
        pltpu.VMEM((half, feat_width), jnp.float32),
        pltpu.VMEM((half, feat_width), jnp.float32),
    )

    width = feat_width // (rows * columns)
    inside = min(early, 2)

    def term_loads(act, hidden, slot, expert, turns):
        some = pl.ds(turns[0], len(turns))
        return (
            pltpu.make_async_copy(act_hbm.at[expert, some], act.at[slot], dots_sem.at[0, slot]),
            pltpu.make_async_copy(
                hidden_hbm.at[expert, some], hidden.at[slot], dots_sem.at[1, slot]
            ),
        )

    def weight_grads(terms, grads):
        up_sum = sum(
            contract(rows_all[block_order(me, owners, turn)], hidden[...], 0, 0)
            for _, hidden, turn in terms
        ).astype(jnp.bfloat16)
        down_sum = sum(
            contract(act[...], cot_all[block_order(me, owners, turn)], 0, 0)
            for act, _, turn in terms
        )
        down_sum = (RESIDUAL * down_sum).T.astype(jnp.bfloat16)
        for y in range(rows):
            for x in range(columns):
                start = (y * columns + x) * width
                for part in range(2):
                    grads[y, x, part, :width] = up_sum[
                        start : start + width, part * units : (part + 1) * units
                    ]
                    at = start + part * (width // 2)
                    grads[y, x, part, width:] = down_sum[at : at + width // 2]

    def store_grads(grads, expert, slot):
        return pltpu.make_async_copy(grads, grads_hbm.at[:, :, expert], grads_sem.at[slot])

    def early_copies(grads, expert):
        found = []
        for part, axis, landing in ((0, "x", early_a), (1, "y", early_b)):
            for shift in range(1, place.sizes[axis]):
                to = place.peer(axis, shift)
                found.append(
                    remote(
                        grads.at[:, to, part] if axis == "x" else grads.at[to, :, part],
                        landing.at[shift - 1, expert],
                        early_send.at[part, shift - 1, expert],
                        early_recv.at[part, shift - 1, expert],
                        place.device(axis, to),
                    )
                )
        return found

    relays = owners == 4
    middle_owner = (me > 0) & (me < owners - 1)

    def goes_back(turn):
        if not relays:
            return turn > 0
        return ((turn != 1) & (turn != 2)) | ~middle_owner

    def back_copy(turn):
        return remote(
            recv_grad.at[turn],
            parts_hbm.at[turn],
            back_send.at[turn],
            back_recv.at[turn],
            {"expert": block_order(me, owners, turn)},
        )

    def dots_copy(turn):
        return remote(
            recv_dots.at[turn],
            dots_hbm.at[turn],
            dots_send.at[turn],
            dots_back.at[turn],
            {"expert": block_order(me, owners, turn)},
        )

    def relay_copy():
        return remote(
            recv_grad.at[2],
            relay,
            relay_sem.at[0],
            relay_sem.at[1],
            {"expert": block_order(me, owners, 3)},
        )

    def expert_phase(
        dot_sum, hold_comb, hold_grad, hold_dot, act_block, hidden_block, act_terms, hidden_terms, grads
    ):
        lane = lax.broadcasted_iota(jnp.int32, (total, lanes), 1)

        def stage_copies(expert, turn):
            return (
                pltpu.make_async_copy(
                    act_block.at[:, own_of(expert)],
                    act_hbm.at[expert, turn],
                    stage_sem.at[0, expert],
                ),
                pltpu.make_async_copy(
                    hidden_block.at[:, both_of(expert)],
                    hidden_hbm.at[expert, turn],
                    stage_sem.at[1, expert],
                ),
            )

        def sums_copies(turn):
            return (
                remote(send_grad, recv_grad.at[turn], sums_send.at[0], grad_recv.at[turn], sibling),
                remote(send_comb, recv_comb.at[turn], sums_send.at[1], comb_recv.at[turn], sibling),
                remote(send_dots, recv_dots.at[turn], sums_send.at[2], dots_recv.at[turn], sibling),
            )

        def own_back():
            return (
                pltpu.make_async_copy(recv_grad.at[0], parts_hbm.at[0], back_send.at[0]),
                pltpu.make_async_copy(recv_dots.at[0], dots_hbm.at[0], dots_send.at[0]),
            )

        def comb_copy(turn, block):
            return pltpu.make_async_copy(
                recv_comb.at[turn],
                comb_hbm.at[lax.rem(block - me + owners, owners)],
                comb_sem.at[turn],
            )

        def settle(turn):
            block = block_order(me, owners, turn)
            copy_grad, copy_comb, copy_dots = sums_copies(turn)
            copy_dots.wait_recv()
            recv_dots[turn] = hold_dot[...] + recv_dots[turn]
            copy_grad.wait_recv()
            recv_grad[turn] = (
                hold_grad[...] + recv_grad[turn].astype(jnp.float32)
            ).astype(jnp.bfloat16)

            @pl.when(turn > 0)
            def _():
                dots_copy(turn).start()

            @pl.when((turn > 0) & goes_back(turn))
            def _():
                back_copy(turn).start()

            if relays:

                @pl.when((turn == 2) & middle_owner)
                def _():
                    relay_copy().start()

            @pl.when(turn == 0)
            def _():
                for copy in own_back():
                    copy.start()

            copy_comb.wait_recv()
            recv_comb[turn] = (hold_comb[...] + recv_comb[turn].astype(jnp.float32)).astype(
                jnp.bfloat16
            )
            comb_copy(turn, block).start()

        last = (owners - 1) * local

        def body(number, carry):
            turn = number // local
            expert = number % local
            block = block_order(me, owners, turn)

            @pl.when(expert == 0)
            def _():
                swap_arrival_needed = turn > 0

                @pl.when(swap_arrival_needed)
                def _():
                    swap_arrival(1, block).wait_recv()
                    hits_arrival(block).wait_recv()

                swap_arrival(0, block).wait_recv()
                hits = hits_all[block].astype(jnp.float32).T > 0.5
                logits = contract(rows_all[block], router_wide[...], 1, 1)
                logits = jnp.where(hits, logits, NEGATIVE)
                raised = jnp.where(
                    hits, jnp.exp(logits - jnp.max(logits, axis=1, keepdims=True)), 0.0
                )
                gates_ref[...] = raised / jnp.sum(raised, axis=1, keepdims=True)

                @pl.when(turn == 0)
                def _():
                    gates_out[...] = gates_ref[mine]

            @pl.when(number < local)
            def _():
                for copy in weight_loads(expert):
                    copy.wait()

            @pl.when((turn > 0) & (number < last))
            def _():
                for copy in stage_copies(expert, turn):
                    copy.wait()

            chosen = rows_all[block]
            gate_part = jnp.dot(
                chosen, gateup_ref[:, part_of(expert, 0)], preferred_element_type=jnp.float32
            )
            up_part = jnp.dot(
                chosen, gateup_ref[:, part_of(expert, 1)], preferred_element_type=jnp.float32
            )
            raw = contract(cot_all[block], down_ref[own_of(expert)], 1, 1)
            here = lane == me * local + expert
            weight = jnp.sum(jnp.where(here, gates_ref[...], 0.0), axis=1, keepdims=True)
            sigmoid_gate = 0.5 * jnp.tanh(0.5 * gate_part) + 0.5
            silu_gate = gate_part * sigmoid_gate
            activation = silu_gate * up_part
            dots = jnp.where(here, jnp.sum(activation * raw, axis=1, keepdims=True), 0.0)
            weighted = (activation * weight).astype(jnp.bfloat16)
            act_block[:, own_of(expert)] = weighted
            grad_act = raw * (RESIDUAL * weight)
            grad_gatepart = (
                grad_act * up_part * (sigmoid_gate * (1.0 + gate_part * (1.0 - sigmoid_gate)))
            ).astype(jnp.bfloat16)
            grad_uppart = (grad_act * silu_gate).astype(jnp.bfloat16)
            hidden_block[:, part_of(expert, 0)] = grad_gatepart
            hidden_block[:, part_of(expert, 1)] = grad_uppart
            for copy in stage_copies(expert, turn):
                copy.start()

            @pl.when(expert == 0)
            def _():
                dot_sum[...] = dots

            @pl.when(expert > 0)
            def _():
                dot_sum[...] += dots

            @pl.when((expert == 1) & (turn > 0) & (turn < owners - 1))
            def _():
                settle(turn - 1)

            for step in range(1, owners - 1):

                @pl.when(number == step * local - 2)
                def _():
                    for late in COT_STEPS.get(step, ()):
                        arrivals(late, 1)
                    arrivals(step, 0)

            @pl.when(expert == local - 1)
            def _():
                @pl.when(turn > 0)
                def _():
                    for copy in sums_copies(turn):
                        copy.wait_send()

                def grad_of(some):
                    return contract(hidden_block[some], gateup_ref[...], 1, 1)

                def comb_of(some):
                    return jnp.dot(
                        act_block[some], down_ref[...], preferred_element_type=jnp.float32
                    )

                send_grad[...] = grad_of(others).astype(jnp.bfloat16)
                send_dots[...] = dot_sum[others].T
                send_comb[...] = comb_of(others).astype(jnp.bfloat16)
                for copy in sums_copies(turn):
                    copy.start()
                hold_grad[...] = grad_of(mine)
                hold_comb[...] = comb_of(mine)
                hold_dot[...] = dot_sum[mine].T

            return carry

        lax.fori_loop(0, last, body, 0)
        settle(owners - 2)
        for expert in range(local):
            for copy in stage_copies(expert, 0):
                copy.wait()
        earlier = range(owners - 1)
        for copy in term_loads(act_terms, hidden_terms, 0, 0, earlier):
            copy.start()
        for step in range(2, owners):
            if not any(step in late for late in COT_STEPS.values()):
                arrivals(step, 1)
        arrivals(owners - 1, 0)


        def with_weights(expert, carry):
            body(last + expert, carry)
            for copy in term_loads(act_terms, hidden_terms, 0, expert, earlier):
                copy.wait()
            terms = [
                (act_terms.at[0, turn], hidden_terms.at[0, turn], turn) for turn in earlier
            ] + [
                (
                    act_block.at[:, own_of(expert)],
                    hidden_block.at[:, both_of(expert)],
                    owners - 1,
                )
            ]
            weight_grads(terms, grads.at[expert % 2])
            store_grads(grads.at[expert % 2], expert, expert % 2).start()
            for copy in early_copies(grads.at[expert % 2], expert):
                copy.start()

            @pl.when(expert + 1 < inside)
            def _():
                for copy in term_loads(act_terms, hidden_terms, 0, expert + 1, earlier):
                    copy.start()

            return carry

        lax.fori_loop(0, inside, with_weights, 0)
        lax.fori_loop(last + inside, owners * local, body, 0)
        settle(owners - 1)
        if relays:

            @pl.when(middle_owner)
            def _():
                relay_copy().wait_recv()
                recv_grad[1] = (
                    recv_grad[1].astype(jnp.float32) + relay[...].astype(jnp.float32)
                ).astype(jnp.bfloat16)
                back_copy(1).start()

        for copy in sums_copies(owners - 1):
            copy.wait_send()
        for expert in range(local):
            for copy in stage_copies(expert, 0):
                copy.wait()
        for expert in range(inside):
            store_grads(grads.at[expert % 2], expert, expert % 2).wait()
            for copy in early_copies(grads.at[expert % 2], expert):
                copy.wait_send()
        for turn in range(owners):
            block = block_order(me, owners, turn)
            comb_copy(turn, block).wait()

    pl.run_scoped(
        expert_phase,
        pltpu.VMEM((total, lanes), jnp.float32),
        pltpu.VMEM((half, feat_width), jnp.float32),
        pltpu.VMEM((half, feat_width), jnp.float32),
        pltpu.VMEM((lanes, half), jnp.float32),
        pltpu.VMEM((total, local * units), jnp.bfloat16),
        pltpu.VMEM((total, 2 * local * units), jnp.bfloat16),
        pltpu.VMEM((1, owners - 1, total, units), jnp.bfloat16),
        pltpu.VMEM((1, owners - 1, total, 2 * units), jnp.bfloat16),
        pltpu.VMEM((2,) + grads_hbm.shape[:2] + grads_hbm.shape[3:], jnp.bfloat16),
    )

    def weights_phase(act, hidden, grads):
        turns = range(owners)

        def loads(expert):
            return term_loads(act, hidden, expert % 2, expert, turns)

        def sent(expert):
            store_grads(grads.at[expert % 2], expert, expert % 2).wait()

            @pl.when(expert < early)
            def _():
                for copy in early_copies(grads.at[expert % 2], expert):
                    copy.wait_send()

        for copy in loads(inside):
            copy.start()

        def body(expert, carry):
            slot = expert % 2

            @pl.when(expert + 1 < local)
            def _():
                for copy in loads(expert + 1):
                    copy.start()

            for copy in loads(expert):
                copy.wait()

            @pl.when(expert >= inside + 2)
            def _():
                sent(expert - 2)

            terms = [(act.at[slot, turn], hidden.at[slot, turn], turn) for turn in turns]
            weight_grads(terms, grads.at[slot])
            store_grads(grads.at[slot], expert, slot).start()

            @pl.when(expert < early)
            def _():
                for copy in early_copies(grads.at[slot], expert):
                    copy.start()

            return carry

        lax.fori_loop(inside, local, body, 0)
        for expert in range(max(inside, local - 2), local):
            sent(expert)

    pl.run_scoped(
        weights_phase,
        pltpu.VMEM((2, owners, total, units), jnp.bfloat16),
        pltpu.VMEM((2, owners, total, 2 * units), jnp.bfloat16),
        pltpu.VMEM((2,) + grads_hbm.shape[:2] + grads_hbm.shape[3:], jnp.bfloat16),
    )
    for expert in range(early):
        for copy in early_copies(grads_hbm.at[:, :, expert], expert):
            copy.wait_recv()

    swap(0, me).wait_send()
    for step in range(1, owners):
        for what in range(2):
            for side in (1, -1):
                there, copy = chain(step, what, side)

                @pl.when(there)
                def _():
                    copy.wait_send()

                block = me - side * step
                arrived = (block >= 0) & (block < owners)
                safe = jnp.clip(block, 0, owners - 1)

                @pl.when(arrived)
                def _():
                    swap(what, safe).wait_send()

    for shift in range(1, owners):
        hits_copy(shift).wait_send()
    pltpu.make_async_copy(recv_grad.at[0], parts_hbm.at[0], back_send.at[0]).wait()
    pltpu.make_async_copy(recv_dots.at[0], dots_hbm.at[0], dots_send.at[0]).wait()
    for turn in range(1, owners):
        dots_copy(turn).wait()
        if relays and turn == 1:
            back_copy(turn).wait()
        elif relays and turn == 2:

            @pl.when(middle_owner)
            def _():
                relay_copy().wait_send()
                back_copy(turn).wait_recv()

            @pl.when(~middle_owner)
            def _():
                back_copy(turn).wait_send()
                none = pltpu.make_async_copy(half_send, parts_hbm.at[turn], load_sem.at[0])
                half_send[...] = jnp.zeros_like(half_send)
                none.start()
                none.wait()

        else:
            back_copy(turn).wait()


def experts(
    tokens,
    cot,
    routes,
    gains,
    cosine,
    sine,
    router,
    query_weight,
    keyvalue_weight,
    out_weight,
    gateup,
    down,
):
    owners = lax.axis_size("expert")
    rows, columns = factors(lax.axis_size("dp"))
    total, feat_width = tokens.shape
    half = total // 2
    local, units = down.shape[0], down.shape[1]
    height = 3 * feat_width // (rows * columns) // 2
    early = min(EARLY, local)
    most = max(rows, columns) - 1
    lanes = 32
    heads = query_weight.shape[1] // HEAD_SIZE
    kv_heads = keyvalue_weight.shape[2] // HEAD_SIZE
    hbm = pl.BlockSpec(memory_space=pl.ANY)
    vmem = pl.BlockSpec(memory_space=pltpu.VMEM)
    bf16, f32 = jnp.bfloat16, jnp.float32
    dma = pltpu.SemaphoreType.DMA
    return pl.pallas_call(
        functools.partial(expert_kernel, rows, columns, owners, local, early),
        in_specs=[hbm, hbm] + [vmem] * 5 + [hbm] * 5,
        out_specs=[hbm, hbm, hbm, vmem] + [hbm] * 11,
        out_shape=[
            jax.ShapeDtypeStruct((owners, half, feat_width), bf16),
            jax.ShapeDtypeStruct((owners, lanes, half), f32),
            jax.ShapeDtypeStruct((owners, half, feat_width), bf16),
            jax.ShapeDtypeStruct((half, lanes), f32),
            jax.ShapeDtypeStruct((rows, columns, local, 2, height, units), bf16),
            jax.ShapeDtypeStruct((columns - 1, early, rows, height, units), bf16),
            jax.ShapeDtypeStruct((rows - 1, early, columns, height, units), bf16),
            jax.ShapeDtypeStruct((local, owners, total, units), bf16),
            jax.ShapeDtypeStruct((local, owners, total, 2 * units), bf16),
            jax.ShapeDtypeStruct((total, feat_width), bf16),
            jax.ShapeDtypeStruct((heads, total, HEAD_SIZE), bf16),
            jax.ShapeDtypeStruct((kv_heads, total, HEAD_SIZE), bf16),
            jax.ShapeDtypeStruct((kv_heads, total, HEAD_SIZE), bf16),
            jax.ShapeDtypeStruct((total, heads * HEAD_SIZE), bf16),
            jax.ShapeDtypeStruct((half, feat_width), f32),
        ],
        scratch_shapes=[
            pltpu.VMEM((owners, total, feat_width), bf16),
            pltpu.VMEM((owners, total, feat_width), bf16),
            pltpu.VMEM((owners, lanes, total), bf16),
            pltpu.VMEM((feat_width, 2 * local * units), bf16),
            pltpu.VMEM((local * units, feat_width), bf16),
            pltpu.VMEM((lanes, feat_width), bf16),
            pltpu.VMEM((half, feat_width), bf16),
            pltpu.VMEM((half, feat_width), bf16),
            pltpu.VMEM((total, lanes), f32),
            pltpu.VMEM((half, feat_width), bf16),
            pltpu.VMEM((half, feat_width), bf16),
            pltpu.VMEM((lanes, half), f32),
            pltpu.VMEM((owners, half, feat_width), bf16),
            pltpu.VMEM((owners, half, feat_width), bf16),
            pltpu.VMEM((owners, lanes, half), f32),
            pltpu.VMEM((half, feat_width), bf16),
            dma((5,)),
            dma((6,)),
            dma((2,)),
            dma((3, local)),
            dma((2, owners - 1, 2)),
            dma((2, owners)),
            dma((2, owners)),
            dma((2, owners)),
            dma((3,)),
            dma((owners,)),
            dma((owners,)),
            dma((owners,)),
            dma((owners,)),
            dma((owners,)),
            dma((owners,)),
            dma((owners,)),
            dma((owners - 1,)),
            dma((owners,)),
            dma((2,)),
            dma((owners,)),
            dma((2, local)),
            dma((2, most, early)),
            dma((2, most, early)),
            dma((2, 2)),
            dma((2,)),
        ],
        compiler_params=pltpu.CompilerParams(
            vmem_limit_bytes=60 * 2**20, collective_id=0, has_side_effects=True
        ),
        cost_estimate=pl.CostEstimate(
            flops=2 * owners * total * feat_width * units * 9 * local,
            bytes_accessed=80 * 2**20,
            transcendentals=owners * total * units * local,
        ),
    )(
        tokens,
        cot,
        routes,
        gains,
        cosine,
        sine,
        router,
        query_weight,
        keyvalue_weight,
        out_weight,
        gateup,
        down,
    )


class Summing:
    def __init__(self, place, source, axes, order, landing, send, recv):
        self.place, self.order, self.landing = place, order, landing
        self.send, self.recv = send, recv
        self.sources, self.positions = [source], []
        left = list(axes)
        for step, axis in enumerate(order):
            self.positions.append(left.index(axis))
            left.pop(self.positions[-1])
            self.sources.append(landing[step].at[0])

    def copies(self, step):
        axis = self.order[step]
        found = []
        for shift in range(1, self.place.sizes[axis]):
            to = self.place.peer(axis, shift)
            found.append(
                pltpu.make_async_remote_copy(
                    src_ref=picked(self.sources[step], self.positions[step], to),
                    dst_ref=self.landing[step].at[shift - 1],
                    send_sem=self.send.at[step, shift - 1],
                    recv_sem=self.recv.at[step, shift - 1],
                    device_id=self.place.device(axis, to),
                    device_id_type=pl.DeviceIdType.MESH,
                )
            )
        return found

    def start(self, step):
        for copy in self.copies(step):
            copy.start()

    def total(self, step):
        axis = self.order[step]
        for copy in self.copies(step):
            copy.wait_recv()
        own = picked(self.sources[step], self.positions[step], self.place.at[axis])
        value = own[...].astype(jnp.float32)
        for shift in range(1, self.place.sizes[axis]):
            value = value + self.landing[step][shift - 1].astype(jnp.float32)
        return value

    def forward(self, step):
        self.landing[step][0] = self.total(step).astype(self.landing[step].dtype)
        self.start(step + 1)

    def close(self):
        for step in range(len(self.order)):
            for copy in self.copies(step):
                copy.wait_send()


def norm_grad(grad, gain, unit, inv_rms):
    grad_unit = grad * gain
    return inv_rms * (grad_unit - unit * jnp.mean(grad_unit * unit, axis=-1, keepdims=True))


def back_kernel(
    rows,
    columns,
    owners,
    parts_hbm,
    dots_hbm,
    comb_hbm,
    grads_hbm,
    early_a,
    early_b,
    gates_ref,
    middle_hbm,
    cot_hbm,
    tokens_hbm,
    gains_ref,
    router_ref,
    out_weight_hbm,
    heads_hbm,
    query_hbm,
    key_hbm,
    value_hbm,
    normed_hbm,
    query_weight_hbm,
    keyvalue_weight_hbm,
    cosine_ref,
    sine_ref,
    mixed_hbm,
    tokens_grad_hbm,
    kept_hbm,
    second_a,
    second_b,
    query_out,
    keyvalue_out,
    output_out,
    router_out,
    expert_gain_out,
    attn_gain_out,
    own_a,
    own_b,
    first_a,
    first_b,
    comb_own,
    comb_left,
    comb_right,
    out_a,
    out_az,
    out_ax,
    out_ay,
    out_b,
    out_by,
    out_bx,
    out_bz,
    near_q,
    near_qx,
    near_qy,
    near_qz,
    near_kv,
    near_kvy,
    near_kvx,
    near_kvz,
    far_q,
    far_qy,
    far_qx,
    far_qz,
    far_kv,
    far_kvx,
    far_kvy,
    far_kvz,
    small_sum,
    small_swap,
    small_stage,
    small_z,
    small_x,
    small_y,
    grad_attn,
    grad_middle,
    grad_query,
    grad_keyvalue,
    half_send,
    half_land,
    mixed_stage,
    load_sem,
    own_sem,
    keep_sem,
    early_sem,
    first_send,
    first_recv,
    second_send,
    second_recv,
    comb_sem,
    comb_send,
    comb_recv,
    sum_send,
    sum_recv,
    swap_send,
    swap_recv,
    store_sem,
):
    place = Place(rows, columns, owners)
    core = lax.axis_index("tensor")
    sibling = {"tensor": 1 - core}
    half, feat_width = middle_hbm.shape
    local = grads_hbm.shape[2]
    early = early_a.shape[1]
    heads, length, head_size = query_hbm.shape
    kv_heads = key_hbm.shape[0]
    groups = heads // kv_heads
    query_width = heads * head_size
    key_width = kv_heads * head_size
    tile = 64
    mine = pl.ds(pl.multiple_of(core * half, half), half)
    others = pl.ds(pl.multiple_of((1 - core) * half, half), half)

    barrier = pltpu.get_barrier_semaphore()
    peers = [sibling]
    for axis in ("x", "y", "z"):
        for shift in range(1, place.sizes[axis]):
            peers.append(place.device(axis, place.peer(axis, shift)))
    for peer in peers:
        pl.semaphore_signal(barrier, inc=1, device_id=peer, device_id_type=pl.DeviceIdType.MESH)
    pl.semaphore_wait(barrier, len(peers))

    def to_sibling(src, dst, at):
        return pltpu.make_async_remote_copy(
            src_ref=src,
            dst_ref=dst,
            send_sem=swap_send.at[at],
            recv_sem=swap_recv.at[at],
            device_id=sibling,
            device_id_type=pl.DeviceIdType.MESH,
        )

    plans = (
        (0, "x", "y", own_a, first_a, second_a),
        (1, "y", "x", own_b, first_b, second_b),
    )

    def grads_of(part, axis, index, expert):
        if axis == "x":
            return grads_hbm.at[:, index, expert, part]
        return grads_hbm.at[index, :, expert, part]

    def own_load(plan, expert):
        part, axis, _, own, _, _ = plan
        return pltpu.make_async_copy(
            grads_of(part, axis, place.at[axis], expert),
            own.at[expert % 2],
            own_sem.at[part, expert],
        )

    def early_load(plan, expert):
        part, _, _, _, first, _ = plan
        source = (early_a, early_b)[part]
        return pltpu.make_async_copy(
            source.at[:, expert], first.at[:, expert], early_sem.at[part, expert]
        )

    def first_copies(plan, expert):
        part, axis, _, _, first, _ = plan
        found = []
        for shift in range(1, place.sizes[axis]):
            to = place.peer(axis, shift)
            found.append(
                pltpu.make_async_remote_copy(
                    src_ref=grads_of(part, axis, to, expert),
                    dst_ref=first.at[shift - 1, expert],
                    send_sem=first_send.at[part, shift - 1, expert],
                    recv_sem=first_recv.at[part, shift - 1, expert],
                    device_id=place.device(axis, to),
                    device_id_type=pl.DeviceIdType.MESH,
                )
            )
        return found

    def second_copies(plan, expert):
        part, _, axis, _, first, second = plan
        found = []
        for shift in range(1, place.sizes[axis]):
            to = place.peer(axis, shift)
            found.append(
                pltpu.make_async_remote_copy(
                    src_ref=first.at[0, expert, to],
                    dst_ref=second.at[shift - 1, expert],
                    send_sem=second_send.at[part, shift - 1, expert],
                    recv_sem=second_recv.at[part, shift - 1, expert],
                    device_id=place.device(axis, to),
                    device_id_type=pl.DeviceIdType.MESH,
                )
            )
        return found

    def first_sum(expert):
        for plan in plans:
            _, axis, after, own, first, _ = plan
            own_load(plan, expert).wait()

            @pl.when(expert < early)
            def _():
                early_load(plan, expert).wait()

            @pl.when(expert >= early)
            def _():
                for copy in first_copies(plan, expert):
                    copy.wait_recv()

            for index in range(place.sizes[after]):
                value = own[expert % 2, index].astype(jnp.float32)
                for shift in range(1, place.sizes[axis]):
                    value = value + first[shift - 1, expert, index].astype(jnp.float32)
                first[0, expert, index] = value.astype(first.dtype)

            @pl.when(expert + 2 < local)
            def _():
                own_load(plan, expert + 2).start()

    def keep(plan, expert):
        part, _, axis, _, first, _ = plan
        return pltpu.make_async_copy(
            first.at[0, expert, place.at[axis]],
            kept_hbm.at[part, expert],
            keep_sem.at[part, expert],
        )

    def start_first(expert, carry):
        for plan in plans:
            for copy in first_copies(plan, expert):
                copy.start()
        return carry

    held = local - 1
    lax.fori_loop(early, held, start_first, 0)
    for plan in plans:
        for expert in range(early):
            early_load(plan, expert).start()
        for expert in range(min(2, local)):
            own_load(plan, expert).start()

    me = place.at["z"]

    def comb_load(shift):
        return pltpu.make_async_copy(comb_hbm.at[shift], comb_own.at[shift], comb_sem.at[shift])

    def comb_copy(side, away):
        landing, at = (comb_right, 0) if side == 1 else (comb_left, 1)
        shift = away if side == 1 else owners - away
        to = jnp.clip(me + side, 0, owners - 1)
        return pltpu.make_async_remote_copy(
            src_ref=comb_own.at[shift],
            dst_ref=landing.at[away - 1],
            send_sem=comb_send.at[at, away],
            recv_sem=comb_recv.at[at, away - 1],
            device_id=place.device("z", to),
            device_id_type=pl.DeviceIdType.MESH,
        )

    def comb_arrival(side, away):
        landing, at = (comb_right, 0) if side == 1 else (comb_left, 1)
        from_ = jnp.clip(me - side, 0, owners - 1)
        return pltpu.make_async_remote_copy(
            src_ref=comb_own.at[0],
            dst_ref=landing.at[away],
            send_sem=comb_send.at[at, away],
            recv_sem=comb_recv.at[at, away],
            device_id=place.device("z", from_),
            device_id_type=pl.DeviceIdType.MESH,
        )

    def inside(at):
        return (at >= 0) & (at < owners)

    def comb_send_on(away):
        for side in (1, -1):

            @pl.when(inside(me + side * away))
            def _():
                comb_copy(side, away).start()

    def comb_add(away):
        for side in (1, -1):

            @pl.when(inside(me + side * away) & inside(me - side))
            def _():
                comb_arrival(side, away).wait_recv()
                landing = comb_right if side == 1 else comb_left
                shift = 0 if away == 0 else (away if side == 1 else owners - away)
                comb_own[shift] = (
                    comb_own[shift].astype(jnp.float32) + landing[away].astype(jnp.float32)
                ).astype(jnp.bfloat16)

    def comb_stage(away):
        comb_add(away)
        if away > 0:
            comb_send_on(away)

    def job(source, order, landing, at):
        return Summing(
            place, source, ("y", "x", "z"), order, landing, sum_send.at[at], sum_recv.at[at]
        )

    output_job_a = job(out_a, ("z", "x", "y"), (out_az, out_ax, out_ay), 0)
    output_job_b = job(out_b, ("y", "x", "z"), (out_by, out_bx, out_bz), 4)
    pair_jobs = (
        (
            job(near_q, ("x", "y", "z"), (near_qx, near_qy, near_qz), 1),
            job(near_kv, ("y", "x", "z"), (near_kvy, near_kvx, near_kvz), 2),
        ),
        (
            job(far_q, ("y", "x", "z"), (far_qy, far_qx, far_qz), 5),
            job(far_kv, ("x", "y", "z"), (far_kvx, far_kvy, far_kvz), 6),
        ),
    )
    pair_stages = ((near_q, near_kv), (far_q, far_kv))
    small_job = job(small_stage, ("z", "x", "y"), (small_z, small_x, small_y), 3)

    def weight_grad(stage, left, right):
        count = stage.shape[3]
        band = feat_width // 4
        for start in range(0, feat_width, band):
            value = contract(left[:, start : start + band], right, 0, 0).astype(jnp.bfloat16)
            for at in range(start, start + band, count):
                index = at // count
                y, x, z = (
                    index // (columns * owners),
                    index // owners % columns,
                    index % owners,
                )
                stage[y, x, z] = value[at - start : at - start + count]

    def middle_phase(parts, middle, cot_ref, dots_parts, dots_sum):
        loads = (
            pltpu.make_async_copy(dots_hbm, dots_parts, load_sem.at[0]),
            pltpu.make_async_copy(cot_hbm.at[mine], cot_ref, load_sem.at[3]),
            pltpu.make_async_copy(parts_hbm, parts, load_sem.at[1]),
            pltpu.make_async_copy(middle_hbm, middle, load_sem.at[2]),
        )
        for copy in loads:
            copy.start()
        for shift in range(owners):
            comb_load(shift).start()
        for copy in loads:
            copy.wait()
        small_sum[...] = jnp.zeros_like(small_sum)
        dots_sum[...] = sum(dots_parts[b] for b in range(owners)).T

        def body(step, carry):
            at = pl.ds(pl.multiple_of(step * tile, tile), tile)
            grad = sum(parts[b, at].astype(jnp.float32) for b in range(owners))
            gates = gates_ref[at]
            grad_gate = RESIDUAL * dots_sum[at]
            grad_logits = (
                gates * (grad_gate - jnp.sum(gates * grad_gate, axis=-1, keepdims=True))
            ).astype(jnp.bfloat16)
            grad = grad + contract(
                grad_logits[:, : router_ref.shape[0]], router_ref[...], 1, 0
            )
            unit, inv_rms = norm_parts(middle[at])
            expert_in = (unit * gains_ref[1:2]).astype(jnp.bfloat16)
            after = cot_ref[at].astype(jnp.float32) + norm_grad(
                grad, gains_ref[1:2], unit, inv_rms
            )
            grad_middle[at] = after
            to = pl.ds(pl.multiple_of(core * half + step * tile, tile), tile)
            grad_attn[to] = (RESIDUAL * after).astype(jnp.bfloat16)
            count = small_sum.shape[0]
            small_sum[...] += contract(grad_logits, expert_in, 0, 0)[:count]
            small_sum[count - 2 : count - 1] += jnp.sum(grad * unit, axis=0, keepdims=True)
            return carry

        lax.fori_loop(0, half // tile, body, 0)

    pl.run_scoped(
        middle_phase,
        pltpu.VMEM(parts_hbm.shape, parts_hbm.dtype),
        pltpu.VMEM(middle_hbm.shape, middle_hbm.dtype),
        pltpu.VMEM(middle_hbm.shape, cot_hbm.dtype),
        pltpu.VMEM(dots_hbm.shape, dots_hbm.dtype),
        pltpu.VMEM(gates_ref.shape, dots_hbm.dtype),
    )
    attn_swap = to_sibling(grad_attn.at[mine], grad_attn.at[mine], 0)
    attn_swap.start()
    for shift in range(owners):
        comb_load(shift).wait()
    comb_send_on(owners - 1)
    to_sibling(grad_attn.at[others], grad_attn.at[others], 0).wait_recv()

    causal = length // 2

    def attention_phase(
        out_weight_ref, heads_ref, query_ref, key_ref, value_ref, key_sum, value_sum, normed_ref
    ):
        load_normed = pltpu.make_async_copy(normed_hbm, normed_ref, load_sem.at[0])
        loads = (
            pltpu.make_async_copy(heads_hbm, heads_ref, load_sem.at[4]),
            pltpu.make_async_copy(out_weight_hbm, out_weight_ref, load_sem.at[5]),
            pltpu.make_async_copy(query_hbm, query_ref, load_sem.at[6]),
            pltpu.make_async_copy(key_hbm, key_ref, load_sem.at[7]),
            pltpu.make_async_copy(value_hbm, value_ref, load_sem.at[8]),
        )
        for copy in loads:
            copy.start()
        load_normed.start()
        loads[0].wait()
        cut = heads_ref.shape[1] // 2
        weight_grad(out_a, grad_attn, heads_ref[:, :cut])
        output_job_a.start(0)
        weight_grad(out_b, grad_attn, heads_ref[:, cut:])
        output_job_b.start(0)
        for copy in loads[1:]:
            copy.wait()

        def turned_back(grads):
            swapped = jnp.concatenate(
                [grads[:, head_size // 2 :], grads[:, : head_size // 2]], axis=1
            )
            return (grads * cosine_ref[...] + swapped * sine_ref[...]).astype(jnp.bfloat16)

        def body(group, carry):
            grad_heads = contract(grad_attn[...], out_weight_ref[group], 1, 1).astype(jnp.bfloat16)
            keys, values = key_ref[group], value_ref[group]
            key_sum[...] = jnp.zeros_like(key_sum)
            value_sum[...] = jnp.zeros_like(value_sum)
            turned = []
            for member in range(groups):
                query = query_ref[group * groups + member]
                grad_head = grad_heads[:, member * head_size : (member + 1) * head_size]
                pieces = []
                for start in (0, causal):
                    stop = start + causal
                    some_q, some_g = query[start:stop], grad_head[start:stop]
                    some_k, some_v = keys[:stop], values[:stop]
                    scores = contract(some_q, some_k, 1, 1) * ATTN_SCALE
                    row = start + lax.broadcasted_iota(jnp.int32, scores.shape, 0)
                    col = lax.broadcasted_iota(jnp.int32, scores.shape, 1)
                    scores = jnp.where(row >= col, scores, NEGATIVE)
                    raised = jnp.exp(scores - jnp.max(scores, axis=1, keepdims=True))
                    probs = raised * (1.0 / jnp.sum(raised, axis=1, keepdims=True))
                    grad_probs = contract(some_g, some_v, 1, 1)
                    value_sum[:stop] += contract(probs.astype(jnp.bfloat16), some_g, 0, 0)
                    grad_scores = (
                        probs
                        * (grad_probs - jnp.sum(probs * grad_probs, axis=1, keepdims=True))
                    ).astype(jnp.bfloat16)
                    pieces.append(
                        jnp.dot(grad_scores, some_k, preferred_element_type=jnp.float32)
                    )
                    key_sum[:stop] += contract(grad_scores, some_q, 0, 0)
                turned.append(turned_back(ATTN_SCALE * jnp.concatenate(pieces, axis=0)))
            grad_query[group] = jnp.concatenate(turned, axis=1)
            grad_keyvalue[0, group] = turned_back(ATTN_SCALE * key_sum[...])
            grad_keyvalue[1, group] = value_sum[...].astype(jnp.bfloat16)

            @pl.when(group < local)
            def _():
                first_sum(group)

            return carry

        pairs = kv_heads // 2
        for pair, (jobs, stages) in enumerate(zip(pair_jobs, pair_stages)):
            chosen = range(pair * pairs, (pair + 1) * pairs)
            lax.fori_loop(chosen[0], chosen[-1] + 1, body, 0)
            queries = jnp.concatenate([grad_query[g] for g in chosen], axis=1)
            keyvalue = jnp.concatenate(
                [grad_keyvalue[what, g] for what in range(2) for g in chosen], axis=1
            )
            if pair == 0:
                comb_stage(owners - 2)
                load_normed.wait()
            weight_grad(stages[0], normed_ref, queries)
            jobs[0].start(0)
            weight_grad(stages[1], normed_ref, keyvalue)
            jobs[1].start(0)
            if pair == 0:
                lax.fori_loop(held, local, start_first, 0)

    pl.run_scoped(
        attention_phase,
        pltpu.VMEM(out_weight_hbm.shape, out_weight_hbm.dtype),
        pltpu.VMEM(heads_hbm.shape, heads_hbm.dtype),
        pltpu.VMEM(query_hbm.shape, query_hbm.dtype),
        pltpu.VMEM(key_hbm.shape, key_hbm.dtype),
        pltpu.VMEM(value_hbm.shape, value_hbm.dtype),
        pltpu.VMEM((length, head_size), jnp.float32),
        pltpu.VMEM((length, head_size), jnp.float32),
        pltpu.VMEM(normed_hbm.shape, normed_hbm.dtype),
    )
    def start_second(expert, carry):
        for plan in plans:
            for copy in second_copies(plan, expert):
                copy.start()
            keep(plan, expert).start()
        return carry

    for which in pair_jobs[0]:
        which.forward(0)
    for away in range(owners - 3, 0, -1):
        comb_stage(away)

    def tokens_phase(query_weight, keyvalue_weight, grad_normed, tokens_ref):
        loads = (
            pltpu.make_async_copy(tokens_hbm.at[mine], tokens_ref, load_sem.at[3]),
            pltpu.make_async_copy(query_weight_hbm, query_weight, load_sem.at[1]),
            pltpu.make_async_copy(keyvalue_weight_hbm, keyvalue_weight, load_sem.at[2]),
        )
        for copy in loads:
            copy.start()
        queries = jnp.concatenate([grad_query[g] for g in range(kv_heads)], axis=1)
        keyvalue = [
            jnp.concatenate([grad_keyvalue[what, g] for g in range(kv_heads)], axis=1)
            for what in range(2)
        ]
        for copy in loads:
            copy.wait()
        grad_normed[...] = (
            contract(queries, query_weight[...], 1, 1)
            + contract(keyvalue[0], keyvalue_weight[0], 1, 1)
            + contract(keyvalue[1], keyvalue_weight[1], 1, 1)
        )
        half_send[...] = grad_normed[others].astype(jnp.bfloat16)
        swap = to_sibling(half_send, half_land, 1)
        swap.start()
        swap.wait_recv()

        def body(step, carry):
            at = pl.ds(pl.multiple_of(step * tile, tile), tile)
            to = pl.ds(pl.multiple_of(core * half + step * tile, tile), tile)
            grad = grad_normed[to] + half_land[at].astype(jnp.float32)
            unit, inv_rms = norm_parts(tokens_ref[at].astype(jnp.float32))
            grad_middle[at] += norm_grad(grad, gains_ref[0:1], unit, inv_rms)
            count = small_sum.shape[0]
            small_sum[count - 1 : count] += jnp.sum(grad * unit, axis=0, keepdims=True)
            return carry

        lax.fori_loop(0, half // tile, body, 0)

    pl.run_scoped(
        tokens_phase,
        pltpu.VMEM(query_weight_hbm.shape, query_weight_hbm.dtype),
        pltpu.VMEM(keyvalue_weight_hbm.shape, keyvalue_weight_hbm.dtype),
        pltpu.VMEM((2 * half, feat_width), jnp.float32),
        pltpu.VMEM((half, feat_width), tokens_hbm.dtype),
    )
    tokens_store = pltpu.make_async_copy(grad_middle, tokens_grad_hbm.at[mine], store_sem.at[0])
    tokens_store.start()
    tokens_swap = to_sibling(grad_middle, tokens_grad_hbm.at[mine], 2)
    tokens_swap.start()
    small_exchange = to_sibling(small_sum, small_swap, 3)
    small_exchange.start()

    small_exchange.wait()
    small_sum[...] += small_swap[...]
    piece = feat_width // (rows * columns * owners)
    small_stage[...] = jnp.zeros_like(small_stage)
    for y in range(rows):
        for x in range(columns):
            for z in range(owners):
                at = ((y * columns + x) * owners + z) * piece
                small_stage[y, x, z, :, :piece] = small_sum[:, at : at + piece]
    small_job.start(0)

    output_job_b.forward(0)
    for which in pair_jobs[1]:
        which.forward(0)
    for expert in range(kv_heads, local):
        first_sum(expert)
    lax.fori_loop(0, local, start_second, 0)
    for which in pair_jobs[0]:
        which.forward(1)
    output_job_a.forward(0)
    output_job_b.forward(1)
    for which in pair_jobs[1]:
        which.forward(1)
    output_job_a.forward(1)
    small_job.forward(0)
    small_job.forward(1)

    def mixed_phase(middle):
        load = pltpu.make_async_copy(middle_hbm, middle, load_sem.at[1])
        load.start()
        comb_stage(0)
        load.wait()

        def body(step, carry):
            at = pl.ds(pl.multiple_of(step * tile, tile), tile)
            comb = comb_own[0, at].astype(jnp.float32)
            mixed_stage[at] = (middle[at] + RESIDUAL * comb).astype(jnp.bfloat16)
            return carry

        lax.fori_loop(0, half // tile, body, 0)

    pl.run_scoped(mixed_phase, pltpu.VMEM(middle_hbm.shape, middle_hbm.dtype))
    mixed_store = pltpu.make_async_copy(mixed_stage, mixed_hbm.at[mine], store_sem.at[1])
    mixed_store.start()
    mixed_swap = to_sibling(mixed_stage, mixed_hbm.at[mine], 4)
    mixed_swap.start()

    cut = out_a.shape[4]
    output_out[:, :cut] = output_job_a.total(2)
    output_out[:, cut:] = output_job_b.total(2)
    small = small_job.total(2)
    count = small.shape[0]
    router_out[...] = small[: router_out.shape[0], :piece]
    expert_gain_out[...] = small[count - 2 : count - 1, :piece]
    attn_gain_out[...] = small[count - 1 :, :piece]
    for pair, jobs in enumerate(pair_jobs):
        cut = near_q.shape[4]
        query_out[:, pair * cut : (pair + 1) * cut] = jobs[0].total(2)
        value = jobs[1].total(2)
        cut = near_kv.shape[4] // 2
        for what in range(2):
            keyvalue_out[what, :, pair * cut : (pair + 1) * cut] = value[
                :, what * cut : (what + 1) * cut
            ]

    def close(expert, carry):
        for plan in plans:

            @pl.when(expert >= early)
            def _():
                for copy in first_copies(plan, expert):
                    copy.wait_send()

            for copy in second_copies(plan, expert):
                copy.wait()
            keep(plan, expert).wait()
        return carry

    lax.fori_loop(0, local, close, 0)
    for away in range(1, owners):
        for side in (1, -1):

            @pl.when(inside(me + side * away))
            def _():
                comb_copy(side, away).wait_send()

    for which in (output_job_a, output_job_b, small_job) + pair_jobs[0] + pair_jobs[1]:
        which.close()
    attn_swap.wait_send()
    to_sibling(half_send, half_land, 1).wait_send()
    tokens_store.wait()
    mixed_store.wait()
    tokens_swap.wait_send()
    mixed_swap.wait_send()
    to_sibling(grad_middle, tokens_grad_hbm.at[others], 2).wait_recv()
    to_sibling(mixed_stage, mixed_hbm.at[others], 4).wait_recv()


def backward(
    parts,
    dots,
    combs,
    grads,
    early_a,
    early_b,
    gates,
    middle,
    cot,
    tokens,
    gains,
    router,
    out_weight,
    heads_out,
    query,
    keys,
    values,
    normed,
    query_weight,
    keyvalue_weight,
    cosine,
    sine,
):
    owners = lax.axis_size("expert")
    chunks = lax.axis_size("dp")
    rows, columns = factors(chunks)
    half, feat_width = middle.shape
    local, _, height, units = grads.shape[2:]
    early = early_a.shape[1]
    piece = feat_width // (chunks * owners)
    heads, length, head_size = query.shape
    kv_heads = keys.shape[0]
    query_width, key_width = heads * head_size, kv_heads * head_size
    lanes = 128
    count = 24
    out_weight = out_weight.reshape(kv_heads, query_width // kv_heads, feat_width)
    bf16, f32 = jnp.bfloat16, jnp.float32
    hbm = pl.BlockSpec(memory_space=pl.ANY)
    vmem = pl.BlockSpec(memory_space=pltpu.VMEM)
    dma = pltpu.SemaphoreType.DMA
    most = max(rows, columns, owners) - 1

    def landings(tail, order, dtype):
        sizes = {"y": rows, "x": columns, "z": owners}
        left = ["y", "x", "z"]
        found = []
        for axis in order:
            left.remove(axis)
            found.append(
                pltpu.VMEM((sizes[axis] - 1,) + tuple(sizes[a] for a in left) + tail, dtype)
            )
        return found

    whole = (rows, columns, owners)
    return pl.pallas_call(
        functools.partial(back_kernel, rows, columns, owners),
        in_specs=[hbm] * 6 + [vmem] + [hbm] * 3 + [vmem] * 2 + [hbm] * 8 + [vmem, vmem],
        out_specs=[hbm] * 5 + [vmem] * 6,
        out_shape=[
            jax.ShapeDtypeStruct((2 * half, feat_width), bf16),
            jax.ShapeDtypeStruct((2 * half, feat_width), f32),
            jax.ShapeDtypeStruct((2, local, height, units), bf16),
            jax.ShapeDtypeStruct((rows - 1, local, height, units), bf16),
            jax.ShapeDtypeStruct((columns - 1, local, height, units), bf16),
            jax.ShapeDtypeStruct((piece, query_width), f32),
            jax.ShapeDtypeStruct((2, piece, key_width), f32),
            jax.ShapeDtypeStruct((piece, query_width), f32),
            jax.ShapeDtypeStruct((router.shape[0], piece), f32),
            jax.ShapeDtypeStruct((1, piece), f32),
            jax.ShapeDtypeStruct((1, piece), f32),
        ],
        scratch_shapes=[
            pltpu.VMEM((2, rows, height, units), bf16),
            pltpu.VMEM((2, columns, height, units), bf16),
            pltpu.VMEM((columns - 1, local, rows, height, units), bf16),
            pltpu.VMEM((rows - 1, local, columns, height, units), bf16),
            pltpu.VMEM((owners, half, feat_width), bf16),
            pltpu.VMEM((owners - 1, half, feat_width), bf16),
            pltpu.VMEM((owners - 1, half, feat_width), bf16),
            pltpu.VMEM(whole + (piece, query_width // 2), bf16),
            *landings((piece, query_width // 2), "zxy", bf16),
            pltpu.VMEM(whole + (piece, query_width // 2), bf16),
            *landings((piece, query_width // 2), "yxz", bf16),
            pltpu.VMEM(whole + (piece, query_width // 2), bf16),
            *landings((piece, query_width // 2), "xyz", bf16),
            pltpu.VMEM(whole + (piece, key_width), bf16),
            *landings((piece, key_width), "yxz", bf16),
            pltpu.VMEM(whole + (piece, query_width // 2), bf16),
            *landings((piece, query_width // 2), "yxz", bf16),
            pltpu.VMEM(whole + (piece, key_width), bf16),
            *landings((piece, key_width), "xyz", bf16),
            pltpu.VMEM((count, feat_width), f32),
            pltpu.VMEM((count, feat_width), f32),
            pltpu.VMEM(whole + (count, lanes), f32),
            *landings((count, lanes), "zxy", f32),
            pltpu.VMEM((2 * half, feat_width), bf16),
            pltpu.VMEM((half, feat_width), f32),
            pltpu.VMEM((kv_heads, length, query_width // kv_heads), bf16),
            pltpu.VMEM((2, kv_heads, length, head_size), bf16),
            pltpu.VMEM((half, feat_width), bf16),
            pltpu.VMEM((half, feat_width), bf16),
            pltpu.VMEM((half, feat_width), bf16),
            dma((9,)),
            dma((2, local)),
            dma((2, local)),
            dma((2, early)),
            dma((2, most, local)),
            dma((2, most, local)),
            dma((2, most, local)),
            dma((2, most, local)),
            dma((owners,)),
            dma((2, owners)),
            dma((2, owners)),
            dma((7, 3, most)),
            dma((7, 3, most)),
            dma((5,)),
            dma((5,)),
            dma((2,)),
        ],
        compiler_params=pltpu.CompilerParams(
            vmem_limit_bytes=60 * 2**20, collective_id=1, has_side_effects=True
        ),
        cost_estimate=pl.CostEstimate(
            flops=12 * 2**30, bytes_accessed=60 * 2**20, transcendentals=heads * length * length
        ),
    )(
        parts,
        dots,
        combs,
        grads,
        early_a,
        early_b,
        gates,
        middle,
        cot,
        tokens,
        gains,
        router,
        out_weight,
        heads_out,
        query,
        keys,
        values,
        normed,
        query_weight,
        keyvalue_weight,
        cosine,
        sine,
    )


def finish_body(large, kept_a, kept_b, second_a, second_b, *refs):
    count = (len(refs) - 4 - large) // 2
    sources, gateup_out, down_out = refs[:count], refs[count], refs[count + 1]
    targets, held = refs[count + 2 : 2 * count + 2], refs[2 * count + 2 : -2]
    load_sem, store_sem = refs[-2:]
    step = pl.program_id(0)
    steps = pl.num_programs(0)
    width = gateup_out.shape[2]
    loads = [
        pltpu.make_async_copy(sources[at], held[at], load_sem.at[at]) for at in range(large)
    ]
    stores = [
        pltpu.make_async_copy(held[at], targets[at], store_sem.at[at]) for at in range(large)
    ]

    @pl.when(step == 0)
    def _():
        for copy in loads:
            copy.start()
        for at in range(large, count):
            targets[at][...] = sources[at][...]

    @pl.when(step == 1)
    def _():
        for load, store in zip(loads, stores):
            load.wait()
            store.start()

    turned = []
    for part, (kept, second) in enumerate(((kept_a, second_a), (kept_b, second_b))):
        value = kept[0, 0].astype(jnp.float32)
        for other in range(second.shape[0]):
            value = value + second[other, 0].astype(jnp.float32)
        gateup_out[0, part] = value[:width]
        turned.append(value[width:])
    down_out[0] = jnp.concatenate(turned, axis=0).T

    @pl.when(step == steps - 1)
    def _():
        for copy in stores:
            copy.wait()


def finish(kept, second_a, second_b, *wholes):
    _, local, height, units = kept.shape
    width = 2 * height // 3
    large = 2
    spaces = [pl.BlockSpec(memory_space=pl.ANY)] * large
    spaces += [pl.BlockSpec(memory_space=pltpu.VMEM)] * (len(wholes) - large)

    def piece(count, at):
        return pl.BlockSpec((count, 1, height, units), lambda step: (at, step, 0, 0))

    return pl.pallas_call(
        functools.partial(finish_body, large),
        grid=(local,),
        in_specs=[
            piece(1, 0),
            piece(1, 1),
            piece(second_a.shape[0], 0),
            piece(second_b.shape[0], 0),
        ]
        + spaces,
        out_specs=[
            pl.BlockSpec((1, 2, width, units), lambda step: (step, 0, 0, 0)),
            pl.BlockSpec((1, units, width), lambda step: (step, 0, 0)),
        ]
        + spaces,
        out_shape=[
            jax.ShapeDtypeStruct((local, 2, width, units), jnp.float32),
            jax.ShapeDtypeStruct((local, units, width), jnp.float32),
        ]
        + [jax.ShapeDtypeStruct(w.shape, w.dtype) for w in wholes],
        scratch_shapes=[pltpu.VMEM(w.shape, w.dtype) for w in wholes[:large]]
        + [pltpu.SemaphoreType.DMA((large,)), pltpu.SemaphoreType.DMA((large,))],
        compiler_params=pltpu.CompilerParams(vmem_limit_bytes=60 * 2**20),
    )(kept, kept, second_a, second_b, *wholes)


def per_device(
    tokens,
    out_grad,
    attn_gain,
    query_weight,
    key_value_weight,
    output_weight,
    expert_gain,
    router_weight,
    gateup_weight,
    down_weight,
    routes,
):
    cosine, sine = rotary_tables()
    gains = jnp.stack([attn_gain, expert_gain])
    parts, dots, combs, gates, grads, early_a, early_b, _, _, normed, *kept = experts(
        tokens,
        out_grad,
        routes.T,
        gains,
        cosine,
        sine,
        router_weight.T,
        query_weight,
        key_value_weight,
        output_weight,
        gateup_weight,
        down_weight,
    )
    query, keys, values, heads_out, middle = kept
    mixed, tokens_grad, kept, second_a, second_b, *small = backward(
        parts,
        dots,
        combs,
        grads,
        early_a,
        early_b,
        gates,
        middle,
        out_grad,
        tokens,
        gains,
        router_weight.T,
        output_weight,
        heads_out,
        query,
        keys,
        values,
        normed,
        query_weight,
        key_value_weight,
        cosine,
        sine,
    )
    (
        gateup_total,
        down_total,
        mixed,
        tokens_grad,
        query_total,
        keyvalue_total,
        output_total,
        router_total,
        expert_gain_total,
        attn_gain_total,
    ) = finish(kept, second_a, second_b, mixed, tokens_grad, *small)
    return (
        mixed,
        tokens_grad,
        attn_gain_total[0],
        query_total,
        keyvalue_total,
        output_total.T,
        expert_gain_total[0],
        router_total.T,
        gateup_total,
        down_total,
    )


def solution(mesh):
    placed = (
        P(("dp", "expert"), None),
        P(("dp", "expert"), None),
        P(),
        P(None, "tensor"),
        P(None, None, "tensor"),
        P("tensor", None),
        P(),
        P(),
        P("expert", None, None, "tensor"),
        P("expert", "tensor", None),
        P(("dp", "expert"), None),
    )
    return jax.shard_map(
        per_device,
        mesh=mesh,
        in_specs=placed,
        out_specs=(
            P(("dp", "expert"), None),
            P(("dp", "expert"), None),
            P(("dp", "expert")),
            P(("dp", "expert"), "tensor"),
            P(None, ("dp", "expert"), "tensor"),
            P("tensor", ("dp", "expert")),
            P(("dp", "expert")),
            P(("dp", "expert"), None),
            P("expert", None, "dp", "tensor"),
            P("expert", "tensor", "dp"),
        ),
        check_vma=False,
    )
```

```python
import functools

import jax
import jax.numpy as jnp
import numpy as np
from jax import lax
from jax.experimental import pallas as pl
from jax.experimental.pallas import tpu as pltpu
from jax.sharding import PartitionSpec as P

HEAD_SIZE = 64
TOPK = 8
SEQUENCE_LENGTH = 512


EPSILON = 1e-06
RESIDUAL = 0.22
ATTN_SCALE = 0.015625
ROPE_BASE = 10000.0
NEGATIVE = -1e30
COT_STEPS = {1: (2,)}
EARLY = 2


def rotary_tables():
    half_dim = HEAD_SIZE // 2
    frequency = ROPE_BASE ** (-np.arange(half_dim, dtype=np.float32) * 2.0 / HEAD_SIZE)
    angles = np.arange(SEQUENCE_LENGTH, dtype=np.float32)[:, None] * frequency[None, :]
    angles = angles.astype(np.float32)
    cosine, sine = np.cos(angles), np.sin(angles)
    return (
        jnp.asarray(np.concatenate([cosine, cosine], axis=1), jnp.float32),
        jnp.asarray(np.concatenate([sine, -sine], axis=1), jnp.float32),
    )


def norm_parts(values):
    inv_rms = lax.rsqrt(jnp.mean(values * values, axis=-1, keepdims=True) + EPSILON)
    return values * inv_rms, inv_rms


def factors(count):
    low = 1 << ((count.bit_length() - 1) // 2)
    return count // low, low


class Place:
    def __init__(self, rows, columns, owners):
        self.sizes = {"y": rows, "x": columns, "z": owners}
        index = lax.axis_index("dp")
        self.at = {"y": index // columns, "x": index % columns, "z": lax.axis_index("expert")}

    def peer(self, axis, shift):
        return lax.rem(self.at[axis] + shift, self.sizes[axis])

    def device(self, axis, to):
        if axis == "z":
            return {"expert": to}
        if axis == "x":
            return {"dp": self.at["y"] * self.sizes["x"] + to}
        return {"dp": to * self.sizes["x"] + self.at["x"]}


def picked(ref, position, index):
    return ref.at[(slice(None),) * position + (index,)]


def contract(left, right, left_dim, right_dim):
    return lax.dot_general(
        left, right, (((left_dim,), (right_dim,)), ((), ())), preferred_element_type=jnp.float32
    )


def block_order(me, count, turn):
    block, unit = 0, 1
    while unit < count:
        block = block + unit * ((me // unit + turn // unit) % 2)
        unit *= 2
    return block


def expert_kernel(
    rows,
    columns,
    owners,
    local,
    early,
    tokens_hbm,
    cot_hbm,
    routes_ref,
    gains_ref,
    cosine_ref,
    sine_ref,
    router_ref,
    query_weight_hbm,
    keyvalue_weight_hbm,
    out_weight_hbm,
    gateup_hbm,
    down_hbm,
    parts_hbm,
    dots_hbm,
    comb_hbm,
    gates_out,
    grads_hbm,
    early_a,
    early_b,
    act_hbm,
    hidden_hbm,
    normed_hbm,
    query_hbm,
    key_hbm,
    value_hbm,
    heads_hbm,
    middle_hbm,
    rows_all,
    cot_all,
    hits_all,
    gateup_ref,
    down_ref,
    router_wide,
    half_send,
    half_land,
    gates_ref,
    send_grad,
    send_comb,
    send_dots,
    recv_grad,
    recv_comb,
    recv_dots,
    relay,
    load_sem,
    keep_sem,
    half_sem,
    weight_sem,
    chain_send,
    chain_recv,
    swap_send,
    swap_recv,
    sums_send,
    grad_recv,
    comb_recv,
    dots_recv,
    back_send,
    back_recv,
    dots_send,
    dots_back,
    hits_send,
    hits_recv,
    relay_sem,
    comb_sem,
    stage_sem,
    early_send,
    early_recv,
    dots_sem,
    grads_sem,
):
    place = Place(rows, columns, owners)
    me = lax.axis_index("expert")
    core = lax.axis_index("tensor")
    sibling = {"tensor": 1 - core}
    total, feat_width = rows_all.shape[1], rows_all.shape[2]
    half = total // 2
    units = down_ref.shape[0] // local
    lanes = gates_ref.shape[1]
    mine = pl.ds(pl.multiple_of(core * half, half), half)
    others = pl.ds(pl.multiple_of((1 - core) * half, half), half)

    barrier = pltpu.get_barrier_semaphore()
    pl.semaphore_signal(barrier, inc=1, device_id=sibling, device_id_type=pl.DeviceIdType.MESH)
    peers = 1
    for axis in ("x", "y", "z"):
        for shift in range(1, place.sizes[axis]):
            pl.semaphore_signal(
                barrier,
                inc=1,
                device_id=place.device(axis, place.peer(axis, shift)),
                device_id_type=pl.DeviceIdType.MESH,
            )
            peers += 1

    def remote(src, dst, send, recv, device):
        return pltpu.make_async_remote_copy(
            src_ref=src,
            dst_ref=dst,
            send_sem=send,
            recv_sem=recv,
            device_id=device,
            device_id_type=pl.DeviceIdType.MESH,
        )

    own_cot = pltpu.make_async_copy(cot_hbm, cot_all.at[me], load_sem.at[0])
    own_cot.start()
    number_of = lax.broadcasted_iota(jnp.int32, (lanes, total), 0)
    hits = number_of == routes_ref[0:1]
    for pick in range(1, routes_ref.shape[0]):
        hits = hits | (number_of == routes_ref[pick : pick + 1])
    hits_all[me] = jnp.where(hits, 1.0, 0.0).astype(jnp.bfloat16)
    experts_named = router_ref.shape[0]
    router_wide[...] = jnp.concatenate(
        [
            router_ref[...].astype(jnp.float32),
            jnp.zeros((lanes - experts_named, feat_width), jnp.float32),
        ],
        axis=0,
    ).astype(jnp.bfloat16)

    buffers = (rows_all, cot_all)

    def hits_copy(shift):
        return remote(
            hits_all.at[me],
            hits_all.at[me],
            hits_send.at[shift - 1],
            hits_recv.at[me],
            place.device("z", place.peer("z", shift)),
        )

    def hits_arrival(block):
        return remote(
            hits_all.at[block],
            hits_all.at[block],
            hits_send.at[0],
            hits_recv.at[block],
            sibling,
        )

    def chain(step, what, side):
        block = me - side * (step - 1)
        to = me + side
        there = (block >= 0) & (block < owners) & (to >= 0) & (to < owners)
        safe = jnp.clip(block, 0, owners - 1)
        at = 0 if side == 1 else 1
        copy = remote(
            buffers[what].at[safe, mine],
            buffers[what].at[safe, mine],
            chain_send.at[what, step - 1, at],
            chain_recv.at[what, safe],
            {"expert": jnp.clip(to, 0, owners - 1)},
        )
        return there, copy

    def swap(what, block):
        return remote(
            buffers[what].at[block, mine],
            buffers[what].at[block, mine],
            swap_send.at[what, block],
            swap_recv.at[what, block],
            sibling,
        )

    def swap_arrival(what, block):
        return remote(
            buffers[what].at[block, others],
            buffers[what].at[block, others],
            swap_send.at[what, block],
            swap_recv.at[what, block],
            sibling,
        )

    def send_step(step, what):
        for side in (1, -1):
            there, copy = chain(step, what, side)

            @pl.when(there)
            def _():
                copy.start()

    def arrivals(step, what):
        for side in (1, -1):
            block = me - side * step
            there = (block >= 0) & (block < owners)
            safe = jnp.clip(block, 0, owners - 1)

            @pl.when(there)
            def _():
                chain_copy = remote(
                    buffers[what].at[safe, mine],
                    buffers[what].at[safe, mine],
                    chain_send.at[what, step - 1, 0],
                    chain_recv.at[what, safe],
                    sibling,
                )
                chain_copy.wait_recv()

        if step + 1 < owners:
            send_step(step + 1, what)
        for side in (1, -1):
            block = me - side * step
            there = (block >= 0) & (block < owners)
            safe = jnp.clip(block, 0, owners - 1)

            @pl.when(there)
            def _():
                swap(what, safe).start()

    heads, length, head_size = query_hbm.shape
    kv_heads = key_hbm.shape[0]
    groups = heads // kv_heads
    tile = 64

    def part_of(expert, part):
        return pl.ds(pl.multiple_of((2 * expert + part) * units, units), units)

    def both_of(expert):
        return pl.ds(pl.multiple_of(2 * expert * units, 2 * units), 2 * units)

    def own_of(expert):
        return pl.ds(pl.multiple_of(expert * units, units), units)

    def weight_loads(expert):
        return [
            pltpu.make_async_copy(
                gateup_hbm.at[expert, part],
                gateup_ref.at[:, part_of(expert, part)],
                weight_sem.at[part, expert],
            )
            for part in range(2)
        ] + [
            pltpu.make_async_copy(
                down_hbm.at[expert], down_ref.at[own_of(expert)], weight_sem.at[2, expert]
            )
        ]

    def attention_phase(
        tokens, query_weight, keyvalue_weight, out_weight, normed, query, key, value, group_out, heads_out, partial, middle
    ):
        load_tokens = pltpu.make_async_copy(tokens_hbm, tokens, load_sem.at[1])
        loads = (
            pltpu.make_async_copy(query_weight_hbm, query_weight, load_sem.at[2]),
            pltpu.make_async_copy(keyvalue_weight_hbm, keyvalue_weight, load_sem.at[3]),
            pltpu.make_async_copy(out_weight_hbm, out_weight, load_sem.at[4]),
        )
        keeps = (
            pltpu.make_async_copy(normed, normed_hbm, keep_sem.at[0]),
            pltpu.make_async_copy(query, query_hbm, keep_sem.at[1]),
            pltpu.make_async_copy(key, key_hbm, keep_sem.at[2]),
            pltpu.make_async_copy(value, value_hbm, keep_sem.at[3]),
            pltpu.make_async_copy(heads_out, heads_hbm, keep_sem.at[4]),
            pltpu.make_async_copy(middle, middle_hbm, keep_sem.at[5]),
        )
        load_tokens.start()
        for copy in loads:
            copy.start()
        for expert in range(local):
            for copy in weight_loads(expert):
                copy.start()
        own_cot.wait()
        pl.semaphore_wait(barrier, peers)
        send_step(1, 1)
        for shift in range(1, owners):
            hits_copy(shift).start()
        load_tokens.wait()

        def first_norm(step, carry):
            at = pl.ds(pl.multiple_of(step * tile, tile), tile)
            unit, _ = norm_parts(tokens[at].astype(jnp.float32))
            normed[at] = (unit * gains_ref[0:1]).astype(jnp.bfloat16)
            return carry

        lax.fori_loop(0, total // tile, first_norm, 0)
        keeps[0].start()

        def turned(values):
            swapped = jnp.concatenate(
                [values[:, head_size // 2 :], values[:, : head_size // 2]], axis=1
            )
            return (values * cosine_ref[...] - swapped * sine_ref[...]).astype(jnp.bfloat16)

        loads[0].wait()
        projected = jnp.dot(normed[...], query_weight[...], preferred_element_type=jnp.float32)
        for head in range(heads):
            query[head] = turned(projected[:, head * head_size : (head + 1) * head_size])
        loads[1].wait()
        projected = jnp.dot(normed[...], keyvalue_weight[0], preferred_element_type=jnp.float32)
        for head in range(kv_heads):
            key[head] = turned(projected[:, head * head_size : (head + 1) * head_size])
        projected = jnp.dot(normed[...], keyvalue_weight[1], preferred_element_type=jnp.float32)
        for head in range(kv_heads):
            value[head] = projected[:, head * head_size : (head + 1) * head_size].astype(
                jnp.bfloat16
            )
        for copy in keeps[1:4]:
            copy.start()
        causal = length // 2

        def body(group, carry):
            keys, values = key[group], value[group]
            found = []
            for member in range(groups):
                some = query[group * groups + member]
                pieces = []
                for start in (0, causal):
                    stop = start + causal
                    scores = contract(some[start:stop], keys[:stop], 1, 1) * ATTN_SCALE
                    row = start + lax.broadcasted_iota(jnp.int32, scores.shape, 0)
                    col = lax.broadcasted_iota(jnp.int32, scores.shape, 1)
                    scores = jnp.where(row >= col, scores, NEGATIVE)
                    raised = jnp.exp(scores - jnp.max(scores, axis=1, keepdims=True))
                    probs = raised * (1.0 / jnp.sum(raised, axis=1, keepdims=True))
                    pieces.append(
                        jnp.dot(
                            probs.astype(jnp.bfloat16),
                            values[:stop],
                            preferred_element_type=jnp.float32,
                        )
                    )
                found.append(jnp.concatenate(pieces, axis=0))
            group_out[group] = jnp.concatenate(found, axis=1).astype(jnp.bfloat16)

            @pl.when(group == kv_heads - 1)
            def _():
                arrivals(1, 1)

            return carry

        lax.fori_loop(0, kv_heads, body, 0)
        heads_out[...] = jnp.concatenate([group_out[g] for g in range(kv_heads)], axis=1)
        keeps[4].start()
        loads[2].wait()
        half_send[...] = jnp.dot(
            heads_out[others], out_weight[...], preferred_element_type=jnp.float32
        ).astype(jnp.bfloat16)
        half_copy = remote(half_send, half_land, half_sem.at[0], half_sem.at[1], sibling)
        half_copy.start()
        partial[...] = jnp.dot(
            heads_out[mine], out_weight[...], preferred_element_type=jnp.float32
        )
        half_copy.wait()

        def second_norm(step, carry):
            at = pl.ds(pl.multiple_of(step * tile, tile), tile)
            to = pl.ds(pl.multiple_of(core * half + step * tile, tile), tile)
            after = tokens[to].astype(jnp.float32) + RESIDUAL * (
                partial[at] + half_land[at].astype(jnp.float32)
            )
            middle[at] = after
            unit, _ = norm_parts(after)
            rows_all[me, to] = (unit * gains_ref[1:2]).astype(jnp.bfloat16)
            return carry

        lax.fori_loop(0, half // tile, second_norm, 0)
        swap(0, me).start()
        send_step(1, 0)
        keeps[5].start()
        for copy in keeps:
            copy.wait()

    pl.run_scoped(
        attention_phase,
        pltpu.VMEM((total, feat_width), jnp.bfloat16),
        pltpu.VMEM(query_weight_hbm.shape, jnp.bfloat16),
        pltpu.VMEM(keyvalue_weight_hbm.shape, jnp.bfloat16),
        pltpu.VMEM(out_weight_hbm.shape, jnp.bfloat16),
        pltpu.VMEM((total, feat_width), jnp.bfloat16),
        pltpu.VMEM(query_hbm.shape, jnp.bfloat16),
        pltpu.VMEM(key_hbm.shape, jnp.bfloat16),
        pltpu.VMEM(value_hbm.shape, jnp.bfloat16),
        pltpu.VMEM((kv_heads, total, groups * head_size), jnp.bfloat16),
        pltpu.VMEM(heads_hbm.shape, jnp.bfloat16),
        pltpu.VMEM((half, feat_width), jnp.float32),
        pltpu.VMEM((half, feat_width), jnp.float32),
    )

    width = feat_width // (rows * columns)
    inside = min(early, 2)

    def term_loads(act, hidden, slot, expert, turns):
        some = pl.ds(turns[0], len(turns))
        return (
            pltpu.make_async_copy(act_hbm.at[expert, some], act.at[slot], dots_sem.at[0, slot]),
            pltpu.make_async_copy(
                hidden_hbm.at[expert, some], hidden.at[slot], dots_sem.at[1, slot]
            ),
        )

    def weight_grads(terms, grads):
        up_sum = sum(
            contract(rows_all[block_order(me, owners, turn)], hidden[...], 0, 0)
            for _, hidden, turn in terms
        ).astype(jnp.bfloat16)
        down_sum = sum(
            contract(act[...], cot_all[block_order(me, owners, turn)], 0, 0)
            for act, _, turn in terms
        )
        down_sum = (RESIDUAL * down_sum).T.astype(jnp.bfloat16)
        for y in range(rows):
            for x in range(columns):
                start = (y * columns + x) * width
                for part in range(2):
                    grads[y, x, part, :width] = up_sum[
                        start : start + width, part * units : (part + 1) * units
                    ]
                    at = start + part * (width // 2)
                    grads[y, x, part, width:] = down_sum[at : at + width // 2]

    def store_grads(grads, expert, slot):
        return pltpu.make_async_copy(grads, grads_hbm.at[:, :, expert], grads_sem.at[slot])

    def early_copies(grads, expert):
        found = []
        for part, axis, landing in ((0, "x", early_a), (1, "y", early_b)):
            for shift in range(1, place.sizes[axis]):
                to = place.peer(axis, shift)
                found.append(
                    remote(
                        grads.at[:, to, part] if axis == "x" else grads.at[to, :, part],
                        landing.at[shift - 1, expert],
                        early_send.at[part, shift - 1, expert],
                        early_recv.at[part, shift - 1, expert],
                        place.device(axis, to),
                    )
                )
        return found

    relays = owners == 4
    middle_owner = (me > 0) & (me < owners - 1)

    def goes_back(turn):
        if not relays:
            return turn > 0
        return ((turn != 1) & (turn != 2)) | ~middle_owner

    def back_copy(turn):
        return remote(
            recv_grad.at[turn],
            parts_hbm.at[turn],
            back_send.at[turn],
            back_recv.at[turn],
            {"expert": block_order(me, owners, turn)},
        )

    def dots_copy(turn):
        return remote(
            recv_dots.at[turn],
            dots_hbm.at[turn],
            dots_send.at[turn],
            dots_back.at[turn],
            {"expert": block_order(me, owners, turn)},
        )

    def relay_copy():
        return remote(
            recv_grad.at[2],
            relay,
            relay_sem.at[0],
            relay_sem.at[1],
            {"expert": block_order(me, owners, 3)},
        )

    def expert_phase(
        dot_sum, hold_comb, hold_grad, hold_dot, act_block, hidden_block, act_terms, hidden_terms, grads
    ):
        lane = lax.broadcasted_iota(jnp.int32, (total, lanes), 1)

        def stage_copies(expert, turn):
            return (
                pltpu.make_async_copy(
                    act_block.at[:, own_of(expert)],
                    act_hbm.at[expert, turn],
                    stage_sem.at[0, expert],
                ),
                pltpu.make_async_copy(
                    hidden_block.at[:, both_of(expert)],
                    hidden_hbm.at[expert, turn],
                    stage_sem.at[1, expert],
                ),
            )

        def sums_copies(turn):
            return (
                remote(send_grad, recv_grad.at[turn], sums_send.at[0], grad_recv.at[turn], sibling),
                remote(send_comb, recv_comb.at[turn], sums_send.at[1], comb_recv.at[turn], sibling),
                remote(send_dots, recv_dots.at[turn], sums_send.at[2], dots_recv.at[turn], sibling),
            )

        def own_back():
            return (
                pltpu.make_async_copy(recv_grad.at[0], parts_hbm.at[0], back_send.at[0]),
                pltpu.make_async_copy(recv_dots.at[0], dots_hbm.at[0], dots_send.at[0]),
            )

        def comb_copy(turn, block):
            return pltpu.make_async_copy(
                recv_comb.at[turn],
                comb_hbm.at[lax.rem(block - me + owners, owners)],
                comb_sem.at[turn],
            )

        def settle(turn):
            block = block_order(me, owners, turn)
            copy_grad, copy_comb, copy_dots = sums_copies(turn)
            copy_dots.wait_recv()
            recv_dots[turn] = hold_dot[...] + recv_dots[turn]
            copy_grad.wait_recv()
            recv_grad[turn] = (
                hold_grad[...] + recv_grad[turn].astype(jnp.float32)
            ).astype(jnp.bfloat16)

            @pl.when(turn > 0)
            def _():
                dots_copy(turn).start()

            @pl.when((turn > 0) & goes_back(turn))
            def _():
                back_copy(turn).start()

            if relays:

                @pl.when((turn == 2) & middle_owner)
                def _():
                    relay_copy().start()

            @pl.when(turn == 0)
            def _():
                for copy in own_back():
                    copy.start()

            copy_comb.wait_recv()
            recv_comb[turn] = (hold_comb[...] + recv_comb[turn].astype(jnp.float32)).astype(
                jnp.bfloat16
            )
            comb_copy(turn, block).start()

        last = (owners - 1) * local

        def body(number, carry):
            turn = number // local
            expert = number % local
            block = block_order(me, owners, turn)

            @pl.when(expert == 0)
            def _():
                swap_arrival_needed = turn > 0

                @pl.when(swap_arrival_needed)
                def _():
                    swap_arrival(1, block).wait_recv()
                    hits_arrival(block).wait_recv()

                swap_arrival(0, block).wait_recv()
                hits = hits_all[block].astype(jnp.float32).T > 0.5
                logits = contract(rows_all[block], router_wide[...], 1, 1)
                logits = jnp.where(hits, logits, NEGATIVE)
                raised = jnp.where(
                    hits, jnp.exp(logits - jnp.max(logits, axis=1, keepdims=True)), 0.0
                )
                gates_ref[...] = raised / jnp.sum(raised, axis=1, keepdims=True)

                @pl.when(turn == 0)
                def _():
                    gates_out[...] = gates_ref[mine]

            @pl.when(number < local)
            def _():
                for copy in weight_loads(expert):
                    copy.wait()

            @pl.when((turn > 0) & (number < last))
            def _():
                for copy in stage_copies(expert, turn):
                    copy.wait()

            chosen = rows_all[block]
            gate_part = jnp.dot(
                chosen, gateup_ref[:, part_of(expert, 0)], preferred_element_type=jnp.float32
            )
            up_part = jnp.dot(
                chosen, gateup_ref[:, part_of(expert, 1)], preferred_element_type=jnp.float32
            )
            raw = contract(cot_all[block], down_ref[own_of(expert)], 1, 1)
            here = lane == me * local + expert
            weight = jnp.sum(jnp.where(here, gates_ref[...], 0.0), axis=1, keepdims=True)
            sigmoid_gate = 0.5 * jnp.tanh(0.5 * gate_part) + 0.5
            silu_gate = gate_part * sigmoid_gate
            activation = silu_gate * up_part
            dots = jnp.where(here, jnp.sum(activation * raw, axis=1, keepdims=True), 0.0)
            weighted = (activation * weight).astype(jnp.bfloat16)
            act_block[:, own_of(expert)] = weighted
            grad_act = raw * (RESIDUAL * weight)
            grad_gatepart = (
                grad_act * up_part * (sigmoid_gate * (1.0 + gate_part * (1.0 - sigmoid_gate)))
            ).astype(jnp.bfloat16)
            grad_uppart = (grad_act * silu_gate).astype(jnp.bfloat16)
            hidden_block[:, part_of(expert, 0)] = grad_gatepart
            hidden_block[:, part_of(expert, 1)] = grad_uppart
            for copy in stage_copies(expert, turn):
                copy.start()

            @pl.when(expert == 0)
            def _():
                dot_sum[...] = dots

            @pl.when(expert > 0)
            def _():
                dot_sum[...] += dots

            @pl.when((expert == 1) & (turn > 0) & (turn < owners - 1))
            def _():
                settle(turn - 1)

            for step in range(1, owners - 1):

                @pl.when(number == step * local - 2)
                def _():
                    for late in COT_STEPS.get(step, ()):
                        arrivals(late, 1)
                    arrivals(step, 0)

            @pl.when(expert == local - 1)
            def _():
                @pl.when(turn > 0)
                def _():
                    for copy in sums_copies(turn):
                        copy.wait_send()

                def grad_of(some):
                    return contract(hidden_block[some], gateup_ref[...], 1, 1)

                def comb_of(some):
                    return jnp.dot(
                        act_block[some], down_ref[...], preferred_element_type=jnp.float32
                    )

                send_grad[...] = grad_of(others).astype(jnp.bfloat16)
                send_dots[...] = dot_sum[others].T
                send_comb[...] = comb_of(others).astype(jnp.bfloat16)
                for copy in sums_copies(turn):
                    copy.start()
                hold_grad[...] = grad_of(mine)
                hold_comb[...] = comb_of(mine)
                hold_dot[...] = dot_sum[mine].T

            return carry

        lax.fori_loop(0, last, body, 0)
        settle(owners - 2)
        for expert in range(local):
            for copy in stage_copies(expert, 0):
                copy.wait()
        earlier = range(owners - 1)
        for copy in term_loads(act_terms, hidden_terms, 0, 0, earlier):
            copy.start()
        for step in range(2, owners):
            if not any(step in late for late in COT_STEPS.values()):
                arrivals(step, 1)
        arrivals(owners - 1, 0)


        def with_weights(expert, carry):
            body(last + expert, carry)
            for copy in term_loads(act_terms, hidden_terms, 0, expert, earlier):
                copy.wait()
            terms = [
                (act_terms.at[0, turn], hidden_terms.at[0, turn], turn) for turn in earlier
            ] + [
                (
                    act_block.at[:, own_of(expert)],
                    hidden_block.at[:, both_of(expert)],
                    owners - 1,
                )
            ]
            weight_grads(terms, grads.at[expert % 2])
            store_grads(grads.at[expert % 2], expert, expert % 2).start()
            for copy in early_copies(grads.at[expert % 2], expert):
                copy.start()

            @pl.when(expert + 1 < inside)
            def _():
                for copy in term_loads(act_terms, hidden_terms, 0, expert + 1, earlier):
                    copy.start()

            return carry

        lax.fori_loop(0, inside, with_weights, 0)
        lax.fori_loop(last + inside, owners * local, body, 0)
        settle(owners - 1)
        if relays:

            @pl.when(middle_owner)
            def _():
                relay_copy().wait_recv()
                recv_grad[1] = (
                    recv_grad[1].astype(jnp.float32) + relay[...].astype(jnp.float32)
                ).astype(jnp.bfloat16)
                back_copy(1).start()

        for copy in sums_copies(owners - 1):
            copy.wait_send()
        for expert in range(local):
            for copy in stage_copies(expert, 0):
                copy.wait()
        for expert in range(inside):
            store_grads(grads.at[expert % 2], expert, expert % 2).wait()
            for copy in early_copies(grads.at[expert % 2], expert):
                copy.wait_send()
        for turn in range(owners):
            block = block_order(me, owners, turn)
            comb_copy(turn, block).wait()

    pl.run_scoped(
        expert_phase,
        pltpu.VMEM((total, lanes), jnp.float32),
        pltpu.VMEM((half, feat_width), jnp.float32),
        pltpu.VMEM((half, feat_width), jnp.float32),
        pltpu.VMEM((lanes, half), jnp.float32),
        pltpu.VMEM((total, local * units), jnp.bfloat16),
        pltpu.VMEM((total, 2 * local * units), jnp.bfloat16),
        pltpu.VMEM((1, owners - 1, total, units), jnp.bfloat16),
        pltpu.VMEM((1, owners - 1, total, 2 * units), jnp.bfloat16),
        pltpu.VMEM((2,) + grads_hbm.shape[:2] + grads_hbm.shape[3:], jnp.bfloat16),
    )

    def weights_phase(act, hidden, grads):
        turns = range(owners)

        def loads(expert):
            return term_loads(act, hidden, expert % 2, expert, turns)

        def sent(expert):
            store_grads(grads.at[expert % 2], expert, expert % 2).wait()

            @pl.when(expert < early)
            def _():
                for copy in early_copies(grads.at[expert % 2], expert):
                    copy.wait_send()

        for copy in loads(inside):
            copy.start()

        def body(expert, carry):
            slot = expert % 2

            @pl.when(expert + 1 < local)
            def _():
                for copy in loads(expert + 1):
                    copy.start()

            for copy in loads(expert):
                copy.wait()

            @pl.when(expert >= inside + 2)
            def _():
                sent(expert - 2)

            terms = [(act.at[slot, turn], hidden.at[slot, turn], turn) for turn in turns]
            weight_grads(terms, grads.at[slot])
            store_grads(grads.at[slot], expert, slot).start()

            @pl.when(expert < early)
            def _():
                for copy in early_copies(grads.at[slot], expert):
                    copy.start()

            return carry

        lax.fori_loop(inside, local, body, 0)
        for expert in range(max(inside, local - 2), local):
            sent(expert)

    pl.run_scoped(
        weights_phase,
        pltpu.VMEM((2, owners, total, units), jnp.bfloat16),
        pltpu.VMEM((2, owners, total, 2 * units), jnp.bfloat16),
        pltpu.VMEM((2,) + grads_hbm.shape[:2] + grads_hbm.shape[3:], jnp.bfloat16),
    )
    for expert in range(early):
        for copy in early_copies(grads_hbm.at[:, :, expert], expert):
            copy.wait_recv()

    swap(0, me).wait_send()
    for step in range(1, owners):
        for what in range(2):
            for side in (1, -1):
                there, copy = chain(step, what, side)

                @pl.when(there)
                def _():
                    copy.wait_send()

                block = me - side * step
                arrived = (block >= 0) & (block < owners)
                safe = jnp.clip(block, 0, owners - 1)

                @pl.when(arrived)
                def _():
                    swap(what, safe).wait_send()

    for shift in range(1, owners):
        hits_copy(shift).wait_send()
    pltpu.make_async_copy(recv_grad.at[0], parts_hbm.at[0], back_send.at[0]).wait()
    pltpu.make_async_copy(recv_dots.at[0], dots_hbm.at[0], dots_send.at[0]).wait()
    for turn in range(1, owners):
        dots_copy(turn).wait()
        if relays and turn == 1:
            back_copy(turn).wait()
        elif relays and turn == 2:

            @pl.when(middle_owner)
            def _():
                relay_copy().wait_send()
                back_copy(turn).wait_recv()

            @pl.when(~middle_owner)
            def _():
                back_copy(turn).wait_send()
                none = pltpu.make_async_copy(half_send, parts_hbm.at[turn], load_sem.at[0])
                half_send[...] = jnp.zeros_like(half_send)
                none.start()
                none.wait()

        else:
            back_copy(turn).wait()


def experts(
    tokens,
    cot,
    routes,
    gains,
    cosine,
    sine,
    router,
    query_weight,
    keyvalue_weight,
    out_weight,
    gateup,
    down,
):
    owners = lax.axis_size("expert")
    rows, columns = factors(lax.axis_size("dp"))
    total, feat_width = tokens.shape
    half = total // 2
    local, units = down.shape[0], down.shape[1]
    height = 3 * feat_width // (rows * columns) // 2
    early = min(EARLY, local)
    most = max(rows, columns) - 1
    lanes = 32
    heads = query_weight.shape[1] // HEAD_SIZE
    kv_heads = keyvalue_weight.shape[2] // HEAD_SIZE
    hbm = pl.BlockSpec(memory_space=pl.ANY)
    vmem = pl.BlockSpec(memory_space=pltpu.VMEM)
    bf16, f32 = jnp.bfloat16, jnp.float32
    dma = pltpu.SemaphoreType.DMA
    return pl.pallas_call(
        functools.partial(expert_kernel, rows, columns, owners, local, early),
        in_specs=[hbm, hbm] + [vmem] * 5 + [hbm] * 5,
        out_specs=[hbm, hbm, hbm, vmem] + [hbm] * 11,
        out_shape=[
            jax.ShapeDtypeStruct((owners, half, feat_width), bf16),
            jax.ShapeDtypeStruct((owners, lanes, half), f32),
            jax.ShapeDtypeStruct((owners, half, feat_width), bf16),
            jax.ShapeDtypeStruct((half, lanes), f32),
            jax.ShapeDtypeStruct((rows, columns, local, 2, height, units), bf16),
            jax.ShapeDtypeStruct((columns - 1, early, rows, height, units), bf16),
            jax.ShapeDtypeStruct((rows - 1, early, columns, height, units), bf16),
            jax.ShapeDtypeStruct((local, owners, total, units), bf16),
            jax.ShapeDtypeStruct((local, owners, total, 2 * units), bf16),
            jax.ShapeDtypeStruct((total, feat_width), bf16),
            jax.ShapeDtypeStruct((heads, total, HEAD_SIZE), bf16),
            jax.ShapeDtypeStruct((kv_heads, total, HEAD_SIZE), bf16),
            jax.ShapeDtypeStruct((kv_heads, total, HEAD_SIZE), bf16),
            jax.ShapeDtypeStruct((total, heads * HEAD_SIZE), bf16),
            jax.ShapeDtypeStruct((half, feat_width), f32),
        ],
        scratch_shapes=[
            pltpu.VMEM((owners, total, feat_width), bf16),
            pltpu.VMEM((owners, total, feat_width), bf16),
            pltpu.VMEM((owners, lanes, total), bf16),
            pltpu.VMEM((feat_width, 2 * local * units), bf16),
            pltpu.VMEM((local * units, feat_width), bf16),
            pltpu.VMEM((lanes, feat_width), bf16),
            pltpu.VMEM((half, feat_width), bf16),
            pltpu.VMEM((half, feat_width), bf16),
            pltpu.VMEM((total, lanes), f32),
            pltpu.VMEM((half, feat_width), bf16),
            pltpu.VMEM((half, feat_width), bf16),
            pltpu.VMEM((lanes, half), f32),
            pltpu.VMEM((owners, half, feat_width), bf16),
            pltpu.VMEM((owners, half, feat_width), bf16),
            pltpu.VMEM((owners, lanes, half), f32),
            pltpu.VMEM((half, feat_width), bf16),
            dma((5,)),
            dma((6,)),
            dma((2,)),
            dma((3, local)),
            dma((2, owners - 1, 2)),
            dma((2, owners)),
            dma((2, owners)),
            dma((2, owners)),
            dma((3,)),
            dma((owners,)),
            dma((owners,)),
            dma((owners,)),
            dma((owners,)),
            dma((owners,)),
            dma((owners,)),
            dma((owners,)),
            dma((owners - 1,)),
            dma((owners,)),
            dma((2,)),
            dma((owners,)),
            dma((2, local)),
            dma((2, most, early)),
            dma((2, most, early)),
            dma((2, 2)),
            dma((2,)),
        ],
        compiler_params=pltpu.CompilerParams(
            vmem_limit_bytes=60 * 2**20, collective_id=0, has_side_effects=True
        ),
        cost_estimate=pl.CostEstimate(
            flops=2 * owners * total * feat_width * units * 9 * local,
            bytes_accessed=80 * 2**20,
            transcendentals=owners * total * units * local,
        ),
    )(
        tokens,
        cot,
        routes,
        gains,
        cosine,
        sine,
        router,
        query_weight,
        keyvalue_weight,
        out_weight,
        gateup,
        down,
    )


class Summing:
    def __init__(self, place, source, axes, order, landing, send, recv):
        self.place, self.order, self.landing = place, order, landing
        self.send, self.recv = send, recv
        self.sources, self.positions = [source], []
        left = list(axes)
        for step, axis in enumerate(order):
            self.positions.append(left.index(axis))
            left.pop(self.positions[-1])
            self.sources.append(landing[step].at[0])

    def copies(self, step):
        axis = self.order[step]
        found = []
        for shift in range(1, self.place.sizes[axis]):
            to = self.place.peer(axis, shift)
            found.append(
                pltpu.make_async_remote_copy(
                    src_ref=picked(self.sources[step], self.positions[step], to),
                    dst_ref=self.landing[step].at[shift - 1],
                    send_sem=self.send.at[step, shift - 1],
                    recv_sem=self.recv.at[step, shift - 1],
                    device_id=self.place.device(axis, to),
                    device_id_type=pl.DeviceIdType.MESH,
                )
            )
        return found

    def start(self, step):
        for copy in self.copies(step):
            copy.start()

    def total(self, step):
        axis = self.order[step]
        for copy in self.copies(step):
            copy.wait_recv()
        own = picked(self.sources[step], self.positions[step], self.place.at[axis])
        value = own[...].astype(jnp.float32)
        for shift in range(1, self.place.sizes[axis]):
            value = value + self.landing[step][shift - 1].astype(jnp.float32)
        return value

    def forward(self, step):
        self.landing[step][0] = self.total(step).astype(self.landing[step].dtype)
        self.start(step + 1)

    def close(self):
        for step in range(len(self.order)):
            for copy in self.copies(step):
                copy.wait_send()


def norm_grad(grad, gain, unit, inv_rms):
    grad_unit = grad * gain
    return inv_rms * (grad_unit - unit * jnp.mean(grad_unit * unit, axis=-1, keepdims=True))


def back_kernel(
    rows,
    columns,
    owners,
    parts_hbm,
    dots_hbm,
    comb_hbm,
    grads_hbm,
    early_a,
    early_b,
    gates_ref,
    middle_hbm,
    cot_hbm,
    tokens_hbm,
    gains_ref,
    router_ref,
    out_weight_hbm,
    heads_hbm,
    query_hbm,
    key_hbm,
    value_hbm,
    normed_hbm,
    query_weight_hbm,
    keyvalue_weight_hbm,
    cosine_ref,
    sine_ref,
    mixed_hbm,
    tokens_grad_hbm,
    kept_hbm,
    second_a,
    second_b,
    query_out,
    keyvalue_out,
    output_out,
    router_out,
    expert_gain_out,
    attn_gain_out,
    own_a,
    own_b,
    first_a,
    first_b,
    comb_own,
    comb_left,
    comb_right,
    out_a,
    out_az,
    out_ax,
    out_ay,
    out_b,
    out_by,
    out_bx,
    out_bz,
    near_q,
    near_qx,
    near_qy,
    near_qz,
    near_kv,
    near_kvy,
    near_kvx,
    near_kvz,
    far_q,
    far_qy,
    far_qx,
    far_qz,
    far_kv,
    far_kvx,
    far_kvy,
    far_kvz,
    small_sum,
    small_swap,
    small_stage,
    small_z,
    small_x,
    small_y,
    grad_attn,
    grad_middle,
    grad_query,
    grad_keyvalue,
    half_send,
    half_land,
    mixed_stage,
    load_sem,
    own_sem,
    keep_sem,
    early_sem,
    first_send,
    first_recv,
    second_send,
    second_recv,
    comb_sem,
    comb_send,
    comb_recv,
    sum_send,
    sum_recv,
    swap_send,
    swap_recv,
    store_sem,
):
    place = Place(rows, columns, owners)
    core = lax.axis_index("tensor")
    sibling = {"tensor": 1 - core}
    half, feat_width = middle_hbm.shape
    local = grads_hbm.shape[2]
    early = early_a.shape[1]
    heads, length, head_size = query_hbm.shape
    kv_heads = key_hbm.shape[0]
    groups = heads // kv_heads
    query_width = heads * head_size
    key_width = kv_heads * head_size
    tile = 64
    mine = pl.ds(pl.multiple_of(core * half, half), half)
    others = pl.ds(pl.multiple_of((1 - core) * half, half), half)

    barrier = pltpu.get_barrier_semaphore()
    peers = [sibling]
    for axis in ("x", "y", "z"):
        for shift in range(1, place.sizes[axis]):
            peers.append(place.device(axis, place.peer(axis, shift)))
    for peer in peers:
        pl.semaphore_signal(barrier, inc=1, device_id=peer, device_id_type=pl.DeviceIdType.MESH)

    def to_sibling(src, dst, at):
        return pltpu.make_async_remote_copy(
            src_ref=src,
            dst_ref=dst,
            send_sem=swap_send.at[at],
            recv_sem=swap_recv.at[at],
            device_id=sibling,
            device_id_type=pl.DeviceIdType.MESH,
        )

    plans = (
        (0, "x", "y", own_a, first_a, second_a),
        (1, "y", "x", own_b, first_b, second_b),
    )

    def grads_of(part, axis, index, expert):
        if axis == "x":
            return grads_hbm.at[:, index, expert, part]
        return grads_hbm.at[index, :, expert, part]

    def own_load(plan, expert):
        part, axis, _, own, _, _ = plan
        return pltpu.make_async_copy(
            grads_of(part, axis, place.at[axis], expert),
            own.at[expert % 2],
            own_sem.at[part, expert],
        )

    def early_load(plan, expert):
        part, _, _, _, first, _ = plan
        source = (early_a, early_b)[part]
        return pltpu.make_async_copy(
            source.at[:, expert], first.at[:, expert], early_sem.at[part, expert]
        )

    def first_copies(plan, expert):
        part, axis, _, _, first, _ = plan
        found = []
        for shift in range(1, place.sizes[axis]):
            to = place.peer(axis, shift)
            found.append(
                pltpu.make_async_remote_copy(
                    src_ref=grads_of(part, axis, to, expert),
                    dst_ref=first.at[shift - 1, expert],
                    send_sem=first_send.at[part, shift - 1, expert],
                    recv_sem=first_recv.at[part, shift - 1, expert],
                    device_id=place.device(axis, to),
                    device_id_type=pl.DeviceIdType.MESH,
                )
            )
        return found

    def second_copies(plan, expert):
        part, _, axis, _, first, second = plan
        found = []
        for shift in range(1, place.sizes[axis]):
            to = place.peer(axis, shift)
            found.append(
                pltpu.make_async_remote_copy(
                    src_ref=first.at[0, expert, to],
                    dst_ref=second.at[shift - 1, expert],
                    send_sem=second_send.at[part, shift - 1, expert],
                    recv_sem=second_recv.at[part, shift - 1, expert],
                    device_id=place.device(axis, to),
                    device_id_type=pl.DeviceIdType.MESH,
                )
            )
        return found

    def first_sum(expert):
        for plan in plans:
            _, axis, after, own, first, _ = plan
            own_load(plan, expert).wait()

            @pl.when(expert < early)
            def _():
                early_load(plan, expert).wait()

            @pl.when(expert >= early)
            def _():
                for copy in first_copies(plan, expert):
                    copy.wait_recv()

            for index in range(place.sizes[after]):
                value = own[expert % 2, index].astype(jnp.float32)
                for shift in range(1, place.sizes[axis]):
                    value = value + first[shift - 1, expert, index].astype(jnp.float32)
                first[0, expert, index] = value.astype(first.dtype)

            @pl.when(expert + 2 < local)
            def _():
                own_load(plan, expert + 2).start()

    def keep(plan, expert):
        part, _, axis, _, first, _ = plan
        return pltpu.make_async_copy(
            first.at[0, expert, place.at[axis]],
            kept_hbm.at[part, expert],
            keep_sem.at[part, expert],
        )

    def start_first(expert, carry):
        for plan in plans:
            for copy in first_copies(plan, expert):
                copy.start()
        return carry

    held = local - 1
    for plan in plans:
        for expert in range(early):
            early_load(plan, expert).start()
        for expert in range(min(2, local)):
            own_load(plan, expert).start()

    me = place.at["z"]

    def comb_load(shift):
        return pltpu.make_async_copy(comb_hbm.at[shift], comb_own.at[shift], comb_sem.at[shift])

    def comb_copy(side, away):
        landing, at = (comb_right, 0) if side == 1 else (comb_left, 1)
        shift = away if side == 1 else owners - away
        to = jnp.clip(me + side, 0, owners - 1)
        return pltpu.make_async_remote_copy(
            src_ref=comb_own.at[shift],
            dst_ref=landing.at[away - 1],
            send_sem=comb_send.at[at, away],
            recv_sem=comb_recv.at[at, away - 1],
            device_id=place.device("z", to),
            device_id_type=pl.DeviceIdType.MESH,
        )

    def comb_arrival(side, away):
        landing, at = (comb_right, 0) if side == 1 else (comb_left, 1)
        from_ = jnp.clip(me - side, 0, owners - 1)
        return pltpu.make_async_remote_copy(
            src_ref=comb_own.at[0],
            dst_ref=landing.at[away],
            send_sem=comb_send.at[at, away],
            recv_sem=comb_recv.at[at, away],
            device_id=place.device("z", from_),
            device_id_type=pl.DeviceIdType.MESH,
        )

    def inside(at):
        return (at >= 0) & (at < owners)

    def comb_send_on(away):
        for side in (1, -1):

            @pl.when(inside(me + side * away))
            def _():
                comb_copy(side, away).start()

    def comb_add(away):
        for side in (1, -1):

            @pl.when(inside(me + side * away) & inside(me - side))
            def _():
                comb_arrival(side, away).wait_recv()
                landing = comb_right if side == 1 else comb_left
                shift = 0 if away == 0 else (away if side == 1 else owners - away)
                comb_own[shift] = (
                    comb_own[shift].astype(jnp.float32) + landing[away].astype(jnp.float32)
                ).astype(jnp.bfloat16)

    def comb_stage(away):
        comb_add(away)
        if away > 0:
            comb_send_on(away)

    def job(source, order, landing, at):
        return Summing(
            place, source, ("y", "x", "z"), order, landing, sum_send.at[at], sum_recv.at[at]
        )

    output_job_a = job(out_a, ("z", "x", "y"), (out_az, out_ax, out_ay), 0)
    output_job_b = job(out_b, ("y", "x", "z"), (out_by, out_bx, out_bz), 4)
    pair_jobs = (
        (
            job(near_q, ("x", "y", "z"), (near_qx, near_qy, near_qz), 1),
            job(near_kv, ("y", "x", "z"), (near_kvy, near_kvx, near_kvz), 2),
        ),
        (
            job(far_q, ("y", "x", "z"), (far_qy, far_qx, far_qz), 5),
            job(far_kv, ("x", "y", "z"), (far_kvx, far_kvy, far_kvz), 6),
        ),
    )
    pair_stages = ((near_q, near_kv), (far_q, far_kv))
    small_job = job(small_stage, ("z", "x", "y"), (small_z, small_x, small_y), 3)

    def weight_grad(stage, left, right):
        count = stage.shape[3]
        band = feat_width // 4
        for start in range(0, feat_width, band):
            value = contract(left[:, start : start + band], right, 0, 0).astype(jnp.bfloat16)
            for at in range(start, start + band, count):
                index = at // count
                y, x, z = (
                    index // (columns * owners),
                    index // owners % columns,
                    index % owners,
                )
                stage[y, x, z] = value[at - start : at - start + count]

    def middle_phase(parts, middle, cot_ref, dots_parts, dots_sum):
        loads = (
            pltpu.make_async_copy(dots_hbm, dots_parts, load_sem.at[0]),
            pltpu.make_async_copy(cot_hbm.at[mine], cot_ref, load_sem.at[3]),
            pltpu.make_async_copy(parts_hbm, parts, load_sem.at[1]),
            pltpu.make_async_copy(middle_hbm, middle, load_sem.at[2]),
        )
        for copy in loads:
            copy.start()
        pl.semaphore_wait(barrier, len(peers))
        lax.fori_loop(early, held, start_first, 0)
        for shift in range(owners):
            comb_load(shift).start()
        for copy in loads:
            copy.wait()
        small_sum[...] = jnp.zeros_like(small_sum)
        dots_sum[...] = sum(dots_parts[b] for b in range(owners)).T

        def body(step, carry):
            at = pl.ds(pl.multiple_of(step * tile, tile), tile)
            grad = sum(parts[b, at].astype(jnp.float32) for b in range(owners))
            gates = gates_ref[at]
            grad_gate = RESIDUAL * dots_sum[at]
            grad_logits = (
                gates * (grad_gate - jnp.sum(gates * grad_gate, axis=-1, keepdims=True))
            ).astype(jnp.bfloat16)
            grad = grad + contract(
                grad_logits[:, : router_ref.shape[0]], router_ref[...], 1, 0
            )
            unit, inv_rms = norm_parts(middle[at])
            expert_in = (unit * gains_ref[1:2]).astype(jnp.bfloat16)
            after = cot_ref[at].astype(jnp.float32) + norm_grad(
                grad, gains_ref[1:2], unit, inv_rms
            )
            grad_middle[at] = after
            to = pl.ds(pl.multiple_of(core * half + step * tile, tile), tile)
            grad_attn[to] = (RESIDUAL * after).astype(jnp.bfloat16)
            count = small_sum.shape[0]
            small_sum[...] += contract(grad_logits, expert_in, 0, 0)[:count]
            small_sum[count - 2 : count - 1] += jnp.sum(grad * unit, axis=0, keepdims=True)
            return carry

        lax.fori_loop(0, half // tile, body, 0)

    pl.run_scoped(
        middle_phase,
        pltpu.VMEM(parts_hbm.shape, parts_hbm.dtype),
        pltpu.VMEM(middle_hbm.shape, middle_hbm.dtype),
        pltpu.VMEM(middle_hbm.shape, cot_hbm.dtype),
        pltpu.VMEM(dots_hbm.shape, dots_hbm.dtype),
        pltpu.VMEM(gates_ref.shape, dots_hbm.dtype),
    )
    attn_swap = to_sibling(grad_attn.at[mine], grad_attn.at[mine], 0)
    attn_swap.start()
    for shift in range(owners):
        comb_load(shift).wait()
    comb_send_on(owners - 1)
    to_sibling(grad_attn.at[others], grad_attn.at[others], 0).wait_recv()

    causal = length // 2

    def attention_phase(
        out_weight_ref, heads_ref, query_ref, key_ref, value_ref, key_sum, value_sum, normed_ref
    ):
        load_normed = pltpu.make_async_copy(normed_hbm, normed_ref, load_sem.at[0])
        loads = (
            pltpu.make_async_copy(heads_hbm, heads_ref, load_sem.at[4]),
            pltpu.make_async_copy(out_weight_hbm, out_weight_ref, load_sem.at[5]),
            pltpu.make_async_copy(query_hbm, query_ref, load_sem.at[6]),
            pltpu.make_async_copy(key_hbm, key_ref, load_sem.at[7]),
            pltpu.make_async_copy(value_hbm, value_ref, load_sem.at[8]),
        )
        for copy in loads:
            copy.start()
        load_normed.start()
        loads[0].wait()
        cut = heads_ref.shape[1] // 2
        weight_grad(out_a, grad_attn, heads_ref[:, :cut])
        output_job_a.start(0)
        weight_grad(out_b, grad_attn, heads_ref[:, cut:])
        output_job_b.start(0)
        for copy in loads[1:]:
            copy.wait()

        def turned_back(grads):
            swapped = jnp.concatenate(
                [grads[:, head_size // 2 :], grads[:, : head_size // 2]], axis=1
            )
            return (grads * cosine_ref[...] + swapped * sine_ref[...]).astype(jnp.bfloat16)

        def body(group, carry):
            grad_heads = contract(grad_attn[...], out_weight_ref[group], 1, 1).astype(jnp.bfloat16)
            keys, values = key_ref[group], value_ref[group]
            key_sum[...] = jnp.zeros_like(key_sum)
            value_sum[...] = jnp.zeros_like(value_sum)
            turned = []
            for member in range(groups):
                query = query_ref[group * groups + member]
                grad_head = grad_heads[:, member * head_size : (member + 1) * head_size]
                pieces = []
                for start in (0, causal):
                    stop = start + causal
                    some_q, some_g = query[start:stop], grad_head[start:stop]
                    some_k, some_v = keys[:stop], values[:stop]
                    scores = contract(some_q, some_k, 1, 1) * ATTN_SCALE
                    row = start + lax.broadcasted_iota(jnp.int32, scores.shape, 0)
                    col = lax.broadcasted_iota(jnp.int32, scores.shape, 1)
                    scores = jnp.where(row >= col, scores, NEGATIVE)
                    raised = jnp.exp(scores - jnp.max(scores, axis=1, keepdims=True))
                    probs = raised * (1.0 / jnp.sum(raised, axis=1, keepdims=True))
                    grad_probs = contract(some_g, some_v, 1, 1)
                    value_sum[:stop] += contract(probs.astype(jnp.bfloat16), some_g, 0, 0)
                    grad_scores = (
                        probs
                        * (grad_probs - jnp.sum(probs * grad_probs, axis=1, keepdims=True))
                    ).astype(jnp.bfloat16)
                    pieces.append(
                        jnp.dot(grad_scores, some_k, preferred_element_type=jnp.float32)
                    )
                    key_sum[:stop] += contract(grad_scores, some_q, 0, 0)
                turned.append(turned_back(ATTN_SCALE * jnp.concatenate(pieces, axis=0)))
            grad_query[group] = jnp.concatenate(turned, axis=1)
            grad_keyvalue[0, group] = turned_back(ATTN_SCALE * key_sum[...])
            grad_keyvalue[1, group] = value_sum[...].astype(jnp.bfloat16)

            @pl.when(group < local)
            def _():
                first_sum(group)

            return carry

        pairs = kv_heads // 2
        for pair, (jobs, stages) in enumerate(zip(pair_jobs, pair_stages)):
            chosen = range(pair * pairs, (pair + 1) * pairs)
            lax.fori_loop(chosen[0], chosen[-1] + 1, body, 0)
            queries = jnp.concatenate([grad_query[g] for g in chosen], axis=1)
            keyvalue = jnp.concatenate(
                [grad_keyvalue[what, g] for what in range(2) for g in chosen], axis=1
            )
            if pair == 0:
                comb_stage(owners - 2)
                load_normed.wait()
            weight_grad(stages[0], normed_ref, queries)
            jobs[0].start(0)
            weight_grad(stages[1], normed_ref, keyvalue)
            jobs[1].start(0)
            if pair == 0:
                lax.fori_loop(held, local, start_first, 0)

    pl.run_scoped(
        attention_phase,
        pltpu.VMEM(out_weight_hbm.shape, out_weight_hbm.dtype),
        pltpu.VMEM(heads_hbm.shape, heads_hbm.dtype),
        pltpu.VMEM(query_hbm.shape, query_hbm.dtype),
        pltpu.VMEM(key_hbm.shape, key_hbm.dtype),
        pltpu.VMEM(value_hbm.shape, value_hbm.dtype),
        pltpu.VMEM((length, head_size), jnp.float32),
        pltpu.VMEM((length, head_size), jnp.float32),
        pltpu.VMEM(normed_hbm.shape, normed_hbm.dtype),
    )
    def start_second(expert, carry):
        for plan in plans:
            for copy in second_copies(plan, expert):
                copy.start()
            keep(plan, expert).start()
        return carry

    def tokens_phase(query_weight, keyvalue_weight, grad_normed, tokens_ref):
        loads = (
            pltpu.make_async_copy(tokens_hbm.at[mine], tokens_ref, load_sem.at[3]),
            pltpu.make_async_copy(query_weight_hbm, query_weight, load_sem.at[1]),
            pltpu.make_async_copy(keyvalue_weight_hbm, keyvalue_weight, load_sem.at[2]),
        )
        for copy in loads:
            copy.start()
        for which in pair_jobs[0]:
            which.forward(0)
        for away in range(owners - 3, 0, -1):
            comb_stage(away)
        queries = jnp.concatenate([grad_query[g] for g in range(kv_heads)], axis=1)
        keyvalue = [
            jnp.concatenate([grad_keyvalue[what, g] for g in range(kv_heads)], axis=1)
            for what in range(2)
        ]
        for copy in loads:
            copy.wait()
        grad_normed[...] = (
            contract(queries, query_weight[...], 1, 1)
            + contract(keyvalue[0], keyvalue_weight[0], 1, 1)
            + contract(keyvalue[1], keyvalue_weight[1], 1, 1)
        )
        half_send[...] = grad_normed[others].astype(jnp.bfloat16)
        swap = to_sibling(half_send, half_land, 1)
        swap.start()
        swap.wait_recv()

        def body(step, carry):
            at = pl.ds(pl.multiple_of(step * tile, tile), tile)
            to = pl.ds(pl.multiple_of(core * half + step * tile, tile), tile)
            grad = grad_normed[to] + half_land[at].astype(jnp.float32)
            unit, inv_rms = norm_parts(tokens_ref[at].astype(jnp.float32))
            grad_middle[at] += norm_grad(grad, gains_ref[0:1], unit, inv_rms)
            count = small_sum.shape[0]
            small_sum[count - 1 : count] += jnp.sum(grad * unit, axis=0, keepdims=True)
            return carry

        lax.fori_loop(0, half // tile, body, 0)

    pl.run_scoped(
        tokens_phase,
        pltpu.VMEM(query_weight_hbm.shape, query_weight_hbm.dtype),
        pltpu.VMEM(keyvalue_weight_hbm.shape, keyvalue_weight_hbm.dtype),
        pltpu.VMEM((2 * half, feat_width), jnp.float32),
        pltpu.VMEM((half, feat_width), tokens_hbm.dtype),
    )
    tokens_store = pltpu.make_async_copy(grad_middle, tokens_grad_hbm.at[mine], store_sem.at[0])
    tokens_store.start()
    tokens_swap = to_sibling(grad_middle, tokens_grad_hbm.at[mine], 2)
    tokens_swap.start()
    small_exchange = to_sibling(small_sum, small_swap, 3)
    small_exchange.start()

    small_exchange.wait()
    small_sum[...] += small_swap[...]
    piece = feat_width // (rows * columns * owners)
    small_stage[...] = jnp.zeros_like(small_stage)
    for y in range(rows):
        for x in range(columns):
            for z in range(owners):
                at = ((y * columns + x) * owners + z) * piece
                small_stage[y, x, z, :, :piece] = small_sum[:, at : at + piece]
    small_job.start(0)

    output_job_b.forward(0)
    for which in pair_jobs[1]:
        which.forward(0)
    for expert in range(kv_heads, local):
        first_sum(expert)
    lax.fori_loop(0, local, start_second, 0)
    for which in pair_jobs[0]:
        which.forward(1)
    output_job_a.forward(0)
    output_job_b.forward(1)
    for which in pair_jobs[1]:
        which.forward(1)
    output_job_a.forward(1)
    small_job.forward(0)
    small_job.forward(1)

    def mixed_phase(middle):
        load = pltpu.make_async_copy(middle_hbm, middle, load_sem.at[1])
        load.start()
        comb_stage(0)
        load.wait()

        def body(step, carry):
            at = pl.ds(pl.multiple_of(step * tile, tile), tile)
            comb = comb_own[0, at].astype(jnp.float32)
            mixed_stage[at] = (middle[at] + RESIDUAL * comb).astype(jnp.bfloat16)
            return carry

        lax.fori_loop(0, half // tile, body, 0)

    pl.run_scoped(mixed_phase, pltpu.VMEM(middle_hbm.shape, middle_hbm.dtype))
    mixed_store = pltpu.make_async_copy(mixed_stage, mixed_hbm.at[mine], store_sem.at[1])
    mixed_store.start()
    mixed_swap = to_sibling(mixed_stage, mixed_hbm.at[mine], 4)
    mixed_swap.start()

    cut = out_a.shape[4]
    output_out[:, :cut] = output_job_a.total(2)
    output_out[:, cut:] = output_job_b.total(2)
    small = small_job.total(2)
    count = small.shape[0]
    router_out[...] = small[: router_out.shape[0], :piece]
    expert_gain_out[...] = small[count - 2 : count - 1, :piece]
    attn_gain_out[...] = small[count - 1 :, :piece]
    for pair, jobs in enumerate(pair_jobs):
        cut = near_q.shape[4]
        query_out[:, pair * cut : (pair + 1) * cut] = jobs[0].total(2)
        value = jobs[1].total(2)
        cut = near_kv.shape[4] // 2
        for what in range(2):
            keyvalue_out[what, :, pair * cut : (pair + 1) * cut] = value[
                :, what * cut : (what + 1) * cut
            ]

    def close(expert, carry):
        for plan in plans:

            @pl.when(expert >= early)
            def _():
                for copy in first_copies(plan, expert):
                    copy.wait_send()

            for copy in second_copies(plan, expert):
                copy.wait()
            keep(plan, expert).wait()
        return carry

    lax.fori_loop(0, local, close, 0)
    for away in range(1, owners):
        for side in (1, -1):

            @pl.when(inside(me + side * away))
            def _():
                comb_copy(side, away).wait_send()

    for which in (output_job_a, output_job_b, small_job) + pair_jobs[0] + pair_jobs[1]:
        which.close()
    attn_swap.wait_send()
    to_sibling(half_send, half_land, 1).wait_send()
    tokens_store.wait()
    mixed_store.wait()
    tokens_swap.wait_send()
    mixed_swap.wait_send()
    to_sibling(grad_middle, tokens_grad_hbm.at[others], 2).wait_recv()
    to_sibling(mixed_stage, mixed_hbm.at[others], 4).wait_recv()


def backward(
    parts,
    dots,
    combs,
    grads,
    early_a,
    early_b,
    gates,
    middle,
    cot,
    tokens,
    gains,
    router,
    out_weight,
    heads_out,
    query,
    keys,
    values,
    normed,
    query_weight,
    keyvalue_weight,
    cosine,
    sine,
):
    owners = lax.axis_size("expert")
    chunks = lax.axis_size("dp")
    rows, columns = factors(chunks)
    half, feat_width = middle.shape
    local, _, height, units = grads.shape[2:]
    early = early_a.shape[1]
    piece = feat_width // (chunks * owners)
    heads, length, head_size = query.shape
    kv_heads = keys.shape[0]
    query_width, key_width = heads * head_size, kv_heads * head_size
    lanes = 128
    count = 24
    out_weight = out_weight.reshape(kv_heads, query_width // kv_heads, feat_width)
    bf16, f32 = jnp.bfloat16, jnp.float32
    hbm = pl.BlockSpec(memory_space=pl.ANY)
    vmem = pl.BlockSpec(memory_space=pltpu.VMEM)
    dma = pltpu.SemaphoreType.DMA
    most = max(rows, columns, owners) - 1

    def landings(tail, order, dtype):
        sizes = {"y": rows, "x": columns, "z": owners}
        left = ["y", "x", "z"]
        found = []
        for axis in order:
            left.remove(axis)
            found.append(
                pltpu.VMEM((sizes[axis] - 1,) + tuple(sizes[a] for a in left) + tail, dtype)
            )
        return found

    whole = (rows, columns, owners)
    return pl.pallas_call(
        functools.partial(back_kernel, rows, columns, owners),
        in_specs=[hbm] * 6 + [vmem] + [hbm] * 3 + [vmem] * 2 + [hbm] * 8 + [vmem, vmem],
        out_specs=[hbm] * 5 + [vmem] * 6,
        out_shape=[
            jax.ShapeDtypeStruct((2 * half, feat_width), bf16),
            jax.ShapeDtypeStruct((2 * half, feat_width), f32),
            jax.ShapeDtypeStruct((2, local, height, units), bf16),
            jax.ShapeDtypeStruct((rows - 1, local, height, units), bf16),
            jax.ShapeDtypeStruct((columns - 1, local, height, units), bf16),
            jax.ShapeDtypeStruct((piece, query_width), f32),
            jax.ShapeDtypeStruct((2, piece, key_width), f32),
            jax.ShapeDtypeStruct((piece, query_width), f32),
            jax.ShapeDtypeStruct((router.shape[0], piece), f32),
            jax.ShapeDtypeStruct((1, piece), f32),
            jax.ShapeDtypeStruct((1, piece), f32),
        ],
        scratch_shapes=[
            pltpu.VMEM((2, rows, height, units), bf16),
            pltpu.VMEM((2, columns, height, units), bf16),
            pltpu.VMEM((columns - 1, local, rows, height, units), bf16),
            pltpu.VMEM((rows - 1, local, columns, height, units), bf16),
            pltpu.VMEM((owners, half, feat_width), bf16),
            pltpu.VMEM((owners - 1, half, feat_width), bf16),
            pltpu.VMEM((owners - 1, half, feat_width), bf16),
            pltpu.VMEM(whole + (piece, query_width // 2), bf16),
            *landings((piece, query_width // 2), "zxy", bf16),
            pltpu.VMEM(whole + (piece, query_width // 2), bf16),
            *landings((piece, query_width // 2), "yxz", bf16),
            pltpu.VMEM(whole + (piece, query_width // 2), bf16),
            *landings((piece, query_width // 2), "xyz", bf16),
            pltpu.VMEM(whole + (piece, key_width), bf16),
            *landings((piece, key_width), "yxz", bf16),
            pltpu.VMEM(whole + (piece, query_width // 2), bf16),
            *landings((piece, query_width // 2), "yxz", bf16),
            pltpu.VMEM(whole + (piece, key_width), bf16),
            *landings((piece, key_width), "xyz", bf16),
            pltpu.VMEM((count, feat_width), f32),
            pltpu.VMEM((count, feat_width), f32),
            pltpu.VMEM(whole + (count, lanes), f32),
            *landings((count, lanes), "zxy", f32),
            pltpu.VMEM((2 * half, feat_width), bf16),
            pltpu.VMEM((half, feat_width), f32),
            pltpu.VMEM((kv_heads, length, query_width // kv_heads), bf16),
            pltpu.VMEM((2, kv_heads, length, head_size), bf16),
            pltpu.VMEM((half, feat_width), bf16),
            pltpu.VMEM((half, feat_width), bf16),
            pltpu.VMEM((half, feat_width), bf16),
            dma((9,)),
            dma((2, local)),
            dma((2, local)),
            dma((2, early)),
            dma((2, most, local)),
            dma((2, most, local)),
            dma((2, most, local)),
            dma((2, most, local)),
            dma((owners,)),
            dma((2, owners)),
            dma((2, owners)),
            dma((7, 3, most)),
            dma((7, 3, most)),
            dma((5,)),
            dma((5,)),
            dma((2,)),
        ],
        compiler_params=pltpu.CompilerParams(
            vmem_limit_bytes=60 * 2**20, collective_id=1, has_side_effects=True
        ),
        cost_estimate=pl.CostEstimate(
            flops=12 * 2**30, bytes_accessed=60 * 2**20, transcendentals=heads * length * length
        ),
    )(
        parts,
        dots,
        combs,
        grads,
        early_a,
        early_b,
        gates,
        middle,
        cot,
        tokens,
        gains,
        router,
        out_weight,
        heads_out,
        query,
        keys,
        values,
        normed,
        query_weight,
        keyvalue_weight,
        cosine,
        sine,
    )


def finish_body(large, kept_a, kept_b, second_a, second_b, *refs):
    count = (len(refs) - 4 - large) // 2
    sources, gateup_out, down_out = refs[:count], refs[count], refs[count + 1]
    targets, held = refs[count + 2 : 2 * count + 2], refs[2 * count + 2 : -2]
    load_sem, store_sem = refs[-2:]
    step = pl.program_id(0)
    steps = pl.num_programs(0)
    width = gateup_out.shape[2]
    loads = [
        pltpu.make_async_copy(sources[at], held[at], load_sem.at[at]) for at in range(large)
    ]
    stores = [
        pltpu.make_async_copy(held[at], targets[at], store_sem.at[at]) for at in range(large)
    ]

    @pl.when(step == 0)
    def _():
        for copy in loads:
            copy.start()
        for at in range(large, count):
            targets[at][...] = sources[at][...]

    @pl.when(step == 1)
    def _():
        for load, store in zip(loads, stores):
            load.wait()
            store.start()

    turned = []
    for part, (kept, second) in enumerate(((kept_a, second_a), (kept_b, second_b))):
        value = kept[0, 0].astype(jnp.float32)
        for other in range(second.shape[0]):
            value = value + second[other, 0].astype(jnp.float32)
        gateup_out[0, part] = value[:width]
        turned.append(value[width:])
    down_out[0] = jnp.concatenate(turned, axis=0).T

    @pl.when(step == steps - 1)
    def _():
        for copy in stores:
            copy.wait()


def finish(kept, second_a, second_b, *wholes):
    _, local, height, units = kept.shape
    width = 2 * height // 3
    large = 2
    spaces = [pl.BlockSpec(memory_space=pl.ANY)] * large
    spaces += [pl.BlockSpec(memory_space=pltpu.VMEM)] * (len(wholes) - large)

    def piece(count, at):
        return pl.BlockSpec((count, 1, height, units), lambda step: (at, step, 0, 0))

    return pl.pallas_call(
        functools.partial(finish_body, large),
        grid=(local,),
        in_specs=[
            piece(1, 0),
            piece(1, 1),
            piece(second_a.shape[0], 0),
            piece(second_b.shape[0], 0),
        ]
        + spaces,
        out_specs=[
            pl.BlockSpec((1, 2, width, units), lambda step: (step, 0, 0, 0)),
            pl.BlockSpec((1, units, width), lambda step: (step, 0, 0)),
        ]
        + spaces,
        out_shape=[
            jax.ShapeDtypeStruct((local, 2, width, units), jnp.float32),
            jax.ShapeDtypeStruct((local, units, width), jnp.float32),
        ]
        + [jax.ShapeDtypeStruct(w.shape, w.dtype) for w in wholes],
        scratch_shapes=[pltpu.VMEM(w.shape, w.dtype) for w in wholes[:large]]
        + [pltpu.SemaphoreType.DMA((large,)), pltpu.SemaphoreType.DMA((large,))],
        compiler_params=pltpu.CompilerParams(vmem_limit_bytes=60 * 2**20),
    )(kept, kept, second_a, second_b, *wholes)


def per_device(
    tokens,
    out_grad,
    attn_gain,
    query_weight,
    key_value_weight,
    output_weight,
    expert_gain,
    router_weight,
    gateup_weight,
    down_weight,
    routes,
):
    cosine, sine = rotary_tables()
    gains = jnp.stack([attn_gain, expert_gain])
    parts, dots, combs, gates, grads, early_a, early_b, _, _, normed, *kept = experts(
        tokens,
        out_grad,
        routes.T,
        gains,
        cosine,
        sine,
        router_weight.T,
        query_weight,
        key_value_weight,
        output_weight,
        gateup_weight,
        down_weight,
    )
    query, keys, values, heads_out, middle = kept
    mixed, tokens_grad, kept, second_a, second_b, *small = backward(
        parts,
        dots,
        combs,
        grads,
        early_a,
        early_b,
        gates,
        middle,
        out_grad,
        tokens,
        gains,
        router_weight.T,
        output_weight,
        heads_out,
        query,
        keys,
        values,
        normed,
        query_weight,
        key_value_weight,
        cosine,
        sine,
    )
    (
        gateup_total,
        down_total,
        mixed,
        tokens_grad,
        query_total,
        keyvalue_total,
        output_total,
        router_total,
        expert_gain_total,
        attn_gain_total,
    ) = finish(kept, second_a, second_b, mixed, tokens_grad, *small)
    return (
        mixed,
        tokens_grad,
        attn_gain_total[0],
        query_total,
        keyvalue_total,
        output_total.T,
        expert_gain_total[0],
        router_total.T,
        gateup_total,
        down_total,
    )


def solution(mesh):
    placed = (
        P(("dp", "expert"), None),
        P(("dp", "expert"), None),
        P(),
        P(None, "tensor"),
        P(None, None, "tensor"),
        P("tensor", None),
        P(),
        P(),
        P("expert", None, None, "tensor"),
        P("expert", "tensor", None),
        P(("dp", "expert"), None),
    )
    return jax.shard_map(
        per_device,
        mesh=mesh,
        in_specs=placed,
        out_specs=(
            P(("dp", "expert"), None),
            P(("dp", "expert"), None),
            P(("dp", "expert")),
            P(("dp", "expert"), "tensor"),
            P(None, ("dp", "expert"), "tensor"),
            P("tensor", ("dp", "expert")),
            P(("dp", "expert")),
            P(("dp", "expert"), None),
            P("expert", None, "dp", "tensor"),
            P("expert", "tensor", "dp"),
        ),
        check_vma=False,
    )
```
